128 devices in a mesh: cell: 16 (over y, x), gene: 8 (over z, core).
Axes of the slice: x: 4, y: 4, z: 4, core: 2. Of those that a mesh axis runs over, the one named last changes fastest.
Arguments:
- expression: float32 [24576, 32768], P('cell', 'gene'), may hold values from -16 to 18, as said below
- tile_mask: int32 [96, 128], P('cell', 'gene'), may hold values from 0 to 1, as said below
- start: float32 [32768, 32], P('gene'), may hold values from -6 to 6
Outputs:
- alphas: float32 [2, 32, 32], replicated
- betas: float32 [2, 32, 32], replicated
- next_block: float32 [32768, 32], P('gene')
The draws below stay inside these ranges and needn't reach their ends.
Inputs may be any that keep to these rules, and one draw needn't show every extreme that they name: expression: positive mean per gene with gene and cell scales and independent noise. `tile_mask`: each row of tiles belongs to one of 8 cell types and each column of tiles to one of 8 gene modules; a tile is 1 where its type expresses its module.
All inputs are finite; a program needn't handle non-finite values.
Results may differ from the reference program's by a relative error of at most 0.0024.
Values sent between devices are 32-bit elements; how exact they have to be, the bound alone decides.
A program may use at most 128 MiB of HBM per device.

```python
import jax
import jax.numpy as jnp
from jax import lax

CELL_DEV = 1536
GENES = 32768
TILE = 256
BLOCK = 32
STEPS = 2
CELLS = 24576
N_CELL = 16


def draw_expression(key, part):
    keys = jax.random.split(key, 3)
    gene_scale = jnp.exp(jax.random.uniform(keys[0], (1, GENES), jnp.float32, -0.7, 0.7))
    cell_scale = jnp.exp(jax.random.uniform(keys[1], (CELLS, 1), jnp.float32, -0.7, 0.7))
    noise = jnp.clip(jax.random.normal(keys[2], (CELLS, GENES), jnp.float32), -4.0, 4.0)
    return gene_scale * (0.6 + cell_scale * noise)


def draw_tile_mask(key, part):
    keys = jax.random.split(key, 3)
    types = jax.random.randint(keys[0], (CELLS // TILE,), 0, 8)
    modules = jax.random.randint(keys[1], (GENES // TILE,), 0, 8)
    table = jnp.maximum(jax.random.randint(keys[2], (8, 8), 0, 2), jnp.eye(8, dtype=jnp.int32))
    return jnp.take(jnp.take(table, types, axis=0), modules, axis=1).astype(jnp.int32)


def steps_of(own_key, shape, cuts, low, high):
    gain = 1.0
    for dim, parts in cuts:
        draws = jax.random.uniform(jax.random.fold_in(jax.random.fold_in(own_key, 6), dim), (parts,), jnp.float32, low / len(cuts), high / len(cuts))
        gain = gain * jnp.repeat(jnp.exp(draws), shape[dim] // parts).reshape((-1,) + (1,) * (len(shape) - 1 - dim))
    return gain


def gaussian(rng, dims, scale, limit, cuts=(), held_as=jnp.bfloat16):
    drawn = scale * jax.random.normal(rng, dims, jnp.float32)
    if cuts:
        drawn = drawn * steps_of(rng, dims, cuts, -0.22, 0.18)
    return jnp.clip(drawn, -limit, limit).astype(held_as)


def setup_inputs(seed: int = 0) -> dict:
    arg_keys = jax.random.split(jax.random.key(seed), 4)
    return {
        "expression": draw_expression(jax.random.fold_in(arg_keys[3], 71), 0),
        "tile_mask": draw_tile_mask(jax.random.fold_in(arg_keys[3], 71), 0),
        "start": gaussian(arg_keys[2], (GENES, BLOCK), 1.0, 6.0, ((0, 8),), jnp.float32),
    }


highest = lax.Precision.HIGHEST

def transposed_dot(left, right):
    return lax.dot_general(left.astype(jnp.float32), right.astype(jnp.float32), (((0,), (0,)), ((), ())), precision=highest, preferred_element_type=jnp.float32)

def product(left, right):
    return jnp.dot(left.astype(jnp.float32), right.astype(jnp.float32), precision=highest, preferred_element_type=jnp.float32)

def finish(resid, gram):
    lower = jnp.linalg.cholesky(gram)
    fresh = lax.linalg.triangular_solve(lower, resid, left_side=False, lower=True, transpose_a=True)
    return (fresh, jnp.transpose(lower))

def reference(expression, tile_mask, start):
    blocks = expression.reshape(N_CELL, CELL_DEV, GENES)
    masks = tile_mask.reshape(N_CELL, CELL_DEV // TILE, GENES // TILE)

    def masked_block(values, occupancy):
        tiles = values.reshape(CELL_DEV // TILE, TILE, GENES // TILE, TILE)
        return (tiles * occupancy.astype(jnp.float32)[:, None, :, None]).reshape(CELL_DEV, GENES)

    def add_means(total, pair):
        return (total + jnp.sum(masked_block(pair[0], pair[1]), axis=0), None)
    col_total = lax.scan(add_means, jnp.zeros((GENES,), jnp.float32), (blocks, masks))[0]
    means = col_total / CELLS

    def apply_gram(current):

        def side(pair):
            return product(masked_block(pair[0], pair[1]), current) - product(means[None, :], current)
        cell_side = lax.map(side, (blocks, masks))

        def add_image(total, triple):
            return (total + transposed_dot(masked_block(triple[0], triple[1]), triple[2]), None)
        summed = lax.scan(add_image, jnp.zeros((GENES, BLOCK), jnp.float32), (blocks, masks, cell_side))[0]
        return summed / CELLS
    current = finish(start, transposed_dot(start, start))[0]
    older = None
    alpha_list = []
    beta_list = []
    for step in range(STEPS):
        image = apply_gram(current)
        alpha = transposed_dot(current, image)
        resid = image - product(current, alpha)
        if older is not None:
            prior = transposed_dot(older, image)
            resid = resid - product(older, prior)
        fresh, beta = finish(resid, transposed_dot(resid, resid))
        alpha_list.append(alpha)
        beta_list.append(beta)
        older = current
        current = fresh
    return (jnp.stack(alpha_list), jnp.stack(beta_list), current * GENES ** 0.5)
```

```python
import functools
import math

import jax
import jax.numpy as jnp
from jax import lax
from jax.experimental import pallas as pl
from jax.experimental.pallas import tpu as pltpu
from jax.sharding import PartitionSpec as P

TILE = 256
BLOCK = 32
MESH = pl.DeviceIdType.MESH
F32 = jnp.float32
BF16 = jnp.bfloat16
HIGHEST = lax.Precision.HIGHEST


def dot(left, right, dims, precision=None):
    return lax.dot_general(left, right, (dims, ((), ())), precision=precision, preferred_element_type=F32)


NN = ((1,), (0,))
NT = ((1,), (1,))


def split3(value):
    first = value.astype(BF16)
    rest = value - first.astype(F32)
    second = rest.astype(BF16)
    third = (rest - second.astype(F32)).astype(BF16)
    return jnp.concatenate([first, second, third], axis=0)


def fold3(value):
    return value[0:BLOCK] + value[BLOCK : 2 * BLOCK] + value[2 * BLOCK : 3 * BLOCK]


def factor(gram):
    row_of = lax.broadcasted_iota(jnp.int32, (BLOCK, 128), 0)
    lane_of = lax.broadcasted_iota(jnp.int32, (BLOCK, 128), 1)
    both = jnp.concatenate([gram, jnp.zeros((BLOCK, 128 - BLOCK), F32)], axis=1)
    both = both + (lane_of == row_of + BLOCK).astype(F32)
    for k in range(BLOCK - 1):
        row = both[k : k + 1, :]
        scaled = row / row[:, k : k + 1]
        column = jnp.where(row_of[:, 0:1] > k, both[:, k : k + 1], 0.0)
        both = both - column * scaled
    diagonal = jnp.sum(jnp.where(lane_of == row_of, both, 0.0), axis=1, keepdims=True)
    both = both / jnp.sqrt(diagonal)
    upper = jnp.where(lane_of >= row_of, both, 0.0)
    return upper[:, 0:BLOCK], both[:, BLOCK : 2 * BLOCK]


def kernel(
    sizes,
    x_ref,
    mask_ref,
    start_ref,
    alphas_ref,
    betas_ref,
    next_ref,
    high,
    low,
    stage,
    start3,
    gram_buf,
    z_send,
    z_recv,
    z_full,
    z_send2,
    z_recv2,
    z_full2,
    y_all,
    y3,
    stat_buf,
    i_send,
    i_recv,
    i_send2,
    i_recv2,
    resid,
    acc,
    load_sem,
    gram_send_sem,
    gram_sem,
    z_send_sem,
    z_sem,
    zg_send_sem,
    zg_sem,
    z2_sems,
    stat_send_sem,
    stat_sem,
    rs_send_sem,
    rs_sem,
    ag_send_sem,
    ag_sem,
):
    n_cell, n_gene, rows, width = sizes
    cells = rows * n_cell
    chunks = rows // TILE
    tiles = width // TILE
    c = lax.axis_index("cell")
    g = lax.axis_index("gene")
    z, core = g // 2, g % 2

    def load(i, slot):
        return pltpu.make_async_copy(
            x_ref.at[pl.ds(pl.multiple_of(i * TILE, TILE), TILE), :], stage.at[slot], load_sem.at[slot]
        )

    for i in range(3):
        load(i, i).start()

    barrier = pltpu.get_barrier_semaphore()

    @pl.loop(1, n_cell)
    def _(k):
        pl.semaphore_signal(barrier, inc=1, device_id=(lax.rem(c + k, n_cell), g), device_id_type=MESH)

    @pl.loop(1, n_gene)
    def _(k):
        pl.semaphore_signal(barrier, inc=1, device_id=(c, lax.rem(g + k, n_gene)), device_id_type=MESH)

    def pad_lanes(value):
        return jnp.concatenate([value, jnp.zeros((value.shape[0], 128 - value.shape[1]), F32)], axis=1)

    def send_gram(step, value):
        gram_buf[step, g] = pad_lanes(value)

        @pl.loop(1, n_gene)
        def _(k):
            pltpu.make_async_remote_copy(
                src_ref=gram_buf.at[step, g],
                dst_ref=gram_buf.at[step, g],
                send_sem=gram_send_sem.at[step],
                recv_sem=gram_sem.at[step],
                device_id=(c, lax.rem(g + k, n_gene)),
                device_id_type=MESH,
            ).start()

    def take_gram(step):
        part = gram_buf.at[step, pl.ds(0, n_gene - 1)]
        pltpu.make_async_copy(part, part, gram_sem.at[step]).wait()
        total = gram_buf[step, 0]
        for k in range(1, n_gene):
            total = total + gram_buf[step, k]
        return total[:, 0:BLOCK]

    start3[...] = split3(start_ref[...])
    gram0 = dot(start_ref[...], start_ref[...], NT, HIGHEST)
    pl.semaphore_wait(barrier, n_cell + n_gene - 2)
    send_gram(0, gram0)

    def spread(i):
        @pl.loop(1, n_gene)
        def _(k):
            peer = lax.rem(g + k, n_gene)
            pltpu.make_async_remote_copy(
                src_ref=z_send.at[
                    i, pl.ds(pl.multiple_of(peer // 2 * 8, 8), 8), pl.ds(pl.multiple_of(peer % 2 * 128, 128), 128)
                ],
                dst_ref=z_recv.at[i, k],
                send_sem=z_send_sem.at[i],
                recv_sem=z_sem.at[i],
                device_id=(c, peer),
                device_id_type=MESH,
            ).start()

    def gather(i):
        part = z_recv.at[i, pl.ds(1, n_gene - 1)]
        pltpu.make_async_copy(part, part, z_sem.at[i]).wait()
        own_rows = pl.ds(pl.multiple_of(z * 8, 8), 8)
        total = z_send[i, own_rows, pl.ds(pl.multiple_of(core * 128, 128), 128)]
        for k in range(1, n_gene):
            total = total + z_recv[i, k]
        place = z_full.at[own_rows, pl.ds(pl.multiple_of(i * TILE + core * 128, 128), 128)]
        place[...] = total

        @pl.loop(1, n_gene)
        def _(k):
            pltpu.make_async_remote_copy(
                src_ref=place,
                dst_ref=place,
                send_sem=zg_send_sem.at[0],
                recv_sem=zg_sem.at[0],
                device_id=(c, lax.rem(g + k, n_gene)),
                device_id_type=MESH,
            ).start()

    @pl.loop(0, chunks)
    def _(i):
        slot = lax.rem(i, 3)
        load(i, slot).wait()
        here = pl.ds(pl.multiple_of(i * TILE, TILE), TILE)

        def tile(j, total):
            lanes = pl.ds(pl.multiple_of(j * TILE, TILE), TILE)
            values = stage[slot, :, lanes] * mask_ref[i, j].astype(F32)
            top = values.astype(BF16)
            rest = (values - top.astype(F32)).astype(BF16)
            high[here, lanes] = top
            low[here, lanes] = rest
            return total + dot(start3[:, lanes], top, NT) + dot(start3[:, lanes], rest, NT)

        total = lax.fori_loop(0, tiles, tile, jnp.zeros((3 * BLOCK, TILE), F32))

        @pl.when(i + 3 < chunks)
        def _():
            load(i + 3, slot).start()

        z_send[i] = fold3(total)
        spread(i)

        @pl.when(i > 0)
        def _():
            gather(i - 1)

    upper, inverse0 = factor(take_gram(0))
    gather(chunks - 1)
    pltpu.make_async_copy(
        z_recv.at[:, pl.ds(1, n_gene - 1)], z_recv.at[:, pl.ds(1, n_gene - 1)], zg_sem.at[0]
    ).wait()

    ones = jnp.ones((16, rows), BF16)
    y3[pl.ds(3 * BLOCK, 16), :] = ones
    y_all[pl.ds(2 * BLOCK, 8), :] = jnp.ones((8, rows), F32)
    y_all[pl.ds(BLOCK, BLOCK), :] = jnp.zeros((BLOCK, rows), F32)
    own = pl.ds(pl.multiple_of(c * TILE, TILE), TILE)
    current = dot(inverse0, start_ref[:, own], NN, HIGHEST)
    older = None
    inverse = inverse0
    column_sums = None

    for step in range(2):
        if step == 0:
            side = dot(inverse, z_full[...], NN, HIGHEST)
        else:
            y_all[pl.ds(BLOCK, BLOCK), :] = y_all[pl.ds(0, BLOCK), :]
            side = dot(inverse, z_full2[...], NN, HIGHEST)
        y_all[pl.ds(0, BLOCK), :] = side
        y3[pl.ds(0, 3 * BLOCK), :] = split3(side)
        stat = dot(jnp.concatenate([side, jnp.ones((8, rows), F32)], axis=0), y_all[...], NT, HIGHEST)
        stat_buf[step, c] = pad_lanes(stat)

        @pl.loop(1, n_cell)
        def _(k):
            pltpu.make_async_remote_copy(
                src_ref=stat_buf.at[step, c],
                dst_ref=stat_buf.at[step, c],
                send_sem=stat_send_sem.at[step],
                recv_sem=stat_sem.at[step],
                device_id=(lax.rem(c + k, n_cell), g),
                device_id_type=MESH,
            ).start()

        sent = i_send if step == 0 else i_send2
        got = i_recv if step == 0 else i_recv2
        left_rows = 3 * BLOCK + 16 if step == 0 else 3 * BLOCK

        def image(k):
            owner = lax.rem(c + k, n_cell)
            lanes = pl.ds(pl.multiple_of(owner * TILE, TILE), TILE)
            left = y3[pl.ds(0, left_rows), :]
            product = dot(left, high[:, lanes], NN) + dot(left, low[:, lanes], NN)
            sent[owner, pl.ds(0, BLOCK), :] = fold3(product)
            if step == 0:
                sent[owner, pl.ds(BLOCK, 8), :] = product[3 * BLOCK : 3 * BLOCK + 8]

        def send_image(k):
            owner = lax.rem(c + k, n_cell)
            pltpu.make_async_remote_copy(
                src_ref=sent.at[owner],
                dst_ref=got.at[k],
                send_sem=rs_send_sem.at[step],
                recv_sem=rs_sem.at[step],
                device_id=(owner, g),
                device_id_type=MESH,
            ).start()

        @pl.loop(0, n_cell // 2)
        def _(t):
            image(2 * t + 1)
            image(2 * t + 2)
            send_image(2 * t + 1)

            @pl.when(t < n_cell // 2 - 1)
            def _():
                send_image(2 * t + 2)

        part = stat_buf.at[step, pl.ds(0, n_cell - 1)]
        pltpu.make_async_copy(part, part, stat_sem.at[step]).wait()
        stat = stat_buf[step, 0]
        for k in range(1, n_cell):
            stat = stat + stat_buf[step, k]
        stat = stat / cells
        mean_column = stat[0:BLOCK, 2 * BLOCK : 2 * BLOCK + 1]
        mean_row = stat[BLOCK : BLOCK + 1, :]
        centered = stat[0:BLOCK, :] - mean_column * mean_row
        alpha = centered[:, 0:BLOCK]
        alphas_ref[step] = alpha

        part = got.at[pl.ds(1, n_cell - 1)]
        pltpu.make_async_copy(part, part, rs_sem.at[step]).wait()
        piece = sent[c]
        for k in range(1, n_cell):
            piece = piece + got[k]
        if step == 0:
            column_sums = piece[BLOCK : BLOCK + 1]
        piece = (piece[0:BLOCK] - mean_column * column_sums) / cells
        piece = piece - dot(alpha, current, NN, HIGHEST)
        if step > 0:
            piece = piece - dot(centered[:, BLOCK : 2 * BLOCK], older, NN, HIGHEST)
        resid[step, :, own] = piece

        @pl.loop(1, n_cell)
        def _(k):
            pltpu.make_async_remote_copy(
                src_ref=resid.at[step, :, own],
                dst_ref=resid.at[step, :, own],
                send_sem=ag_send_sem.at[step],
                recv_sem=ag_sem.at[step, k],
                device_id=(lax.rem(c + k, n_cell), g),
                device_id_type=MESH,
            ).start()

        def wait_piece(k):
            lanes = pl.ds(pl.multiple_of(lax.rem(c - k + n_cell, n_cell) * TILE, TILE), TILE)
            pltpu.make_async_copy(resid.at[step, :, lanes], resid.at[step, :, lanes], ag_sem.at[step, k]).wait()
            return lanes

        if step == 0:

            def multiply(lanes):
                left = split3(resid[step, :, lanes])
                return dot(left, high[:, lanes], NT) + dot(left, low[:, lanes], NT)

            acc[...] = multiply(own)

            @pl.loop(1, n_cell)
            def _(k):
                acc[...] += multiply(wait_piece(k))

            send_gram(1, dot(resid[step], resid[step], NT, HIGHEST))
            z_send2[...] = fold3(acc)
            half = rows // 2

            @pl.loop(1, n_gene)
            def _(k):
                peer = lax.rem(g + k, n_gene)
                pltpu.make_async_remote_copy(
                    src_ref=z_send2.at[
                        pl.ds(pl.multiple_of(peer // 2 * 8, 8), 8), pl.ds(pl.multiple_of(peer % 2 * half, half), half)
                    ],
                    dst_ref=z_recv2.at[k],
                    send_sem=z2_sems.at[0],
                    recv_sem=z2_sems.at[1],
                    device_id=(c, peer),
                    device_id_type=MESH,
                ).start()

            parts = z_recv2.at[pl.ds(1, n_gene - 1)]
            pltpu.make_async_copy(parts, parts, z2_sems.at[1]).wait()
            place = z_full2.at[
                pl.ds(pl.multiple_of(z * 8, 8), 8), pl.ds(pl.multiple_of(core * half, half), half)
            ]
            total = z_send2[pl.ds(pl.multiple_of(z * 8, 8), 8), pl.ds(pl.multiple_of(core * half, half), half)]
            for k in range(1, n_gene):
                total = total + z_recv2[k]
            place[...] = total

            @pl.loop(1, n_gene)
            def _(k):
                pltpu.make_async_remote_copy(
                    src_ref=place,
                    dst_ref=place,
                    send_sem=z2_sems.at[2],
                    recv_sem=z2_sems.at[3],
                    device_id=(c, lax.rem(g + k, n_gene)),
                    device_id_type=MESH,
                ).start()

            upper, inverse = factor(take_gram(1))
            betas_ref[0] = upper
            older = current
            current = dot(inverse, piece, NN, HIGHEST)
            pltpu.make_async_copy(parts, parts, z2_sems.at[3]).wait()
            for sem in (0, 2):
                pltpu.make_async_copy(parts, parts, z2_sems.at[sem]).wait()
        else:

            @pl.loop(1, n_cell)
            def _(k):
                wait_piece(k)

            send_gram(2, dot(resid[step], resid[step], NT, HIGHEST))
            upper, inverse = factor(take_gram(2))
            betas_ref[1] = upper
            next_ref[...] = dot(inverse * math.sqrt(width * n_gene), resid[step], NN, HIGHEST)

    for step in range(3):
        part = gram_buf.at[step, pl.ds(0, n_gene - 1)]
        pltpu.make_async_copy(part, part, gram_send_sem.at[step]).wait()
    for i in range(chunks):
        part = z_recv.at[i, pl.ds(1, n_gene - 1)]
        pltpu.make_async_copy(part, part, z_send_sem.at[i]).wait()
    part = z_recv.at[:, pl.ds(1, n_gene - 1)]
    pltpu.make_async_copy(part, part, zg_send_sem.at[0]).wait()
    for step in range(2):
        part = stat_buf.at[step, pl.ds(0, n_cell - 1)]
        pltpu.make_async_copy(part, part, stat_send_sem.at[step]).wait()
        part = (i_recv if step == 0 else i_recv2).at[pl.ds(1, n_cell - 1)]
        pltpu.make_async_copy(part, part, rs_send_sem.at[step]).wait()
        part = resid.at[step, :, pl.ds(0, (n_cell - 1) * TILE)]
        pltpu.make_async_copy(part, part, ag_send_sem.at[step]).wait()


def per_device(sizes, expression, tile_mask, start):
    n_cell, n_gene, rows, width = sizes
    chunks = rows // TILE
    vmem = pl.BlockSpec(memory_space=pltpu.VMEM)
    dma = pltpu.SemaphoreType.DMA
    alphas, betas, fresh = pl.pallas_call(
        functools.partial(kernel, sizes),
        out_shape=(
            jax.ShapeDtypeStruct((2, BLOCK, BLOCK), F32),
            jax.ShapeDtypeStruct((2, BLOCK, BLOCK), F32),
            jax.ShapeDtypeStruct((BLOCK, width), F32),
        ),
        in_specs=[pl.BlockSpec(memory_space=pl.ANY), pl.BlockSpec(memory_space=pltpu.SMEM), vmem],
        out_specs=(vmem, vmem, vmem),
        scratch_shapes=[
            pltpu.VMEM((rows, width), BF16),
            pltpu.VMEM((rows, width), BF16),
            pltpu.VMEM((3, TILE, width), F32),
            pltpu.VMEM((3 * BLOCK, width), BF16),
            pltpu.VMEM((3, n_gene, BLOCK, 128), F32),
            pltpu.VMEM((chunks, BLOCK, TILE), F32),
            pltpu.VMEM((chunks, n_gene, 8, 128), F32),
            pltpu.VMEM((BLOCK, rows), F32),
            pltpu.VMEM((BLOCK, rows), F32),
            pltpu.VMEM((n_gene, 8, rows // 2), F32),
            pltpu.VMEM((BLOCK, rows), F32),
            pltpu.VMEM((2 * BLOCK + 8, rows), F32),
            pltpu.VMEM((3 * BLOCK + 16, rows), BF16),
            pltpu.VMEM((2, n_cell, BLOCK + 8, 128), F32),
            pltpu.VMEM((n_cell, BLOCK + 8, TILE), F32),
            pltpu.VMEM((n_cell, BLOCK + 8, TILE), F32),
            pltpu.VMEM((n_cell, BLOCK, TILE), F32),
            pltpu.VMEM((n_cell, BLOCK, TILE), F32),
            pltpu.VMEM((2, BLOCK, width), F32),
            pltpu.VMEM((3 * BLOCK, rows), F32),
            dma((3,)),
            dma((3,)),
            dma((3,)),
            dma((chunks,)),
            dma((chunks,)),
            dma((1,)),
            dma((1,)),
            dma((4,)),
            dma((2,)),
            dma((2,)),
            dma((2,)),
            dma((2,)),
            dma((2,)),
            dma((2, n_cell)),
        ],
        compiler_params=pltpu.CompilerParams(
            collective_id=0, has_side_effects=True, vmem_limit_bytes=60 * 2**20
        ),
        name="lanczos",
    )(expression, tile_mask, start.T)
    return alphas, betas, fresh.T


def solution(mesh):
    n_cell, n_gene = mesh.shape["cell"], mesh.shape["gene"]

    def run(expression, tile_mask, start):
        sizes = (n_cell, n_gene, expression.shape[0] // n_cell, expression.shape[1] // n_gene)
        return jax.shard_map(
            functools.partial(per_device, sizes),
            mesh=mesh,
            in_specs=(P("cell", "gene"), P("cell", "gene"), P("gene", None)),
            out_specs=(P(), P(), P("gene", None)),
            check_vma=False,
        )(expression, tile_mask, start)

    return run
```

```python
import functools
import math

import jax
import jax.numpy as jnp
from jax import lax
from jax.experimental import pallas as pl
from jax.experimental.pallas import tpu as pltpu
from jax.sharding import PartitionSpec as P

TILE = 256
BLOCK = 32
MESH = pl.DeviceIdType.MESH
F32 = jnp.float32
BF16 = jnp.bfloat16
UNROLL = 4
EARLY = 3

NN = ((1,), (0,))
NT = ((1,), (1,))
SIDE = 4
ORDER = sorted(
    ((dy, dx) for dy in range(SIDE) for dx in range(SIDE)),
    key=lambda at: (min(at[0], SIDE - at[0]) + min(at[1], SIDE - at[1]), at),
)


def dot(left, right, dims):
    return lax.dot_general(left, right, (dims, ((), ())), preferred_element_type=F32)


def pieces(value):
    first = value.astype(BF16)
    rest = value - first.astype(F32)
    second = rest.astype(BF16)
    third = (rest - second.astype(F32)).astype(BF16)
    return first, second, third


def split3(value):
    return jnp.concatenate(pieces(value), axis=0)


def fold3(value):
    return value[0:BLOCK] + value[BLOCK : 2 * BLOCK] + value[2 * BLOCK : 3 * BLOCK]


def fold_lanes(value, at=0):
    a, b, d = (value[:, at + BLOCK * k : at + BLOCK * (k + 1)] for k in range(3))
    return a + b + d


def small_product(left, right):
    a1, a2, a3 = pieces(left)
    b1, b2, b3 = pieces(right)
    lhs = jnp.concatenate([a1, a2, a3, a1, a2, a1], axis=1)
    rhs = jnp.concatenate([b1, b1, b1, b2, b2, b3], axis=0)
    return dot(lhs, rhs, NN)


def gram_of(split):
    return fold_lanes(fold3(dot(split, split, NT)))


def pack(matrix):
    return jnp.concatenate([matrix[8 * k : 8 * (k + 1), :] for k in range(4)], axis=1)


def unpack(tile):
    return jnp.concatenate([tile[:, BLOCK * k : BLOCK * (k + 1)] for k in range(4)], axis=0)


def factor(gram):
    row_of = lax.broadcasted_iota(jnp.int32, (BLOCK, 128), 0)
    lane_of = lax.broadcasted_iota(jnp.int32, (BLOCK, 128), 1)
    both = jnp.concatenate([gram, jnp.zeros((BLOCK, 128 - BLOCK), F32)], axis=1)
    both = both + (lane_of == row_of + BLOCK).astype(F32)
    for k in range(BLOCK - 1):
        row = both[k : k + 1, :]
        scaled = row / row[:, k : k + 1]
        column = jnp.where(row_of[:, 0:1] > k, both[:, k : k + 1], 0.0)
        both = both - column * scaled
    diagonal = jnp.sum(jnp.where(lane_of == row_of, both, 0.0), axis=1, keepdims=True)
    both = both / jnp.sqrt(diagonal)
    upper = jnp.where(lane_of >= row_of, both, 0.0)
    return upper[:, 0:BLOCK], both[:, BLOCK : 2 * BLOCK]


def kernel(
    sizes,
    x_ref,
    mask_ref,
    start_ref,
    small_ref,
    resid_ref,
    high,
    low,
    stage,
    start3,
    gram_buf,
    last_buf,
    z_send,
    z_recv,
    z_full,
    z_send2,
    z_recv2,
    z_full2,
    y3,
    stat_buf,
    image_acc,
    i_send,
    i_recv,
    i_send2,
    i_recv2,
    resid,
    resid3,
    acc,
    load_sem,
    gram_sems,
    last_sems,
    z_send_sem,
    z_sem,
    zg_send_sem,
    zg_sem,
    z2_sems,
    stat_send_sem,
    stat_sem,
    rs_send_sem,
    rs_sem,
    ag_send_sem,
    ag_sem,
):
    n_cell, n_gene, rows, width = sizes
    cells = rows * n_cell
    chunks = rows // TILE
    tiles = width // TILE
    c = lax.axis_index("cell")
    g = lax.axis_index("gene")
    z, core = g // 2, g % 2
    y_at, x_at = c // SIDE, c % SIDE

    def cell_at(k, sign):
        if isinstance(k, int):
            dy, dx = ORDER[k]
        else:
            dy, dx = ORDER[0]
            for i in range(1, n_cell):
                dy = jnp.where(k == i, ORDER[i][0], dy)
                dx = jnp.where(k == i, ORDER[i][1], dx)
        return lax.rem(y_at + sign * dy + SIDE, SIDE) * SIDE + lax.rem(x_at + sign * dx + SIDE, SIDE)

    def block(index, size=TILE):
        return pl.ds(pl.multiple_of(index * size, size), size)

    def wait_bytes(ref, sem):
        pltpu.make_async_copy(ref, ref, sem).wait()

    def load(i, slot):
        return pltpu.make_async_copy(x_ref.at[block(i), :], stage.at[slot], load_sem.at[slot])

    for i in range(3):
        load(i, i).start()

    barrier = pltpu.get_barrier_semaphore()

    @pl.loop(1, n_cell)
    def _(k):
        pl.semaphore_signal(barrier, inc=1, device_id=(lax.rem(c + k, n_cell), g), device_id_type=MESH)

    @pl.loop(1, n_gene)
    def _(k):
        pl.semaphore_signal(barrier, inc=1, device_id=(c, lax.rem(g + k, n_gene)), device_id_type=MESH)

    def to_genes(src, dst, send_sem, recv_sem):
        @pl.loop(1, n_gene)
        def _(k):
            pltpu.make_async_remote_copy(
                src_ref=src,
                dst_ref=dst,
                send_sem=send_sem,
                recv_sem=recv_sem,
                device_id=(c, lax.rem(g + k, n_gene)),
                device_id_type=MESH,
            ).start()

    def to_cells(src, dst, send_sem, recv_sem_of):
        @pl.loop(1, n_cell)
        def _(t):
            k = n_cell - t
            pltpu.make_async_remote_copy(
                src_ref=src,
                dst_ref=dst,
                send_sem=send_sem,
                recv_sem=recv_sem_of(k),
                device_id=(cell_at(k, 1), g),
                device_id_type=MESH,
            ).start()

    def sum_slots(buf, count):
        total = buf[0]
        for k in range(1, count):
            total = total + buf[k]
        return total

    def send_gram(step, tile):
        gram_buf[step, g] = tile
        here = gram_buf.at[step, g]
        to_genes(here, here, gram_sems.at[step, 0], gram_sems.at[step, 1])

    def take_gram(step):
        wait_bytes(gram_buf.at[step, pl.ds(0, n_gene - 1)], gram_sems.at[step, 1])
        return unpack(sum_slots(gram_buf.at[step], n_gene))

    start3[...] = split3(start_ref[...])
    gram0 = pack(gram_of(start3[...]))
    y3[0, pl.ds(3 * BLOCK, 16), :] = jnp.ones((16, rows), BF16)
    y3[1, pl.ds(3 * BLOCK, 16), :] = jnp.ones((16, rows), BF16)
    pl.semaphore_wait(barrier, n_cell + n_gene - 2)
    send_gram(0, gram0)

    def spread(i):
        @pl.loop(1, n_gene)
        def _(k):
            peer = lax.rem(g + k, n_gene)
            pltpu.make_async_remote_copy(
                src_ref=z_send.at[i, block(peer // 2, 8), block(peer % 2, 128)],
                dst_ref=z_recv.at[i, k],
                send_sem=z_send_sem.at[i],
                recv_sem=z_sem.at[i],
                device_id=(c, peer),
                device_id_type=MESH,
            ).start()

    def gather(i):
        wait_bytes(z_recv.at[i, pl.ds(1, n_gene - 1)], z_sem.at[i])
        total = z_send[i, block(z, 8), block(core, 128)]
        for k in range(1, n_gene):
            total = total + z_recv[i, k]
        place = z_full.at[block(z, 8), pl.ds(pl.multiple_of(i * TILE + core * 128, 128), 128)]
        place[...] = total
        to_genes(place, place, zg_send_sem.at[i], zg_sem.at[i])

    @pl.loop(0, chunks)
    def _(i):
        slot = lax.rem(i, 3)
        load(i, slot).wait()
        here = block(i)

        def tile(j, total):
            lanes = block(j)
            values = stage[slot, :, lanes] * mask_ref[i, j].astype(F32)
            top = values.astype(BF16)
            rest = (values - top.astype(F32)).astype(BF16)
            high[here, lanes] = top
            low[here, lanes] = rest
            return total + dot(start3[:, lanes], top, NT) + dot(start3[:, lanes], rest, NT)

        total = lax.fori_loop(0, tiles, tile, jnp.zeros((3 * BLOCK, TILE), F32), unroll=UNROLL)

        @pl.when(i + 3 < chunks)
        def _():
            load(i + 3, slot).start()

        z_send[i] = fold3(total)
        spread(i)

        @pl.when(i > 0)
        def _():
            gather(i - 1)

    _, inverse0 = factor(take_gram(0))

    def side_of(step, inverse, full, first, count):
        lanes = pl.ds(first * TILE, count * TILE)
        y3[step, pl.ds(0, 3 * BLOCK), lanes] = split3(small_product(inverse, full[:, lanes]))

    def back(step, left_rows, first, count, lanes):
        there = pl.ds(first * TILE, count * TILE)
        left = y3[step, pl.ds(0, left_rows), there]
        return dot(left, high[there, lanes], NN) + dot(left, low[there, lanes], NN)

    with_ones = 3 * BLOCK + 16
    early, middle = EARLY, chunks - 1

    def wait_chunks(first, last):
        for i in range(first, last):
            wait_bytes(z_recv.at[i, pl.ds(1, n_gene - 1)], zg_sem.at[i])

    wait_chunks(0, early)
    side_of(0, inverse0, z_full, 0, early)

    @pl.loop(0, tiles // 2)
    def _(t):
        lanes = block(t, 2 * TILE)
        image_acc[:, lanes] = back(0, with_ones, 0, early, lanes)

    gather(chunks - 1)
    wait_chunks(early, middle)
    side_of(0, inverse0, z_full, early, middle - early)

    @pl.loop(0, tiles // 2)
    def _(t):
        lanes = block(t, 2 * TILE)
        image_acc[:, lanes] += back(0, with_ones, early, middle - early, lanes)

    own = block(c)
    current = small_product(inverse0, start_ref[:, own])
    older = None
    inverse = inverse0
    wait_chunks(middle, chunks)
    side_of(0, inverse0, z_full, middle, chunks - middle)
    eye = lax.broadcasted_iota(jnp.int32, (BLOCK, BLOCK), 0) == lax.broadcasted_iota(jnp.int32, (BLOCK, BLOCK), 1)
    column_sums = None
    older_mean = None

    for step in range(2):
        if step == 0:
            stat = dot(y3[0], y3[0], NT)
        else:
            stat = dot(y3[1], jnp.concatenate([y3[1], y3[0]], axis=0), NT)
        row = fold_lanes(stat[3 * BLOCK : 3 * BLOCK + 8])
        stat = fold3(stat)
        stat_buf[step, c, 0] = pack(fold_lanes(stat))
        stat_buf[step, c, 1] = jnp.concatenate([row, jnp.zeros((8, 128 - BLOCK), F32)], axis=1)
        count = 2
        if step == 1:
            stat_buf[step, c, 2] = pack(fold_lanes(stat, with_ones))
            count = 3
        here = stat_buf.at[step, c, pl.ds(0, count)]
        to_cells(here, here, stat_send_sem.at[step], lambda k: stat_sem.at[step])

        sent = i_send if step == 0 else i_send2
        got = i_recv if step == 0 else i_recv2

        def image(k):
            owner = cell_at(k, 1)
            lanes = block(owner)
            if step == 0:
                product = image_acc[:, lanes] + back(0, with_ones, middle, chunks - middle, lanes)
                sent[k, pl.ds(BLOCK, 8), :] = product[3 * BLOCK : 3 * BLOCK + 8]
            else:
                product = back(1, 3 * BLOCK, 0, chunks, lanes)
            sent[k, pl.ds(0, BLOCK), :] = fold3(product)
            return owner

        def send_image(k, owner):
            pltpu.make_async_remote_copy(
                src_ref=sent.at[k],
                dst_ref=got.at[k],
                send_sem=rs_send_sem.at[step],
                recv_sem=rs_sem.at[step],
                device_id=(owner, g),
                device_id_type=MESH,
            ).start()

        @pl.loop(0, n_cell // 2)
        def _(t):
            one, two = n_cell - 1 - 2 * t, n_cell - 2 - 2 * t
            owner_one = image(one)
            owner_two = image(two)
            send_image(one, owner_one)

            @pl.when(t < n_cell // 2 - 1)
            def _():
                send_image(two, owner_two)

        wait_bytes(stat_buf.at[step, pl.ds(0, n_cell - 1), pl.ds(0, count)], stat_sem.at[step])
        stats = [sum_slots(stat_buf.at[step, :, k], n_cell) / cells for k in range(count)]
        mean_row = stats[1][0:1, 0:BLOCK]
        mean_column = jnp.sum(jnp.where(eye, mean_row, 0.0), axis=1, keepdims=True)
        alpha = unpack(stats[0]) - mean_column * mean_row
        small_ref[1 + step] = alpha

        wait_bytes(got.at[pl.ds(1, n_cell - 1)], rs_sem.at[step])
        piece = sent[0]
        for k in range(1, n_cell):
            piece = piece + got[k]
        if step == 0:
            column_sums = piece[BLOCK : BLOCK + 1]
        piece = (piece[0:BLOCK] - mean_column * column_sums) / cells
        piece = piece - small_product(alpha, current)
        if step > 0:
            prior = unpack(stats[2]) - mean_column * older_mean
            piece = piece - small_product(prior, older)
        place = resid.at[step, :, own]
        place[...] = piece

        if step == 0:
            to_cells(place, place, ag_send_sem.at[step], lambda k: ag_sem.at[step, k])
            older_mean = mean_row

            def multiply(lanes):
                left = split3(resid[step, :, lanes])
                resid3[:, lanes] = left
                return dot(left, high[:, lanes], NT) + dot(left, low[:, lanes], NT)

            def arrived(k):
                lanes = block(cell_at(k, -1))
                wait_bytes(resid.at[step, :, lanes], ag_sem.at[step, k])
                return lanes

            acc[...] = multiply(own)

            @pl.loop(0, n_cell // 2 - 1)
            def _(t):
                one = arrived(2 * t + 1)
                two = arrived(2 * t + 2)
                acc[...] += multiply(one) + multiply(two)

            acc[...] += multiply(arrived(n_cell - 1))
            z_send2[...] = fold3(acc)
            half = rows // 2

            @pl.loop(1, n_gene)
            def _(k):
                peer = lax.rem(g + k, n_gene)
                pltpu.make_async_remote_copy(
                    src_ref=z_send2.at[block(peer // 2, 8), block(peer % 2, half)],
                    dst_ref=z_recv2.at[k],
                    send_sem=z2_sems.at[0],
                    recv_sem=z2_sems.at[1],
                    device_id=(c, peer),
                    device_id_type=MESH,
                ).start()

            send_gram(1, pack(gram_of(resid3[...])))
            parts = z_recv2.at[pl.ds(1, n_gene - 1)]
            wait_bytes(parts, z2_sems.at[1])
            total = z_send2[block(z, 8), block(core, half)]
            for k in range(1, n_gene):
                total = total + z_recv2[k]
            place = z_full2.at[block(z, 8), block(core, half)]
            place[...] = total
            to_genes(place, place, z2_sems.at[2], z2_sems.at[3])
            upper, inverse = factor(take_gram(1))
            small_ref[3] = upper
            older = current
            current = small_product(inverse, piece)
            wait_bytes(parts, z2_sems.at[3])
            wait_bytes(parts, z2_sems.at[0])
            wait_bytes(parts, z2_sems.at[2])
            side_of(1, inverse, z_full2, 0, chunks)
        else:
            last_buf[c] = pack(gram_of(split3(piece)))
            here = last_buf.at[c]
            to_cells(here, here, last_sems.at[0], lambda k: last_sems.at[1])
            to_cells(place, place, ag_send_sem.at[step], lambda k: ag_sem.at[step, 0])
            wait_bytes(last_buf.at[pl.ds(0, n_cell - 1)], last_sems.at[1])
            send_gram(2, sum_slots(last_buf, n_cell))
            wait_bytes(resid.at[step, :, pl.ds(0, (n_cell - 1) * TILE)], ag_sem.at[step, 0])
            resid_ref[...] = resid[step]
            upper, inverse = factor(take_gram(2))
            small_ref[0] = inverse
            small_ref[4] = upper

    for step in range(3):
        wait_bytes(gram_buf.at[step, pl.ds(0, n_gene - 1)], gram_sems.at[step, 0])
    wait_bytes(last_buf.at[pl.ds(0, n_cell - 1)], last_sems.at[0])
    for i in range(chunks):
        wait_bytes(z_recv.at[i, pl.ds(1, n_gene - 1)], z_send_sem.at[i])
        wait_bytes(z_recv.at[i, pl.ds(1, n_gene - 1)], zg_send_sem.at[i])
    for step in range(2):
        wait_bytes(stat_buf.at[step, pl.ds(0, n_cell - 1), pl.ds(0, 2 + step)], stat_send_sem.at[step])
        wait_bytes((i_recv if step == 0 else i_recv2).at[pl.ds(1, n_cell - 1)], rs_send_sem.at[step])
        wait_bytes(resid.at[step, :, pl.ds(0, (n_cell - 1) * TILE)], ag_send_sem.at[step])


def finish(scale, small_ref, resid_ref, alphas_ref, betas_ref, next_ref):
    next_ref[...] = small_product(small_ref[0] * scale, resid_ref[...])
    alphas_ref[...] = small_ref[1:3]
    betas_ref[...] = small_ref[3:5]


def per_device(sizes, expression, tile_mask, start):
    n_cell, n_gene, rows, width = sizes
    chunks = rows // TILE
    vmem = pl.BlockSpec(memory_space=pltpu.VMEM)
    dma = pltpu.SemaphoreType.DMA
    small, resid = pl.pallas_call(
        functools.partial(kernel, sizes),
        out_shape=(
            jax.ShapeDtypeStruct((5, BLOCK, BLOCK), F32),
            jax.ShapeDtypeStruct((BLOCK, width), F32),
        ),
        in_specs=[pl.BlockSpec(memory_space=pl.ANY), pl.BlockSpec(memory_space=pltpu.SMEM), vmem],
        out_specs=(vmem, vmem),
        scratch_shapes=[
            pltpu.VMEM((rows, width), BF16),
            pltpu.VMEM((rows, width), BF16),
            pltpu.VMEM((3, TILE, width), F32),
            pltpu.VMEM((3 * BLOCK, width), BF16),
            pltpu.VMEM((3, n_gene, 8, 128), F32),
            pltpu.VMEM((n_cell, 8, 128), F32),
            pltpu.VMEM((chunks, BLOCK, TILE), F32),
            pltpu.VMEM((chunks, n_gene, 8, 128), F32),
            pltpu.VMEM((BLOCK, rows), F32),
            pltpu.VMEM((BLOCK, rows), F32),
            pltpu.VMEM((n_gene, 8, rows // 2), F32),
            pltpu.VMEM((BLOCK, rows), F32),
            pltpu.VMEM((2, 3 * BLOCK + 16, rows), BF16),
            pltpu.VMEM((2, n_cell, 3, 8, 128), F32),
            pltpu.VMEM((3 * BLOCK + 16, width), F32),
            pltpu.VMEM((n_cell, BLOCK + 8, TILE), F32),
            pltpu.VMEM((n_cell, BLOCK + 8, TILE), F32),
            pltpu.VMEM((n_cell, BLOCK, TILE), F32),
            pltpu.VMEM((n_cell, BLOCK, TILE), F32),
            pltpu.VMEM((2, BLOCK, width), F32),
            pltpu.VMEM((3 * BLOCK, width), BF16),
            pltpu.VMEM((3 * BLOCK, rows), F32),
            dma((3,)),
            dma((3, 2)),
            dma((2,)),
            dma((chunks,)),
            dma((chunks,)),
            dma((chunks,)),
            dma((chunks,)),
            dma((4,)),
            dma((2,)),
            dma((2,)),
            dma((2,)),
            dma((2,)),
            dma((2,)),
            dma((2, n_cell)),
        ],
        compiler_params=pltpu.CompilerParams(
            collective_id=0, has_side_effects=True, vmem_limit_bytes=60 * 2**20
        ),
        name="lanczos",
    )(expression, tile_mask, start.T)
    alphas, betas, fresh = pl.pallas_call(
        functools.partial(finish, math.sqrt(width * n_gene)),
        out_shape=(
            jax.ShapeDtypeStruct((2, BLOCK, BLOCK), F32),
            jax.ShapeDtypeStruct((2, BLOCK, BLOCK), F32),
            jax.ShapeDtypeStruct((BLOCK, width), F32),
        ),
        in_specs=[vmem, vmem],
        out_specs=(vmem, vmem, vmem),
        name="finish",
    )(small, resid)
    return alphas, betas, fresh.T


def solution(mesh):
    n_cell, n_gene = mesh.shape["cell"], mesh.shape["gene"]

    def run(expression, tile_mask, start):
        sizes = (n_cell, n_gene, expression.shape[0] // n_cell, expression.shape[1] // n_gene)
        return jax.shard_map(
            functools.partial(per_device, sizes),
            mesh=mesh,
            in_specs=(P("cell", "gene"), P("cell", "gene"), P("gene", None)),
            out_specs=(P(), P(), P("gene", None)),
            check_vma=False,
        )(expression, tile_mask, start)

    return run
```

```python
import functools
import math

import jax
import jax.numpy as jnp
from jax import lax
from jax.experimental import pallas as pl
from jax.experimental.pallas import tpu as pltpu
from jax.sharding import PartitionSpec as P

TILE = 256
BLOCK = 32
MESH = pl.DeviceIdType.MESH
F32 = jnp.float32
BF16 = jnp.bfloat16
FP8 = jnp.float8_e4m3fn
LOW_SCALE = 4096.0
GROUPS = ((0, 4), (4, 2))

NN = ((1,), (0,))
NT = ((1,), (1,))
SIDE = 4
ORDER = sorted(
    ((dy, dx) for dy in range(SIDE) for dx in range(SIDE)),
    key=lambda at: (min(at[0], SIDE - at[0]) + min(at[1], SIDE - at[1]), at),
)


def dot(left, right, dims):
    return lax.dot_general(left, right, (dims, ((), ())), preferred_element_type=F32)


def pieces(value):
    first = value.astype(BF16)
    rest = value - first.astype(F32)
    second = rest.astype(BF16)
    third = (rest - second.astype(F32)).astype(BF16)
    return first, second, third


def pieces8(value, scale):
    value = value * scale
    first = value.astype(FP8)
    second = ((value - first.astype(F32)) * 16.0).astype(FP8)
    return jnp.concatenate([first, second], axis=0)


def fold8(value):
    return value[0:BLOCK] + value[BLOCK : 2 * BLOCK] * (1.0 / 16.0)


def largest(values):
    top = functools.reduce(jnp.maximum, [jnp.max(jnp.abs(v), axis=0, keepdims=True) for v in values])
    return jnp.maximum(jnp.max(top, axis=1, keepdims=True), 1e-30)


def split3(value):
    return jnp.concatenate(pieces(value), axis=0)


def fold3(value):
    return value[0:BLOCK] + value[BLOCK : 2 * BLOCK] + value[2 * BLOCK : 3 * BLOCK]


def fold_lanes(value, at=0):
    a, b, d = (value[:, at + BLOCK * k : at + BLOCK * (k + 1)] for k in range(3))
    return a + b + d


def small_product(left, right):
    a1, a2, a3 = pieces(left)
    b1, b2, b3 = pieces(right)
    lhs = jnp.concatenate([a1, a2, a3, a1, a2, a1], axis=1)
    rhs = jnp.concatenate([b1, b1, b1, b2, b2, b3], axis=0)
    return dot(lhs, rhs, NN)


def gram_of(split):
    return fold_lanes(fold3(dot(split, split, NT)))


def pack(matrix):
    return jnp.concatenate([matrix[8 * k : 8 * (k + 1), :] for k in range(4)], axis=1)


def unpack(tile):
    return jnp.concatenate([tile[:, BLOCK * k : BLOCK * (k + 1)] for k in range(4)], axis=0)


def factor(gram):
    row_of = lax.broadcasted_iota(jnp.int32, (BLOCK, 128), 0)
    lane_of = lax.broadcasted_iota(jnp.int32, (BLOCK, 128), 1)
    both = jnp.concatenate([gram, jnp.zeros((BLOCK, 128 - BLOCK), F32)], axis=1)
    both = both + (lane_of == row_of + BLOCK).astype(F32)
    for k in range(BLOCK - 1):
        row = both[k : k + 1, :]
        scaled = row / row[:, k : k + 1]
        column = jnp.where(row_of[:, 0:1] > k, both[:, k : k + 1], 0.0)
        both = both - column * scaled
    diagonal = jnp.sum(jnp.where(lane_of == row_of, both, 0.0), axis=1, keepdims=True)
    both = both / jnp.sqrt(diagonal)
    upper = jnp.where(lane_of >= row_of, both, 0.0)
    return upper[:, 0:BLOCK], both[:, BLOCK : 2 * BLOCK]


def kernel(
    sizes,
    x_ref,
    mask_ref,
    start_ref,
    small_ref,
    resid_ref,
    high,
    low,
    stage,
    start3,
    start8,
    gram_buf,
    last_buf,
    z_send,
    z_recv,
    z_recv_b,
    z_full,
    z_send2,
    z_recv2,
    z_full2,
    y3,
    y8,
    stat_buf,
    image_acc,
    i_send,
    i_recv,
    i_send2,
    i_recv2,
    resid,
    resid3,
    resid8,
    load_sem,
    gram_sems,
    last_sems,
    z_send_sem,
    z_sem,
    zg_send_sem,
    zg_sem,
    z2_sems,
    stat_send_sem,
    stat_sem,
    rs_send_sem,
    rs_sem,
    ag_send_sem,
    ag_sem,
):
    n_cell, n_gene, rows, width = sizes
    cells = rows * n_cell
    chunks = rows // TILE
    tiles = width // TILE
    c = lax.axis_index("cell")
    g = lax.axis_index("gene")
    z, core = g // 2, g % 2
    y_at, x_at = c // SIDE, c % SIDE

    def cell_at(k, sign):
        if isinstance(k, int):
            dy, dx = ORDER[k]
        else:
            dy, dx = ORDER[0]
            for i in range(1, n_cell):
                dy = jnp.where(k == i, ORDER[i][0], dy)
                dx = jnp.where(k == i, ORDER[i][1], dx)
        return lax.rem(y_at + sign * dy + SIDE, SIDE) * SIDE + lax.rem(x_at + sign * dx + SIDE, SIDE)

    def block(index, size=TILE):
        return pl.ds(pl.multiple_of(index * size, size), size)

    def wait_bytes(ref, sem):
        pltpu.make_async_copy(ref, ref, sem).wait()

    def load(i, slot):
        return pltpu.make_async_copy(x_ref.at[block(i), :], stage.at[slot], load_sem.at[slot])

    for i in range(3):
        load(i, i).start()

    barrier = pltpu.get_barrier_semaphore()

    @pl.loop(1, n_cell)
    def _(k):
        pl.semaphore_signal(barrier, inc=1, device_id=(lax.rem(c + k, n_cell), g), device_id_type=MESH)

    @pl.loop(1, n_gene)
    def _(k):
        pl.semaphore_signal(barrier, inc=1, device_id=(c, lax.rem(g + k, n_gene)), device_id_type=MESH)

    def to_genes(src, dst, send_sem, recv_sem):
        @pl.loop(1, n_gene)
        def _(k):
            pltpu.make_async_remote_copy(
                src_ref=src,
                dst_ref=dst,
                send_sem=send_sem,
                recv_sem=recv_sem,
                device_id=(c, lax.rem(g + k, n_gene)),
                device_id_type=MESH,
            ).start()

    def to_cells(src, dst, send_sem, recv_sem_of):
        @pl.loop(1, n_cell)
        def _(t):
            k = n_cell - t
            pltpu.make_async_remote_copy(
                src_ref=src,
                dst_ref=dst,
                send_sem=send_sem,
                recv_sem=recv_sem_of(k),
                device_id=(cell_at(k, 1), g),
                device_id_type=MESH,
            ).start()

    def sum_slots(buf, count):
        total = buf[0]
        for k in range(1, count):
            total = total + buf[k]
        return total

    def send_gram(step, tile):
        gram_buf[step, g] = tile
        here = gram_buf.at[step, g]
        to_genes(here, here, gram_sems.at[step, 0], gram_sems.at[step, 1])

    def take_gram(step):
        wait_bytes(gram_buf.at[step, pl.ds(0, n_gene - 1)], gram_sems.at[step, 1])
        return unpack(sum_slots(gram_buf.at[step], n_gene))

    start3[...] = split3(start_ref[...])
    start8[...] = pieces8(start_ref[...], 64.0)
    gram0 = pack(gram_of(start3[...]))
    y3[0, pl.ds(3 * BLOCK, 16), :] = jnp.ones((16, rows), BF16)
    y3[1, pl.ds(3 * BLOCK, 16), :] = jnp.ones((16, rows), BF16)
    y8[pl.ds(2 * BLOCK, BLOCK), :] = jnp.ones((BLOCK, rows), FP8)
    pl.semaphore_wait(barrier, n_cell + n_gene - 2)
    send_gram(0, gram0)

    z_parts = (z_recv, z_recv_b)

    def spread(n):
        first, count = GROUPS[n]
        half = count * 128

        @pl.loop(1, n_gene)
        def _(k):
            peer = lax.rem(g + k, n_gene)
            pltpu.make_async_remote_copy(
                src_ref=z_send.at[
                    block(peer // 2, 8), pl.ds(pl.multiple_of(first * TILE + peer % 2 * half, 128), half)
                ],
                dst_ref=z_parts[n].at[k],
                send_sem=z_send_sem.at[n],
                recv_sem=z_sem.at[n],
                device_id=(c, peer),
                device_id_type=MESH,
            ).start()

    def gather(n):
        first, count = GROUPS[n]
        half = count * 128
        wait_bytes(z_parts[n].at[pl.ds(1, n_gene - 1)], z_sem.at[n])
        there = (block(z, 8), pl.ds(pl.multiple_of(first * TILE + core * half, 128), half))
        total = z_send[there]
        for k in range(1, n_gene):
            total = total + z_parts[n][k]
        place = z_full.at[there]
        place[...] = total
        to_genes(place, place, zg_send_sem.at[n], zg_sem.at[n])

    @pl.loop(0, chunks)
    def _(i):
        slot = lax.rem(i, 3)
        load(i, slot).wait()
        here = block(i)
        total = jnp.zeros((3 * BLOCK, TILE), F32)
        total8 = jnp.zeros((2 * BLOCK, TILE), F32)
        for j in range(tiles):
            lanes = pl.ds(j * TILE, TILE)
            values = stage[slot, :, lanes] * mask_ref[i, j].astype(F32)
            top = values.astype(BF16)
            rest = ((values - top.astype(F32)) * LOW_SCALE).astype(FP8)
            high[here, lanes] = top
            low[here, lanes] = rest
            total = total + dot(start3[:, lanes], top, NT)
            total8 = total8 + dot(start8[:, lanes], rest, NT)

        @pl.when(i + 3 < chunks)
        def _():
            load(i + 3, slot).start()

        z_send[:, here] = fold3(total) + fold8(total8) * (1.0 / (64.0 * LOW_SCALE))

        @pl.when(i == GROUPS[1][0] - 1)
        def _():
            spread(0)

        @pl.when(i == chunks - 1)
        def _():
            spread(1)
            gather(0)

    _, inverse0 = factor(take_gram(0))

    def side_of(step, inverse, full, first, count):
        lanes = pl.ds(first * TILE, count * TILE)
        side = small_product(inverse, full[:, lanes])
        top = largest([side])
        y3[step, pl.ds(0, 3 * BLOCK), lanes] = split3(side)
        y8[pl.ds(0, 2 * BLOCK), lanes] = pieces8(side, 256.0 / top)
        return top * (1.0 / (256.0 * LOW_SCALE))

    def back(step, undo, first, count, lanes):
        there = pl.ds(first * TILE, count * TILE)
        extra = step == 0
        product = dot(y3[step, pl.ds(0, 3 * BLOCK + 16 * extra), there], high[there, lanes], NN)
        product8 = dot(y8[pl.ds(0, 2 * BLOCK + BLOCK * extra), there], low[there, lanes], NN)
        part = fold3(product) + fold8(product8) * undo
        if extra:
            sums = product[3 * BLOCK : 3 * BLOCK + 8] + product8[2 * BLOCK : 2 * BLOCK + 8] * (1.0 / LOW_SCALE)
            part = jnp.concatenate([part, sums], axis=0)
        return part

    with_ones = 3 * BLOCK + 16
    wait_bytes(z_recv.at[pl.ds(1, n_gene - 1)], zg_sem.at[0])
    undo0 = side_of(0, inverse0, z_full, *GROUPS[0])

    def early(t):
        lanes = block(t, 2 * TILE)
        image_acc[:, lanes] = back(0, undo0, *GROUPS[0], lanes)

    pl.loop(0, 5)(early)
    gather(1)
    pl.loop(5, tiles // 2)(early)
    own = block(c)
    current = small_product(inverse0, start_ref[:, own])
    older = None
    inverse = inverse0
    wait_bytes(z_recv_b.at[pl.ds(1, n_gene - 1)], zg_sem.at[1])
    undo = side_of(0, inverse0, z_full, *GROUPS[1])
    eye = lax.broadcasted_iota(jnp.int32, (BLOCK, BLOCK), 0) == lax.broadcasted_iota(jnp.int32, (BLOCK, BLOCK), 1)
    column_sums = None
    older_mean = None

    for step in range(2):
        if step == 0:
            stat = dot(y3[0], y3[0], NT)
        else:
            stat = dot(y3[1], jnp.concatenate([y3[1], y3[0]], axis=0), NT)
        row = fold_lanes(stat[3 * BLOCK : 3 * BLOCK + 8])
        stat = fold3(stat)
        stat_buf[step, c, 0] = pack(fold_lanes(stat))
        stat_buf[step, c, 1] = jnp.concatenate([row, jnp.zeros((8, 128 - BLOCK), F32)], axis=1)
        count = 2
        if step == 1:
            stat_buf[step, c, 2] = pack(fold_lanes(stat, with_ones))
            count = 3
        here = stat_buf.at[step, c, pl.ds(0, count)]
        to_cells(here, here, stat_send_sem.at[step], lambda k: stat_sem.at[step])

        sent = i_send if step == 0 else i_send2
        got = i_recv if step == 0 else i_recv2

        def image(k):
            owner = cell_at(k, 1)
            lanes = block(owner)
            if step == 0:
                sent[k] = image_acc[:, lanes] + back(0, undo, *GROUPS[1], lanes)
            else:
                sent[k] = back(1, undo, 0, chunks, lanes)
            return owner

        def send_image(k, owner):
            pltpu.make_async_remote_copy(
                src_ref=sent.at[k],
                dst_ref=got.at[k],
                send_sem=rs_send_sem.at[step],
                recv_sem=rs_sem.at[step],
                device_id=(owner, g),
                device_id_type=MESH,
            ).start()

        @pl.loop(0, n_cell // 2)
        def _(t):
            one, two = n_cell - 1 - 2 * t, n_cell - 2 - 2 * t
            owner_one = image(one)
            owner_two = image(two)
            send_image(one, owner_one)

            @pl.when(t < n_cell // 2 - 1)
            def _():
                send_image(two, owner_two)

        wait_bytes(stat_buf.at[step, pl.ds(0, n_cell - 1), pl.ds(0, count)], stat_sem.at[step])
        stats = [sum_slots(stat_buf.at[step, :, k], n_cell) / cells for k in range(count)]
        mean_row = stats[1][0:1, 0:BLOCK]
        mean_column = jnp.sum(jnp.where(eye, mean_row, 0.0), axis=1, keepdims=True)
        alpha = unpack(stats[0]) - mean_column * mean_row
        small_ref[1 + step] = alpha

        wait_bytes(got.at[pl.ds(1, n_cell - 1)], rs_sem.at[step])
        piece = sent[0]
        for k in range(1, n_cell):
            piece = piece + got[k]
        if step == 0:
            column_sums = piece[BLOCK : BLOCK + 1]
        piece = (piece[0:BLOCK] - mean_column * column_sums) / cells
        piece = piece - small_product(alpha, current)
        if step > 0:
            prior = unpack(stats[2]) - mean_column * older_mean
            piece = piece - small_product(prior, older)
        place = resid.at[step, :, own]
        place[...] = piece

        if step == 0:
            to_cells(place, place, ag_send_sem.at[step], lambda k: ag_sem.at[step, k])
            older_mean = mean_row

            def arrived(k):
                lanes = block(cell_at(k, -1))
                wait_bytes(resid.at[step, :, lanes], ag_sem.at[step, k])
                return lanes

            for first, last in ((0, 5), (5, 11), (11, 16)):
                lanes_of = [own if k == 0 else arrived(k) for k in range(first, last)]
                values = [resid[step, :, lanes] for lanes in lanes_of]
                top = largest(values)
                for lanes, value in zip(lanes_of, values):
                    resid3[:, lanes] = split3(value)
                    resid8[:, lanes] = pieces8(value, 256.0 / top)
                undo = top * (1.0 / (256.0 * LOW_SCALE))

                @pl.loop(0, chunks // 2)
                def _(i):
                    for one in (2 * i, 2 * i + 1):
                        there = block(one)
                        total, total8 = 0.0, 0.0
                        for lanes in lanes_of:
                            total = total + dot(resid3[:, lanes], high[there, lanes], NT)
                            total8 = total8 + dot(resid8[:, lanes], low[there, lanes], NT)
                        total = fold3(total) + fold8(total8) * undo
                        z_send2[:, there] = total if first == 0 else z_send2[:, there] + total

            half = rows // 2

            @pl.loop(1, n_gene)
            def _(k):
                peer = lax.rem(g + k, n_gene)
                pltpu.make_async_remote_copy(
                    src_ref=z_send2.at[block(peer // 2, 8), block(peer % 2, half)],
                    dst_ref=z_recv2.at[k],
                    send_sem=z2_sems.at[0],
                    recv_sem=z2_sems.at[1],
                    device_id=(c, peer),
                    device_id_type=MESH,
                ).start()

            send_gram(1, pack(gram_of(resid3[...])))
            parts = z_recv2.at[pl.ds(1, n_gene - 1)]
            wait_bytes(parts, z2_sems.at[1])
            total = z_send2[block(z, 8), block(core, half)]
            for k in range(1, n_gene):
                total = total + z_recv2[k]
            place = z_full2.at[block(z, 8), block(core, half)]
            place[...] = total
            to_genes(place, place, z2_sems.at[2], z2_sems.at[3])
            upper, inverse = factor(take_gram(1))
            small_ref[3] = upper
            older = current
            current = small_product(inverse, piece)
            wait_bytes(parts, z2_sems.at[3])
            wait_bytes(parts, z2_sems.at[0])
            wait_bytes(parts, z2_sems.at[2])
            undo = side_of(1, inverse, z_full2, 0, chunks)
        else:
            last_buf[c] = pack(gram_of(split3(piece)))
            here = last_buf.at[c]
            to_cells(here, here, last_sems.at[0], lambda k: last_sems.at[1])
            to_cells(place, place, ag_send_sem.at[step], lambda k: ag_sem.at[step, 0])
            wait_bytes(last_buf.at[pl.ds(0, n_cell - 1)], last_sems.at[1])
            send_gram(2, sum_slots(last_buf, n_cell))
            wait_bytes(resid.at[step, :, pl.ds(0, (n_cell - 1) * TILE)], ag_sem.at[step, 0])
            resid_ref[...] = resid[step]
            upper, inverse = factor(take_gram(2))
            small_ref[0] = inverse
            small_ref[4] = upper

    for step in range(3):
        wait_bytes(gram_buf.at[step, pl.ds(0, n_gene - 1)], gram_sems.at[step, 0])
    wait_bytes(last_buf.at[pl.ds(0, n_cell - 1)], last_sems.at[0])
    for n in range(2):
        wait_bytes(z_parts[n].at[pl.ds(1, n_gene - 1)], z_send_sem.at[n])
        wait_bytes(z_parts[n].at[pl.ds(1, n_gene - 1)], zg_send_sem.at[n])
    for step in range(2):
        wait_bytes(stat_buf.at[step, pl.ds(0, n_cell - 1), pl.ds(0, 2 + step)], stat_send_sem.at[step])
        wait_bytes((i_recv if step == 0 else i_recv2).at[pl.ds(1, n_cell - 1)], rs_send_sem.at[step])
        wait_bytes(resid.at[step, :, pl.ds(0, (n_cell - 1) * TILE)], ag_send_sem.at[step])


def finish(scale, small_ref, resid_ref, alphas_ref, betas_ref, next_ref):
    next_ref[...] = small_product(small_ref[0] * scale, resid_ref[...])
    alphas_ref[...] = small_ref[1:3]
    betas_ref[...] = small_ref[3:5]


def per_device(sizes, expression, tile_mask, start):
    n_cell, n_gene, rows, width = sizes
    chunks = rows // TILE
    vmem = pl.BlockSpec(memory_space=pltpu.VMEM)
    dma = pltpu.SemaphoreType.DMA
    small, resid = pl.pallas_call(
        functools.partial(kernel, sizes),
        out_shape=(
            jax.ShapeDtypeStruct((5, BLOCK, BLOCK), F32),
            jax.ShapeDtypeStruct((BLOCK, width), F32),
        ),
        in_specs=[pl.BlockSpec(memory_space=pl.ANY), pl.BlockSpec(memory_space=pltpu.SMEM), vmem],
        out_specs=(vmem, vmem),
        scratch_shapes=[
            pltpu.VMEM((rows, width), BF16),
            pltpu.VMEM((rows, width), FP8),
            pltpu.VMEM((3, TILE, width), F32),
            pltpu.VMEM((3 * BLOCK, width), BF16),
            pltpu.VMEM((2 * BLOCK, width), FP8),
            pltpu.VMEM((3, n_gene, 8, 128), F32),
            pltpu.VMEM((n_cell, 8, 128), F32),
            pltpu.VMEM((BLOCK, rows), F32),
            pltpu.VMEM((n_gene, 8, GROUPS[0][1] * 128), F32),
            pltpu.VMEM((n_gene, 8, GROUPS[1][1] * 128), F32),
            pltpu.VMEM((BLOCK, rows), F32),
            pltpu.VMEM((BLOCK, rows), F32),
            pltpu.VMEM((n_gene, 8, rows // 2), F32),
            pltpu.VMEM((BLOCK, rows), F32),
            pltpu.VMEM((2, 3 * BLOCK + 16, rows), BF16),
            pltpu.VMEM((3 * BLOCK, rows), FP8),
            pltpu.VMEM((2, n_cell, 3, 8, 128), F32),
            pltpu.VMEM((BLOCK + 8, width), F32),
            pltpu.VMEM((n_cell, BLOCK + 8, TILE), F32),
            pltpu.VMEM((n_cell, BLOCK + 8, TILE), F32),
            pltpu.VMEM((n_cell, BLOCK, TILE), F32),
            pltpu.VMEM((n_cell, BLOCK, TILE), F32),
            pltpu.VMEM((2, BLOCK, width), F32),
            pltpu.VMEM((3 * BLOCK, width), BF16),
            pltpu.VMEM((2 * BLOCK, width), FP8),
            dma((3,)),
            dma((3, 2)),
            dma((2,)),
            dma((2,)),
            dma((2,)),
            dma((2,)),
            dma((2,)),
            dma((4,)),
            dma((2,)),
            dma((2,)),
            dma((2,)),
            dma((2,)),
            dma((2,)),
            dma((2, n_cell)),
        ],
        compiler_params=pltpu.CompilerParams(
            collective_id=0, has_side_effects=True, vmem_limit_bytes=60 * 2**20
        ),
        name="lanczos",
    )(expression, tile_mask, start.T)
    alphas, betas, fresh = pl.pallas_call(
        functools.partial(finish, math.sqrt(width * n_gene)),
        out_shape=(
            jax.ShapeDtypeStruct((2, BLOCK, BLOCK), F32),
            jax.ShapeDtypeStruct((2, BLOCK, BLOCK), F32),
            jax.ShapeDtypeStruct((BLOCK, width), F32),
        ),
        in_specs=[vmem, vmem],
        out_specs=(vmem, vmem, vmem),
        name="finish",
    )(small, resid)
    return alphas, betas, fresh.T


def solution(mesh):
    n_cell, n_gene = mesh.shape["cell"], mesh.shape["gene"]

    def run(expression, tile_mask, start):
        sizes = (n_cell, n_gene, expression.shape[0] // n_cell, expression.shape[1] // n_gene)
        return jax.shard_map(
            functools.partial(per_device, sizes),
            mesh=mesh,
            in_specs=(P("cell", "gene"), P("cell", "gene"), P("gene", None)),
            out_specs=(P(), P(), P("gene", None)),
            check_vma=False,
        )(expression, tile_mask, start)

    return run
```

```python
import functools
import math

import jax
import jax.numpy as jnp
from jax import lax
from jax.experimental import pallas as pl
from jax.experimental.pallas import tpu as pltpu
from jax.sharding import PartitionSpec as P

TILE = 256
BLOCK = 32
MESH = pl.DeviceIdType.MESH
F32 = jnp.float32
BF16 = jnp.bfloat16
FP8 = jnp.float8_e4m3fn
LOW_SCALE = 4096.0
GROUPS = ((0, 3), (3, 3))

NN = ((1,), (0,))
NT = ((1,), (1,))
SIDE = 4
ORDER = sorted(
    ((dy, dx) for dy in range(SIDE) for dx in range(SIDE)),
    key=lambda at: (min(at[0], SIDE - at[0]) + min(at[1], SIDE - at[1]), at),
)


def dot(left, right, dims):
    return lax.dot_general(left, right, (dims, ((), ())), preferred_element_type=F32)


def pieces(value):
    first = value.astype(BF16)
    rest = value - first.astype(F32)
    second = rest.astype(BF16)
    third = (rest - second.astype(F32)).astype(BF16)
    return first, second, third


def pieces8(value, scale):
    value = value * scale
    first = value.astype(FP8)
    second = ((value - first.astype(F32)) * 16.0).astype(FP8)
    return jnp.concatenate([first, second], axis=0)


def fold8(value):
    return value[0:BLOCK] + value[BLOCK : 2 * BLOCK] * (1.0 / 16.0)


def largest(values):
    top = functools.reduce(jnp.maximum, [jnp.max(jnp.abs(v), axis=0, keepdims=True) for v in values])
    return jnp.maximum(jnp.max(top, axis=1, keepdims=True), 1e-30)


def split3(value):
    return jnp.concatenate(pieces(value), axis=0)


def fold3(value):
    return value[0:BLOCK] + value[BLOCK : 2 * BLOCK] + value[2 * BLOCK : 3 * BLOCK]


def fold_lanes(value, at=0):
    a, b, d = (value[:, at + BLOCK * k : at + BLOCK * (k + 1)] for k in range(3))
    return a + b + d


def small_product(left, right):
    a1, a2, a3 = pieces(left)
    b1, b2, b3 = pieces(right)
    lhs = jnp.concatenate([a1, a2, a3, a1, a2, a1], axis=1)
    rhs = jnp.concatenate([b1, b1, b1, b2, b2, b3], axis=0)
    return dot(lhs, rhs, NN)


def gram_of(split):
    return fold_lanes(fold3(dot(split, split, NT)))


def pack(matrix):
    return jnp.concatenate([matrix[8 * k : 8 * (k + 1), :] for k in range(4)], axis=1)


def unpack(tile):
    return jnp.concatenate([tile[:, BLOCK * k : BLOCK * (k + 1)] for k in range(4)], axis=0)


def factor(gram):
    row_of = lax.broadcasted_iota(jnp.int32, (BLOCK, 128), 0)
    lane_of = lax.broadcasted_iota(jnp.int32, (BLOCK, 128), 1)
    both = jnp.concatenate([gram, jnp.zeros((BLOCK, 128 - BLOCK), F32)], axis=1)
    both = both + (lane_of == row_of + BLOCK).astype(F32)
    for k in range(BLOCK - 1):
        row = both[k : k + 1, :]
        scaled = row / row[:, k : k + 1]
        column = jnp.where(row_of[:, 0:1] > k, both[:, k : k + 1], 0.0)
        both = both - column * scaled
    diagonal = jnp.sum(jnp.where(lane_of == row_of, both, 0.0), axis=1, keepdims=True)
    both = both / jnp.sqrt(diagonal)
    upper = jnp.where(lane_of >= row_of, both, 0.0)
    return upper[:, 0:BLOCK], both[:, BLOCK : 2 * BLOCK]


def kernel(
    sizes,
    x_ref,
    mask_ref,
    start_ref,
    small_ref,
    resid_ref,
    high,
    low,
    stage,
    start3,
    start8,
    gram_buf,
    last_buf,
    z_send,
    z_recv,
    z_full,
    y3,
    y8,
    stat_buf,
    image_acc,
    i_send,
    i_recv,
    i_send2,
    i_recv2,
    resid,
    resid3,
    resid8,
    load_sem,
    gram_sems,
    last_sems,
    z_send_sem,
    z_sem,
    zg_send_sem,
    zg_sem,
    stat_send_sem,
    stat_sem,
    rs_send_sem,
    rs_sem,
    ag_send_sem,
    ag_sem,
    out_sem,
):
    n_cell, n_gene, rows, width = sizes
    cells = rows * n_cell
    chunks = rows // TILE
    tiles = width // TILE
    c = lax.axis_index("cell")
    g = lax.axis_index("gene")
    z, core = g // 2, g % 2
    y_at, x_at = c // SIDE, c % SIDE

    def cell_at(k, sign):
        if isinstance(k, int):
            dy, dx = ORDER[k]
        else:
            dy, dx = ORDER[0]
            for i in range(1, n_cell):
                dy = jnp.where(k == i, ORDER[i][0], dy)
                dx = jnp.where(k == i, ORDER[i][1], dx)
        return lax.rem(y_at + sign * dy + SIDE, SIDE) * SIDE + lax.rem(x_at + sign * dx + SIDE, SIDE)

    def block(index, size=TILE):
        return pl.ds(pl.multiple_of(index * size, size), size)

    def wait_bytes(ref, sem):
        pltpu.make_async_copy(ref, ref, sem).wait()

    def load(i, slot):
        return pltpu.make_async_copy(x_ref.at[block(i), :], stage.at[slot], load_sem.at[slot])

    for i in range(3):
        load(i, i).start()

    barrier = pltpu.get_barrier_semaphore()

    @pl.loop(1, n_cell)
    def _(k):
        pl.semaphore_signal(barrier, inc=1, device_id=(lax.rem(c + k, n_cell), g), device_id_type=MESH)

    @pl.loop(1, n_gene)
    def _(k):
        pl.semaphore_signal(barrier, inc=1, device_id=(c, lax.rem(g + k, n_gene)), device_id_type=MESH)

    def to_genes(src, dst, send_sem, recv_sem):
        @pl.loop(1, n_gene)
        def _(k):
            pltpu.make_async_remote_copy(
                src_ref=src,
                dst_ref=dst,
                send_sem=send_sem,
                recv_sem=recv_sem,
                device_id=(c, lax.rem(g + k, n_gene)),
                device_id_type=MESH,
            ).start()

    def to_cells(src, dst, send_sem, recv_sem_of, near=False):
        @pl.loop(1, n_cell)
        def _(t):
            k = t if near else n_cell - t
            pltpu.make_async_remote_copy(
                src_ref=src,
                dst_ref=dst,
                send_sem=send_sem,
                recv_sem=recv_sem_of(k),
                device_id=(cell_at(k, 1), g),
                device_id_type=MESH,
            ).start()

    def sum_slots(buf, count):
        total = buf[0]
        for k in range(1, count):
            total = total + buf[k]
        return total

    def send_gram(step, tile):
        gram_buf[step, g] = tile
        here = gram_buf.at[step, g]
        to_genes(here, here, gram_sems.at[step, 0], gram_sems.at[step, 1])

    def take_gram(step):
        wait_bytes(gram_buf.at[step, pl.ds(0, n_gene - 1)], gram_sems.at[step, 1])
        return unpack(sum_slots(gram_buf.at[step], n_gene))

    start3[...] = split3(start_ref[...])
    start8[...] = pieces8(start_ref[...], 64.0)
    gram0 = pack(gram_of(start3[...]))
    y3[0, pl.ds(3 * BLOCK, 16), :] = jnp.ones((16, rows), BF16)
    y3[1, pl.ds(3 * BLOCK, 16), :] = jnp.ones((16, rows), BF16)
    y8[pl.ds(2 * BLOCK, BLOCK), :] = jnp.ones((BLOCK, rows), FP8)
    pl.semaphore_wait(barrier, n_cell + n_gene - 2)
    send_gram(0, gram0)

    def spread(step, n):
        first, count = GROUPS[n]
        half = count * 128

        @pl.loop(1, n_gene)
        def _(k):
            peer = lax.rem(g + k, n_gene)
            pltpu.make_async_remote_copy(
                src_ref=z_send.at[
                    step, block(peer // 2, 8), pl.ds(pl.multiple_of(first * TILE + peer % 2 * half, 128), half)
                ],
                dst_ref=z_recv.at[step, n, k],
                send_sem=z_send_sem.at[step, n],
                recv_sem=z_sem.at[step, n],
                device_id=(c, peer),
                device_id_type=MESH,
            ).start()

    def gather(step, n):
        first, count = GROUPS[n]
        half = count * 128
        wait_bytes(z_recv.at[step, n, pl.ds(1, n_gene - 1)], z_sem.at[step, n])
        there = (step, block(z, 8), pl.ds(pl.multiple_of(first * TILE + core * half, 128), half))
        total = z_send[there]
        for k in range(1, n_gene):
            total = total + z_recv[step, n, k]
        place = z_full.at[there]
        place[...] = total
        to_genes(place, place, zg_send_sem.at[step, n], zg_sem.at[step, n])

    def gathered(step, n):
        wait_bytes(z_recv.at[step, n, pl.ds(1, n_gene - 1)], zg_sem.at[step, n])

    @pl.loop(0, chunks)
    def _(i):
        slot = lax.rem(i, 3)
        load(i, slot).wait()
        here = block(i)
        total = jnp.zeros((3 * BLOCK, TILE), F32)
        total8 = jnp.zeros((2 * BLOCK, TILE), F32)
        for j in range(tiles):
            lanes = pl.ds(j * TILE, TILE)
            values = stage[slot, :, lanes] * mask_ref[i, j].astype(F32)
            top = values.astype(BF16)
            rest = ((values - top.astype(F32)) * LOW_SCALE).astype(FP8)
            high[here, lanes] = top
            low[here, lanes] = rest
            total = total + dot(start3[:, lanes], top, NT)
            total8 = total8 + dot(start8[:, lanes], rest, NT)

        @pl.when(i + 3 < chunks)
        def _():
            load(i + 3, slot).start()

        z_send[0, :, here] = fold3(total) + fold8(total8) * (1.0 / (64.0 * LOW_SCALE))

        @pl.when(i == GROUPS[1][0] - 1)
        def _():
            spread(0, 0)

        @pl.when(i == chunks - 2)
        def _():
            gather(0, 0)

        @pl.when(i == chunks - 1)
        def _():
            spread(0, 1)

    _, inverse0 = factor(take_gram(0))

    def side_of(step, inverse, first, count):
        lanes = pl.ds(first * TILE, count * TILE)
        side = small_product(inverse, z_full[step, :, lanes])
        top = largest([side])
        y3[step, pl.ds(0, 3 * BLOCK), lanes] = split3(side)
        y8[pl.ds(0, 2 * BLOCK), lanes] = pieces8(side, 256.0 / top)
        return top * (1.0 / (256.0 * LOW_SCALE))

    def back(step, undo, first, count, lanes):
        there = pl.ds(first * TILE, count * TILE)
        extra = step == 0
        product = dot(y3[step, pl.ds(0, 3 * BLOCK + 16 * extra), there], high[there, lanes], NN)
        product8 = dot(y8[pl.ds(0, 2 * BLOCK + BLOCK * extra), there], low[there, lanes], NN)
        part = fold3(product) + fold8(product8) * undo
        if extra:
            sums = product[3 * BLOCK : 3 * BLOCK + 8] + product8[2 * BLOCK : 2 * BLOCK + 8] * (1.0 / LOW_SCALE)
            part = jnp.concatenate([part, sums], axis=0)
        return part

    with_ones = 3 * BLOCK + 16
    gathered(0, 0)
    undo0 = side_of(0, inverse0, *GROUPS[0])

    def early(t):
        lanes = block(t, 2 * TILE)
        image_acc[:, lanes] = back(0, undo0, *GROUPS[0], lanes)

    pl.loop(0, 5)(early)
    gather(0, 1)
    pl.loop(5, tiles // 2)(early)
    own = block(c)
    current = small_product(inverse0, start_ref[:, own])
    older = None
    inverse = inverse0
    gathered(0, 1)
    undo = side_of(0, inverse0, *GROUPS[1])
    eye = lax.broadcasted_iota(jnp.int32, (BLOCK, BLOCK), 0) == lax.broadcasted_iota(jnp.int32, (BLOCK, BLOCK), 1)
    column_sums = None
    older_mean = None

    for step in range(2):
        count = 2 + step

        def send_stat():
            if step == 0:
                stat = dot(y3[0], y3[0], NT)
            else:
                stat = dot(y3[1], jnp.concatenate([y3[1], y3[0]], axis=0), NT)
            row = fold_lanes(stat[3 * BLOCK : 3 * BLOCK + 8])
            stat = fold3(stat)
            stat_buf[step, c, 0] = pack(fold_lanes(stat))
            stat_buf[step, c, 1] = jnp.concatenate([row, jnp.zeros((8, 128 - BLOCK), F32)], axis=1)
            if step == 1:
                stat_buf[step, c, 2] = pack(fold_lanes(stat, with_ones))
            here = stat_buf.at[step, c, pl.ds(0, count)]
            to_cells(here, here, stat_send_sem.at[step], lambda k: stat_sem.at[step])

        sent = i_send if step == 0 else i_send2
        got = i_recv if step == 0 else i_recv2

        def image(k):
            owner = cell_at(k, 1)
            lanes = block(owner)
            if step == 0:
                sent[k] = image_acc[:, lanes] + back(0, undo, *GROUPS[1], lanes)
            else:
                sent[k] = back(1, undo, 0, chunks, lanes)
            return owner

        def send_image(k, owner):
            pltpu.make_async_remote_copy(
                src_ref=sent.at[k],
                dst_ref=got.at[k],
                send_sem=rs_send_sem.at[step],
                recv_sem=rs_sem.at[step],
                device_id=(owner, g),
                device_id_type=MESH,
            ).start()

        @pl.loop(0, n_cell // 2)
        def _(t):
            one, two = n_cell - 1 - 2 * t, n_cell - 2 - 2 * t
            owner_one = image(one)
            owner_two = image(two)
            send_image(one, owner_one)

            @pl.when(t < n_cell // 2 - 1)
            def _():
                send_image(two, owner_two)

            pl.when(t == 1)(send_stat)

        wait_bytes(stat_buf.at[step, pl.ds(0, n_cell - 1), pl.ds(0, count)], stat_sem.at[step])
        stats = [sum_slots(stat_buf.at[step, :, k], n_cell) / cells for k in range(count)]
        mean_row = stats[1][0:1, 0:BLOCK]
        mean_column = jnp.sum(jnp.where(eye, mean_row, 0.0), axis=1, keepdims=True)
        alpha = unpack(stats[0]) - mean_column * mean_row
        small_ref[1 + step] = alpha

        wait_bytes(got.at[pl.ds(1, n_cell - 1)], rs_sem.at[step])
        piece = sent[0]
        for k in range(1, n_cell):
            piece = piece + got[k]
        if step == 0:
            column_sums = piece[BLOCK : BLOCK + 1]
        piece = (piece[0:BLOCK] - mean_column * column_sums) / cells
        piece = piece - small_product(alpha, current)
        if step > 0:
            prior = unpack(stats[2]) - mean_column * older_mean
            piece = piece - small_product(prior, older)
        place = resid.at[step, :, own]
        place[...] = piece

        if step == 0:
            to_cells(place, place, ag_send_sem.at[step], lambda k: ag_sem.at[step, k], True)
            older_mean = mean_row

            def arrived(k):
                lanes = block(cell_at(k, -1))
                wait_bytes(resid.at[step, :, lanes], ag_sem.at[step, k])
                return lanes

            for first, last in ((0, 5), (5, 11), (11, 16)):
                lanes_of = [own if k == 0 else arrived(k) for k in range(first, last)]
                values = [resid[step, :, lanes] for lanes in lanes_of]
                top = largest(values)
                for lanes, value in zip(lanes_of, values):
                    resid3[:, lanes] = split3(value)
                    resid8[:, lanes] = pieces8(value, 256.0 / top)
                undo = top * (1.0 / (256.0 * LOW_SCALE))

                @pl.loop(0, 2)
                def _(i):
                    for one in (3 * i, 3 * i + 1, 3 * i + 2):
                        there = block(one)
                        total, total8 = 0.0, 0.0
                        for lanes in lanes_of:
                            total = total + dot(resid3[:, lanes], high[there, lanes], NT)
                            total8 = total8 + dot(resid8[:, lanes], low[there, lanes], NT)
                        total = fold3(total) + fold8(total8) * undo
                        z_send[1, :, there] = total if first == 0 else z_send[1, :, there] + total
                    if last == n_cell:
                        for n in range(2):
                            pl.when(i == n)(functools.partial(spread, 1, n))

            send_gram(1, pack(gram_of(resid3[...])))
            gather(1, 0)
            gather(1, 1)
            upper, inverse = factor(take_gram(1))
            small_ref[3] = upper
            older = current
            current = small_product(inverse, piece)
            gathered(1, 0)
            gathered(1, 1)
            undo = side_of(1, inverse, 0, chunks)
        else:
            last_buf[c] = pack(gram_of(split3(piece)))
            here = last_buf.at[c]
            to_cells(here, here, last_sems.at[0], lambda k: last_sems.at[1])
            to_cells(place, place, ag_send_sem.at[step], lambda k: ag_sem.at[step, 0])
            wait_bytes(last_buf.at[pl.ds(0, n_cell - 1)], last_sems.at[1])
            send_gram(2, sum_slots(last_buf, n_cell))
            wait_bytes(resid.at[step, :, pl.ds(0, (n_cell - 1) * TILE)], ag_sem.at[step, 0])
            pltpu.make_async_copy(resid.at[step], resid_ref, out_sem).start()
            upper, inverse = factor(take_gram(2))
            small_ref[0] = inverse
            small_ref[4] = upper
            pltpu.make_async_copy(resid.at[step], resid_ref, out_sem).wait()

    for step in range(3):
        wait_bytes(gram_buf.at[step, pl.ds(0, n_gene - 1)], gram_sems.at[step, 0])
    wait_bytes(last_buf.at[pl.ds(0, n_cell - 1)], last_sems.at[0])
    for step in range(2):
        for n in range(2):
            wait_bytes(z_recv.at[step, n, pl.ds(1, n_gene - 1)], z_send_sem.at[step, n])
            wait_bytes(z_recv.at[step, n, pl.ds(1, n_gene - 1)], zg_send_sem.at[step, n])
        wait_bytes(stat_buf.at[step, pl.ds(0, n_cell - 1), pl.ds(0, 2 + step)], stat_send_sem.at[step])
        wait_bytes((i_recv if step == 0 else i_recv2).at[pl.ds(1, n_cell - 1)], rs_send_sem.at[step])
        wait_bytes(resid.at[step, :, pl.ds(0, (n_cell - 1) * TILE)], ag_send_sem.at[step])


def finish(scale, small_ref, resid_ref, alphas_ref, betas_ref, next_ref):
    next_ref[...] = small_product(small_ref[0] * scale, resid_ref[...])
    alphas_ref[...] = small_ref[1:3]
    betas_ref[...] = small_ref[3:5]


def per_device(sizes, expression, tile_mask, start):
    n_cell, n_gene, rows, width = sizes
    chunks = rows // TILE
    vmem = pl.BlockSpec(memory_space=pltpu.VMEM)
    dma = pltpu.SemaphoreType.DMA
    small, resid = pl.pallas_call(
        functools.partial(kernel, sizes),
        out_shape=(
            jax.ShapeDtypeStruct((5, BLOCK, BLOCK), F32),
            jax.ShapeDtypeStruct((BLOCK, width), F32),
        ),
        in_specs=[pl.BlockSpec(memory_space=pl.ANY), pl.BlockSpec(memory_space=pltpu.SMEM), vmem],
        out_specs=(vmem, pl.BlockSpec(memory_space=pl.ANY)),
        scratch_shapes=[
            pltpu.VMEM((rows, width), BF16),
            pltpu.VMEM((rows, width), FP8),
            pltpu.VMEM((3, TILE, width), F32),
            pltpu.VMEM((3 * BLOCK, width), BF16),
            pltpu.VMEM((2 * BLOCK, width), FP8),
            pltpu.VMEM((3, n_gene, 8, 128), F32),
            pltpu.VMEM((n_cell, 8, 128), F32),
            pltpu.VMEM((2, BLOCK, rows), F32),
            pltpu.VMEM((2, 2, n_gene, 8, GROUPS[0][1] * 128), F32),
            pltpu.VMEM((2, BLOCK, rows), F32),
            pltpu.VMEM((2, 3 * BLOCK + 16, rows), BF16),
            pltpu.VMEM((3 * BLOCK, rows), FP8),
            pltpu.VMEM((2, n_cell, 3, 8, 128), F32),
            pltpu.VMEM((BLOCK + 8, width), F32),
            pltpu.VMEM((n_cell, BLOCK + 8, TILE), F32),
            pltpu.VMEM((n_cell, BLOCK + 8, TILE), F32),
            pltpu.VMEM((n_cell, BLOCK, TILE), F32),
            pltpu.VMEM((n_cell, BLOCK, TILE), F32),
            pltpu.VMEM((2, BLOCK, width), F32),
            pltpu.VMEM((3 * BLOCK, width), BF16),
            pltpu.VMEM((2 * BLOCK, width), FP8),
            dma((3,)),
            dma((3, 2)),
            dma((2,)),
            dma((2, 2)),
            dma((2, 2)),
            dma((2, 2)),
            dma((2, 2)),
            dma((2,)),
            dma((2,)),
            dma((2,)),
            dma((2,)),
            dma((2,)),
            dma((2, n_cell)),
            dma,
        ],
        compiler_params=pltpu.CompilerParams(
            collective_id=0, has_side_effects=True, vmem_limit_bytes=60 * 2**20
        ),
        name="lanczos",
    )(expression, tile_mask, start.T)
    alphas, betas, fresh = pl.pallas_call(
        functools.partial(finish, math.sqrt(width * n_gene)),
        out_shape=(
            jax.ShapeDtypeStruct((2, BLOCK, BLOCK), F32),
            jax.ShapeDtypeStruct((2, BLOCK, BLOCK), F32),
            jax.ShapeDtypeStruct((BLOCK, width), F32),
        ),
        in_specs=[vmem, vmem],
        out_specs=(vmem, vmem, vmem),
        name="finish",
    )(small, resid)
    return alphas, betas, fresh.T


def solution(mesh):
    n_cell, n_gene = mesh.shape["cell"], mesh.shape["gene"]

    def run(expression, tile_mask, start):
        sizes = (n_cell, n_gene, expression.shape[0] // n_cell, expression.shape[1] // n_gene)
        return jax.shard_map(
            functools.partial(per_device, sizes),
            mesh=mesh,
            in_specs=(P("cell", "gene"), P("cell", "gene"), P("gene", None)),
            out_specs=(P(), P(), P("gene", None)),
            check_vma=False,
        )(expression, tile_mask, start)

    return run
```

```python
import functools
import math

import jax
import jax.numpy as jnp
from jax import lax
from jax.experimental import pallas as pl
from jax.experimental.pallas import tpu as pltpu
from jax.sharding import PartitionSpec as P

TILE = 256
BLOCK = 32
MESH = pl.DeviceIdType.MESH
F32 = jnp.float32
BF16 = jnp.bfloat16
FP8 = jnp.float8_e4m3fn
LOW_SCALE = 4096.0
GROUPS = ((0, 3), (3, 3))

NN = ((1,), (0,))
NT = ((1,), (1,))
SIDE = 4
ORDER = sorted(
    ((dy, dx) for dy in range(SIDE) for dx in range(SIDE)),
    key=lambda at: (min(at[0], SIDE - at[0]) + min(at[1], SIDE - at[1]), at),
)


def dot(left, right, dims):
    return lax.dot_general(left, right, (dims, ((), ())), preferred_element_type=F32)


def pieces(value):
    first = value.astype(BF16)
    rest = value - first.astype(F32)
    second = rest.astype(BF16)
    third = (rest - second.astype(F32)).astype(BF16)
    return first, second, third


def pieces8(value, scale):
    value = value * scale
    first = value.astype(FP8)
    second = ((value - first.astype(F32)) * 16.0).astype(FP8)
    return jnp.concatenate([first, second], axis=0)


def fold8(value):
    return value[0:BLOCK] + value[BLOCK : 2 * BLOCK] * (1.0 / 16.0)


def largest(values):
    top = functools.reduce(jnp.maximum, [jnp.max(jnp.abs(v), axis=0, keepdims=True) for v in values])
    return jnp.maximum(jnp.max(top, axis=1, keepdims=True), 1e-30)


def split3(value):
    return jnp.concatenate(pieces(value), axis=0)


def fold3(value):
    return value[0:BLOCK] + value[BLOCK : 2 * BLOCK] + value[2 * BLOCK : 3 * BLOCK]


def fold_lanes(value, at=0):
    a, b, d = (value[:, at + BLOCK * k : at + BLOCK * (k + 1)] for k in range(3))
    return a + b + d


def small_product(left, right):
    a1, a2, a3 = pieces(left)
    b1, b2, b3 = pieces(right)
    lhs = jnp.concatenate([a1, a2, a3, a1, a2, a1], axis=1)
    rhs = jnp.concatenate([b1, b1, b1, b2, b2, b3], axis=0)
    return dot(lhs, rhs, NN)


def gram_of(split):
    return fold_lanes(fold3(dot(split, split, NT)))


def pack(matrix):
    return jnp.concatenate([matrix[8 * k : 8 * (k + 1), :] for k in range(4)], axis=1)


def unpack(tile):
    return jnp.concatenate([tile[:, BLOCK * k : BLOCK * (k + 1)] for k in range(4)], axis=0)


def factor(gram):
    row_of = lax.broadcasted_iota(jnp.int32, (BLOCK, 128), 0)
    lane_of = lax.broadcasted_iota(jnp.int32, (BLOCK, 128), 1)
    both = jnp.concatenate([gram, jnp.zeros((BLOCK, 128 - BLOCK), F32)], axis=1)
    both = both + (lane_of == row_of + BLOCK).astype(F32)
    for k in range(BLOCK - 1):
        row = both[k : k + 1, :]
        scaled = row / row[:, k : k + 1]
        column = jnp.where(row_of[:, 0:1] > k, both[:, k : k + 1], 0.0)
        both = both - column * scaled
    diagonal = jnp.sum(jnp.where(lane_of == row_of, both, 0.0), axis=1, keepdims=True)
    both = both / jnp.sqrt(diagonal)
    upper = jnp.where(lane_of >= row_of, both, 0.0)
    return upper[:, 0:BLOCK], both[:, BLOCK : 2 * BLOCK]


def kernel(
    sizes,
    x_ref,
    mask_ref,
    start_ref,
    small_ref,
    resid_ref,
    high,
    low,
    stage,
    start3,
    start8,
    gram_buf,
    last_buf,
    z_send,
    z_recv,
    z_full,
    y3,
    y8,
    stat_buf,
    image_acc,
    i_send,
    i_recv,
    i_send2,
    i_recv2,
    resid,
    resid3,
    resid8,
    load_sem,
    gram_sems,
    last_sems,
    z_send_sem,
    z_sem,
    zg_send_sem,
    zg_sem,
    stat_send_sem,
    stat_sem,
    rs_send_sem,
    rs_sem,
    ag_send_sem,
    ag_sem,
    out_sem,
):
    n_cell, n_gene, rows, width = sizes
    cells = rows * n_cell
    chunks = rows // TILE
    tiles = width // TILE
    c = lax.axis_index("cell")
    g = lax.axis_index("gene")
    z, core = g // 2, g % 2
    y_at, x_at = c // SIDE, c % SIDE

    def cell_at(k, sign):
        if isinstance(k, int):
            dy, dx = ORDER[k]
        else:
            dy, dx = ORDER[0]
            for i in range(1, n_cell):
                dy = jnp.where(k == i, ORDER[i][0], dy)
                dx = jnp.where(k == i, ORDER[i][1], dx)
        return lax.rem(y_at + sign * dy + SIDE, SIDE) * SIDE + lax.rem(x_at + sign * dx + SIDE, SIDE)

    def block(index, size=TILE):
        return pl.ds(pl.multiple_of(index * size, size), size)

    def wait_bytes(ref, sem):
        pltpu.make_async_copy(ref, ref, sem).wait()

    def load(i, slot):
        return pltpu.make_async_copy(x_ref.at[block(i), :], stage.at[slot], load_sem.at[slot])

    for i in range(3):
        load(i, i).start()

    barrier = pltpu.get_barrier_semaphore()

    @pl.loop(1, n_cell)
    def _(k):
        pl.semaphore_signal(barrier, inc=1, device_id=(lax.rem(c + k, n_cell), g), device_id_type=MESH)

    @pl.loop(1, n_gene)
    def _(k):
        pl.semaphore_signal(barrier, inc=1, device_id=(c, lax.rem(g + k, n_gene)), device_id_type=MESH)

    def to_genes(src, dst, send_sem, recv_sem):
        @pl.loop(1, n_gene)
        def _(k):
            pltpu.make_async_remote_copy(
                src_ref=src,
                dst_ref=dst,
                send_sem=send_sem,
                recv_sem=recv_sem,
                device_id=(c, lax.rem(g + k, n_gene)),
                device_id_type=MESH,
            ).start()

    def to_cells(src, dst, send_sem, recv_sem_of, near=False):
        @pl.loop(1, n_cell)
        def _(t):
            k = t if near else n_cell - t
            pltpu.make_async_remote_copy(
                src_ref=src,
                dst_ref=dst,
                send_sem=send_sem,
                recv_sem=recv_sem_of(k),
                device_id=(cell_at(k, 1), g),
                device_id_type=MESH,
            ).start()

    def sum_slots(buf, count):
        total = buf[0]
        for k in range(1, count):
            total = total + buf[k]
        return total

    def send_gram(step, tile):
        gram_buf[step, g] = tile
        here = gram_buf.at[step, g]
        to_genes(here, here, gram_sems.at[step, 0], gram_sems.at[step, 1])

    def take_gram(step):
        wait_bytes(gram_buf.at[step, pl.ds(0, n_gene - 1)], gram_sems.at[step, 1])
        return unpack(sum_slots(gram_buf.at[step], n_gene))

    start3[...] = split3(start_ref[...])
    start8[...] = pieces8(start_ref[...], 64.0)
    y3[0, pl.ds(3 * BLOCK, 16), :] = jnp.ones((16, rows), BF16)
    y3[1, pl.ds(3 * BLOCK, 16), :] = jnp.ones((16, rows), BF16)
    y8[pl.ds(2 * BLOCK, BLOCK), :] = jnp.ones((BLOCK, rows), FP8)

    def spread(step, n):
        first, count = GROUPS[n]
        half = count * 128

        @pl.loop(1, n_gene)
        def _(k):
            peer = lax.rem(g + k, n_gene)
            pltpu.make_async_remote_copy(
                src_ref=z_send.at[
                    step, block(peer // 2, 8), pl.ds(pl.multiple_of(first * TILE + peer % 2 * half, 128), half)
                ],
                dst_ref=z_recv.at[step, n, k],
                send_sem=z_send_sem.at[step, n],
                recv_sem=z_sem.at[step, n],
                device_id=(c, peer),
                device_id_type=MESH,
            ).start()

    def gather(step, n):
        first, count = GROUPS[n]
        half = count * 128
        wait_bytes(z_recv.at[step, n, pl.ds(1, n_gene - 1)], z_sem.at[step, n])
        there = (step, block(z, 8), pl.ds(pl.multiple_of(first * TILE + core * half, 128), half))
        total = z_send[there]
        for k in range(1, n_gene):
            total = total + z_recv[step, n, k]
        place = z_full.at[there]
        place[...] = total
        to_genes(place, place, zg_send_sem.at[step, n], zg_sem.at[step, n])

    def gathered(step, n):
        wait_bytes(z_recv.at[step, n, pl.ds(1, n_gene - 1)], zg_sem.at[step, n])

    @pl.loop(0, chunks)
    def _(i):
        slot = lax.rem(i, 3)
        load(i, slot).wait()
        here = block(i)
        total = jnp.zeros((3 * BLOCK, TILE), F32)
        total8 = jnp.zeros((2 * BLOCK, TILE), F32)
        for j in range(tiles):
            lanes = pl.ds(j * TILE, TILE)
            values = stage[slot, :, lanes] * mask_ref[i, j].astype(F32)
            top = values.astype(BF16)
            rest = ((values - top.astype(F32)) * LOW_SCALE).astype(FP8)
            high[here, lanes] = top
            low[here, lanes] = rest
            total = total + dot(start3[:, lanes], top, NT)
            total8 = total8 + dot(start8[:, lanes], rest, NT)

        @pl.when(i + 3 < chunks)
        def _():
            load(i + 3, slot).start()

        @pl.when(i == 1)
        def _():
            pl.semaphore_wait(barrier, n_cell + n_gene - 2)
            send_gram(0, pack(gram_of(start3[...])))

        z_send[0, :, here] = fold3(total) + fold8(total8) * (1.0 / (64.0 * LOW_SCALE))

        @pl.when(i == GROUPS[1][0] - 1)
        def _():
            spread(0, 0)

        @pl.when(i == chunks - 1)
        def _():
            spread(0, 1)
            gather(0, 0)

    _, inverse0 = factor(take_gram(0))
    current = small_product(inverse0, start_ref[:, block(c)])
    gather(0, 1)

    def side_of(step, inverse, first, count):
        lanes = pl.ds(first * TILE, count * TILE)
        side = small_product(inverse, z_full[step, :, lanes])
        top = largest([side])
        y3[step, pl.ds(0, 3 * BLOCK), lanes] = split3(side)
        y8[pl.ds(0, 2 * BLOCK), lanes] = pieces8(side, 256.0 / top)
        return top * (1.0 / (256.0 * LOW_SCALE))

    def back(step, undo, first, count, lanes):
        there = pl.ds(first * TILE, count * TILE)
        extra = step == 0
        product = dot(y3[step, pl.ds(0, 3 * BLOCK + 16 * extra), there], high[there, lanes], NN)
        product8 = dot(y8[pl.ds(0, 2 * BLOCK + BLOCK * extra), there], low[there, lanes], NN)
        part = fold3(product) + fold8(product8) * undo
        if extra:
            sums = product[3 * BLOCK : 3 * BLOCK + 8] + product8[2 * BLOCK : 2 * BLOCK + 8] * (1.0 / LOW_SCALE)
            part = jnp.concatenate([part, sums], axis=0)
        return part

    with_ones = 3 * BLOCK + 16
    gathered(0, 0)
    undo0 = side_of(0, inverse0, *GROUPS[0])

    def early(t):
        lanes = block(t, 2 * TILE)
        image_acc[:, lanes] = back(0, undo0, *GROUPS[0], lanes)

    pl.loop(0, tiles // 2)(early)
    own = block(c)
    older = None
    inverse = inverse0
    gathered(0, 1)
    undo = side_of(0, inverse0, *GROUPS[1])
    eye = lax.broadcasted_iota(jnp.int32, (BLOCK, BLOCK), 0) == lax.broadcasted_iota(jnp.int32, (BLOCK, BLOCK), 1)
    column_sums = None
    older_mean = None

    for step in range(2):
        count = 2 + step

        def send_stat():
            if step == 0:
                stat = dot(y3[0], y3[0], NT)
            else:
                stat = dot(y3[1], jnp.concatenate([y3[1], y3[0]], axis=0), NT)
            row = fold_lanes(stat[3 * BLOCK : 3 * BLOCK + 8])
            stat = fold3(stat)
            stat_buf[step, c, 0] = pack(fold_lanes(stat))
            stat_buf[step, c, 1] = jnp.concatenate([row, jnp.zeros((8, 128 - BLOCK), F32)], axis=1)
            if step == 1:
                stat_buf[step, c, 2] = pack(fold_lanes(stat, with_ones))
            here = stat_buf.at[step, c, pl.ds(0, count)]
            to_cells(here, here, stat_send_sem.at[step], lambda k: stat_sem.at[step])

        sent = i_send if step == 0 else i_send2
        got = i_recv if step == 0 else i_recv2

        def image(k):
            owner = cell_at(k, 1)
            lanes = block(owner)
            if step == 0:
                sent[k] = image_acc[:, lanes] + back(0, undo, *GROUPS[1], lanes)
            else:
                sent[k] = back(1, undo, 0, chunks, lanes)
            return owner

        def send_image(k, owner):
            pltpu.make_async_remote_copy(
                src_ref=sent.at[k],
                dst_ref=got.at[k],
                send_sem=rs_send_sem.at[step],
                recv_sem=rs_sem.at[step],
                device_id=(owner, g),
                device_id_type=MESH,
            ).start()

        @pl.loop(0, n_cell // 2)
        def _(t):
            one, two = n_cell - 1 - 2 * t, n_cell - 2 - 2 * t
            owner_one = image(one)
            owner_two = image(two)
            send_image(one, owner_one)

            @pl.when(t < n_cell // 2 - 1)
            def _():
                send_image(two, owner_two)

            pl.when(t == 1)(send_stat)

        wait_bytes(stat_buf.at[step, pl.ds(0, n_cell - 1), pl.ds(0, count)], stat_sem.at[step])
        stats = [sum_slots(stat_buf.at[step, :, k], n_cell) / cells for k in range(count)]
        mean_row = stats[1][0:1, 0:BLOCK]
        mean_column = jnp.sum(jnp.where(eye, mean_row, 0.0), axis=1, keepdims=True)
        alpha = unpack(stats[0]) - mean_column * mean_row
        small_ref[1 + step] = alpha

        wait_bytes(got.at[pl.ds(1, n_cell - 1)], rs_sem.at[step])
        piece = sent[0]
        for k in range(1, n_cell):
            piece = piece + got[k]
        if step == 0:
            column_sums = piece[BLOCK : BLOCK + 1]
        piece = (piece[0:BLOCK] - mean_column * column_sums) / cells
        piece = piece - small_product(alpha, current)
        if step > 0:
            prior = unpack(stats[2]) - mean_column * older_mean
            piece = piece - small_product(prior, older)
        place = resid.at[step, :, own]
        place[...] = piece

        if step == 0:
            to_cells(place, place, ag_send_sem.at[step], lambda k: ag_sem.at[step, k], True)
            older_mean = mean_row

            def arrived(k):
                lanes = block(cell_at(k, -1))
                wait_bytes(resid.at[step, :, lanes], ag_sem.at[step, k])
                return lanes

            for first, last in ((0, 5), (5, 11), (11, 16)):
                lanes_of = [own if k == 0 else arrived(k) for k in range(first, last)]
                values = [resid[step, :, lanes] for lanes in lanes_of]
                top = largest(values)
                for lanes, value in zip(lanes_of, values):
                    resid3[:, lanes] = split3(value)
                    resid8[:, lanes] = pieces8(value, 256.0 / top)
                undo = top * (1.0 / (256.0 * LOW_SCALE))

                @pl.loop(0, 2)
                def _(i):
                    for one in (3 * i, 3 * i + 1, 3 * i + 2):
                        there = block(one)
                        total, total8 = 0.0, 0.0
                        for lanes in lanes_of:
                            total = total + dot(resid3[:, lanes], high[there, lanes], NT)
                            total8 = total8 + dot(resid8[:, lanes], low[there, lanes], NT)
                        total = fold3(total) + fold8(total8) * undo
                        z_send[1, :, there] = total if first == 0 else z_send[1, :, there] + total
                    if last == n_cell:
                        for n in range(2):
                            pl.when(i == n)(functools.partial(spread, 1, n))

            send_gram(1, pack(gram_of(resid3[...])))
            gather(1, 0)
            gather(1, 1)
            upper, inverse = factor(take_gram(1))
            small_ref[3] = upper
            older = current
            current = small_product(inverse, piece)
            gathered(1, 0)
            gathered(1, 1)
            undo = side_of(1, inverse, 0, chunks)
        else:
            last_buf[c] = pack(gram_of(split3(piece)))
            here = last_buf.at[c]
            to_cells(here, here, last_sems.at[0], lambda k: last_sems.at[1])
            to_cells(place, place, ag_send_sem.at[step], lambda k: ag_sem.at[step, 0])
            wait_bytes(last_buf.at[pl.ds(0, n_cell - 1)], last_sems.at[1])
            send_gram(2, sum_slots(last_buf, n_cell))
            wait_bytes(resid.at[step, :, pl.ds(0, (n_cell - 1) * TILE)], ag_sem.at[step, 0])
            pltpu.make_async_copy(resid.at[step], resid_ref, out_sem).start()
            upper, inverse = factor(take_gram(2))
            small_ref[0] = inverse
            small_ref[4] = upper
            pltpu.make_async_copy(resid.at[step], resid_ref, out_sem).wait()

    for step in range(3):
        wait_bytes(gram_buf.at[step, pl.ds(0, n_gene - 1)], gram_sems.at[step, 0])
    wait_bytes(last_buf.at[pl.ds(0, n_cell - 1)], last_sems.at[0])
    for step in range(2):
        for n in range(2):
            wait_bytes(z_recv.at[step, n, pl.ds(1, n_gene - 1)], z_send_sem.at[step, n])
            wait_bytes(z_recv.at[step, n, pl.ds(1, n_gene - 1)], zg_send_sem.at[step, n])
        wait_bytes(stat_buf.at[step, pl.ds(0, n_cell - 1), pl.ds(0, 2 + step)], stat_send_sem.at[step])
        wait_bytes((i_recv if step == 0 else i_recv2).at[pl.ds(1, n_cell - 1)], rs_send_sem.at[step])
        wait_bytes(resid.at[step, :, pl.ds(0, (n_cell - 1) * TILE)], ag_send_sem.at[step])


def finish(scale, small_ref, resid_ref, alphas_ref, betas_ref, next_ref):
    next_ref[...] = small_product(small_ref[0] * scale, resid_ref[...])
    alphas_ref[...] = small_ref[1:3]
    betas_ref[...] = small_ref[3:5]


def per_device(sizes, expression, tile_mask, start):
    n_cell, n_gene, rows, width = sizes
    chunks = rows // TILE
    vmem = pl.BlockSpec(memory_space=pltpu.VMEM)
    dma = pltpu.SemaphoreType.DMA
    small, resid = pl.pallas_call(
        functools.partial(kernel, sizes),
        out_shape=(
            jax.ShapeDtypeStruct((5, BLOCK, BLOCK), F32),
            jax.ShapeDtypeStruct((BLOCK, width), F32),
        ),
        in_specs=[pl.BlockSpec(memory_space=pl.ANY), pl.BlockSpec(memory_space=pltpu.SMEM), vmem],
        out_specs=(vmem, pl.BlockSpec(memory_space=pl.ANY)),
        scratch_shapes=[
            pltpu.VMEM((rows, width), BF16),
            pltpu.VMEM((rows, width), FP8),
            pltpu.VMEM((3, TILE, width), F32),
            pltpu.VMEM((3 * BLOCK, width), BF16),
            pltpu.VMEM((2 * BLOCK, width), FP8),
            pltpu.VMEM((3, n_gene, 8, 128), F32),
            pltpu.VMEM((n_cell, 8, 128), F32),
            pltpu.VMEM((2, BLOCK, rows), F32),
            pltpu.VMEM((2, 2, n_gene, 8, GROUPS[0][1] * 128), F32),
            pltpu.VMEM((2, BLOCK, rows), F32),
            pltpu.VMEM((2, 3 * BLOCK + 16, rows), BF16),
            pltpu.VMEM((3 * BLOCK, rows), FP8),
            pltpu.VMEM((2, n_cell, 3, 8, 128), F32),
            pltpu.VMEM((BLOCK + 8, width), F32),
            pltpu.VMEM((n_cell, BLOCK + 8, TILE), F32),
            pltpu.VMEM((n_cell, BLOCK + 8, TILE), F32),
            pltpu.VMEM((n_cell, BLOCK, TILE), F32),
            pltpu.VMEM((n_cell, BLOCK, TILE), F32),
            pltpu.VMEM((2, BLOCK, width), F32),
            pltpu.VMEM((3 * BLOCK, width), BF16),
            pltpu.VMEM((2 * BLOCK, width), FP8),
            dma((3,)),
            dma((3, 2)),
            dma((2,)),
            dma((2, 2)),
            dma((2, 2)),
            dma((2, 2)),
            dma((2, 2)),
            dma((2,)),
            dma((2,)),
            dma((2,)),
            dma((2,)),
            dma((2,)),
            dma((2, n_cell)),
            dma,
        ],
        compiler_params=pltpu.CompilerParams(
            collective_id=0, has_side_effects=True, vmem_limit_bytes=60 * 2**20
        ),
        name="lanczos",
    )(expression, tile_mask, start.T)
    alphas, betas, fresh = pl.pallas_call(
        functools.partial(finish, math.sqrt(width * n_gene)),
        out_shape=(
            jax.ShapeDtypeStruct((2, BLOCK, BLOCK), F32),
            jax.ShapeDtypeStruct((2, BLOCK, BLOCK), F32),
            jax.ShapeDtypeStruct((BLOCK, width), F32),
        ),
        in_specs=[vmem, vmem],
        out_specs=(vmem, vmem, vmem),
        name="finish",
    )(small, resid)
    return alphas, betas, fresh.T


def solution(mesh):
    n_cell, n_gene = mesh.shape["cell"], mesh.shape["gene"]

    def run(expression, tile_mask, start):
        sizes = (n_cell, n_gene, expression.shape[0] // n_cell, expression.shape[1] // n_gene)
        return jax.shard_map(
            functools.partial(per_device, sizes),
            mesh=mesh,
            in_specs=(P("cell", "gene"), P("cell", "gene"), P("gene", None)),
            out_specs=(P(), P(), P("gene", None)),
            check_vma=False,
        )(expression, tile_mask, start)

    return run
```

```python
import functools
import math

import jax
import jax.numpy as jnp
from jax import lax
from jax.experimental import pallas as pl
from jax.experimental.pallas import tpu as pltpu
from jax.sharding import PartitionSpec as P

TILE = 256
BLOCK = 32
MESH = pl.DeviceIdType.MESH
F32 = jnp.float32
BF16 = jnp.bfloat16
FP8 = jnp.float8_e4m3fn
LOW_SCALE = 4096.0
PIVOTS = 8
GROUPS = ((0, 3), (3, 3))

NN = ((1,), (0,))
NT = ((1,), (1,))
SIDE = 4
ORDER = sorted(
    ((dy, dx) for dy in range(SIDE) for dx in range(SIDE)),
    key=lambda at: (min(at[0], SIDE - at[0]) + min(at[1], SIDE - at[1]), at),
)


def dot(left, right, dims):
    return lax.dot_general(left, right, (dims, ((), ())), preferred_element_type=F32)


def pieces(value):
    first = value.astype(BF16)
    rest = value - first.astype(F32)
    second = rest.astype(BF16)
    third = (rest - second.astype(F32)).astype(BF16)
    return first, second, third


def pieces8(value, scale):
    value = value * scale
    first = value.astype(FP8)
    second = ((value - first.astype(F32)) * 16.0).astype(FP8)
    return jnp.concatenate([first, second], axis=0)


def fold8(value):
    return value[0:BLOCK] + value[BLOCK : 2 * BLOCK] * (1.0 / 16.0)


def largest(values):
    top = functools.reduce(jnp.maximum, [jnp.max(jnp.abs(v), axis=0, keepdims=True) for v in values])
    return jnp.maximum(jnp.max(top, axis=1, keepdims=True), 1e-30)


def split3(value):
    return jnp.concatenate(pieces(value), axis=0)


def fold3(value):
    return value[0:BLOCK] + value[BLOCK : 2 * BLOCK] + value[2 * BLOCK : 3 * BLOCK]


def fold_lanes(value, at=0):
    a, b, d = (value[:, at + BLOCK * k : at + BLOCK * (k + 1)] for k in range(3))
    return a + b + d


def small_product(left, right):
    a1, a2, a3 = pieces(left)
    b1, b2, b3 = pieces(right)
    lhs = jnp.concatenate([a1, a2, a3, a1, a2, a1], axis=1)
    rhs = jnp.concatenate([b1, b1, b1, b2, b2, b3], axis=0)
    return dot(lhs, rhs, NN)


def gram_of(split):
    return fold_lanes(fold3(dot(split, split, NT)))


def pack(matrix):
    return jnp.concatenate([matrix[8 * k : 8 * (k + 1), :] for k in range(4)], axis=1)


def unpack(tile):
    return jnp.concatenate([tile[:, BLOCK * k : BLOCK * (k + 1)] for k in range(4)], axis=0)


def factor(gram):
    row_of = lax.broadcasted_iota(jnp.int32, (BLOCK, 128), 0)
    lane_of = lax.broadcasted_iota(jnp.int32, (BLOCK, 128), 1)
    both = jnp.concatenate([gram, jnp.zeros((BLOCK, 128 - BLOCK), F32)], axis=1)
    both = both + (lane_of == row_of + BLOCK).astype(F32)
    for first in range(0, BLOCK, PIVOTS):
        columns = [jnp.broadcast_to(both[:, first + p : first + p + 1], (BLOCK, 128)) for p in range(PIVOTS)]
        for p in range(PIVOTS):
            at = first + p
            factors = jnp.where(row_of > at, columns[p] * (1.0 / columns[p][at : at + 1, :]), 0.0)
            for q in range(p + 1, PIVOTS):
                columns[q] = columns[q] - factors * columns[q][at : at + 1, :]
            both = both - factors * both[at : at + 1, :]
    diagonal = jnp.sum(jnp.where(lane_of == row_of, both, 0.0), axis=1, keepdims=True)
    both = both / jnp.sqrt(diagonal)
    upper = jnp.where(lane_of >= row_of, both, 0.0)
    return upper[:, 0:BLOCK], both[:, BLOCK : 2 * BLOCK]


def kernel(
    sizes,
    x_ref,
    mask_ref,
    start_ref,
    small_ref,
    resid_ref,
    high,
    low,
    stage,
    start3,
    start8,
    gram_buf,
    last_buf,
    z_send,
    z_recv,
    z_full,
    y3,
    y8,
    stat_buf,
    image_acc,
    i_send,
    i_recv,
    column_part,
    column_recv,
    resid,
    resid3,
    resid8,
    load_sem,
    gram_sems,
    last_sems,
    z_send_sem,
    z_sem,
    zg_send_sem,
    zg_sem,
    stat_send_sem,
    stat_sem,
    rs_send_sem,
    rs_sem,
    ag_send_sem,
    ag_sem,
    out_sem,
    column_sems,
):
    n_cell, n_gene, rows, width = sizes
    cells = rows * n_cell
    chunks = rows // TILE
    tiles = width // TILE
    c = lax.axis_index("cell")
    g = lax.axis_index("gene")
    z, core = g // 2, g % 2
    y_at, x_at = c // SIDE, c % SIDE

    def cell_at(k, sign):
        if isinstance(k, int):
            dy, dx = ORDER[k]
        else:
            dy, dx = ORDER[0]
            for i in range(1, n_cell):
                dy = jnp.where(k == i, ORDER[i][0], dy)
                dx = jnp.where(k == i, ORDER[i][1], dx)
        return lax.rem(y_at + sign * dy + SIDE, SIDE) * SIDE + lax.rem(x_at + sign * dx + SIDE, SIDE)

    def block(index, size=TILE):
        return pl.ds(pl.multiple_of(index * size, size), size)

    def wait_bytes(ref, sem):
        pltpu.make_async_copy(ref, ref, sem).wait()

    def load(i, slot):
        return pltpu.make_async_copy(x_ref.at[block(i), :], stage.at[slot], load_sem.at[slot])

    for i in range(3):
        load(i, i).start()

    barrier = pltpu.get_barrier_semaphore()

    @pl.loop(1, n_cell)
    def _(k):
        pl.semaphore_signal(barrier, inc=1, device_id=(lax.rem(c + k, n_cell), g), device_id_type=MESH)

    @pl.loop(1, n_gene)
    def _(k):
        pl.semaphore_signal(barrier, inc=1, device_id=(c, lax.rem(g + k, n_gene)), device_id_type=MESH)

    def to_genes(src, dst, send_sem, recv_sem):
        @pl.loop(1, n_gene)
        def _(k):
            pltpu.make_async_remote_copy(
                src_ref=src,
                dst_ref=dst,
                send_sem=send_sem,
                recv_sem=recv_sem,
                device_id=(c, lax.rem(g + k, n_gene)),
                device_id_type=MESH,
            ).start()

    def to_cells(src, dst, send_sem, recv_sem_of, near=False):
        @pl.loop(1, n_cell)
        def _(t):
            k = t if near else n_cell - t
            pltpu.make_async_remote_copy(
                src_ref=src,
                dst_ref=dst,
                send_sem=send_sem,
                recv_sem=recv_sem_of(k),
                device_id=(cell_at(k, 1), g),
                device_id_type=MESH,
            ).start()

    def sum_slots(buf, count):
        total = buf[0]
        for k in range(1, count):
            total = total + buf[k]
        return total

    def send_gram(step, tile):
        gram_buf[step, g] = tile
        here = gram_buf.at[step, g]
        to_genes(here, here, gram_sems.at[step, 0], gram_sems.at[step, 1])

    def take_gram(step):
        wait_bytes(gram_buf.at[step, pl.ds(0, n_gene - 1)], gram_sems.at[step, 1])
        return unpack(sum_slots(gram_buf.at[step], n_gene))

    start3[...] = split3(start_ref[...])
    start8[...] = pieces8(start_ref[...], 64.0)
    y3[0, pl.ds(3 * BLOCK, 16), :] = jnp.ones((16, rows), BF16)
    y3[1, pl.ds(3 * BLOCK, 16), :] = jnp.ones((16, rows), BF16)
    column_part[...] = jnp.zeros((8, width), F32)

    def spread(step, n):
        first, count = GROUPS[n]
        half = count * 128

        @pl.loop(1, n_gene)
        def _(k):
            peer = lax.rem(g + k, n_gene)
            pltpu.make_async_remote_copy(
                src_ref=z_send.at[
                    step, block(peer // 2, 8), pl.ds(pl.multiple_of(first * TILE + peer % 2 * half, 128), half)
                ],
                dst_ref=z_recv.at[step, n, k],
                send_sem=z_send_sem.at[step, n],
                recv_sem=z_sem.at[step, n],
                device_id=(c, peer),
                device_id_type=MESH,
            ).start()

    def gather(step, n):
        first, count = GROUPS[n]
        half = count * 128
        wait_bytes(z_recv.at[step, n, pl.ds(1, n_gene - 1)], z_sem.at[step, n])
        there = (step, block(z, 8), pl.ds(pl.multiple_of(first * TILE + core * half, 128), half))
        total = z_send[there]
        for k in range(1, n_gene):
            total = total + z_recv[step, n, k]
        place = z_full.at[there]
        place[...] = total
        to_genes(place, place, zg_send_sem.at[step, n], zg_sem.at[step, n])

    def gathered(step, n):
        wait_bytes(z_recv.at[step, n, pl.ds(1, n_gene - 1)], zg_sem.at[step, n])

    @pl.loop(0, chunks)
    def _(i):
        slot = lax.rem(i, 3)
        load(i, slot).wait()
        here = block(i)
        total = jnp.zeros((3 * BLOCK, TILE), F32)
        total8 = jnp.zeros((2 * BLOCK, TILE), F32)
        for j in range(tiles):
            lanes = pl.ds(j * TILE, TILE)
            values = stage[slot, :, lanes] * mask_ref[i, j].astype(F32)
            top = values.astype(BF16)
            rest = ((values - top.astype(F32)) * LOW_SCALE).astype(FP8)
            column_part[:, lanes] += jnp.sum(values.reshape(TILE // 8, 8, TILE), axis=0)
            high[here, lanes] = top
            low[here, lanes] = rest
            total = total + dot(start3[:, lanes], top, NT)
            total8 = total8 + dot(start8[:, lanes], rest, NT)

        @pl.when(i + 3 < chunks)
        def _():
            load(i + 3, slot).start()

        @pl.when(i == 1)
        def _():
            pl.semaphore_wait(barrier, n_cell + n_gene - 2)
            send_gram(0, pack(gram_of(start3[...])))

        z_send[0, :, here] = fold3(total) + fold8(total8) * (1.0 / (64.0 * LOW_SCALE))

        @pl.when(i == GROUPS[1][0] - 1)
        def _():
            spread(0, 0)

        @pl.when(i == chunks - 1)
        def _():
            spread(0, 1)
            gather(0, 0)

    _, inverse0 = factor(take_gram(0))
    current = small_product(inverse0, start_ref[:, block(c)])
    gather(0, 1)

    @pl.loop(1, n_cell)
    def _(k):
        owner = cell_at(k, 1)
        pltpu.make_async_remote_copy(
            src_ref=column_part.at[:, block(owner)],
            dst_ref=column_recv.at[k],
            send_sem=column_sems.at[0],
            recv_sem=column_sems.at[1],
            device_id=(owner, g),
            device_id_type=MESH,
        ).start()


    def side_of(step, inverse, first, count):
        lanes = pl.ds(first * TILE, count * TILE)
        side = small_product(inverse, z_full[step, :, lanes])
        top = largest([side])
        y3[step, pl.ds(0, 3 * BLOCK), lanes] = split3(side)
        y8[:, lanes] = pieces8(side, 256.0 / top)
        return top * (1.0 / (256.0 * LOW_SCALE))

    def back(step, undo, first, count, lanes):
        there = pl.ds(first * TILE, count * TILE)
        product = dot(y3[step, pl.ds(0, 3 * BLOCK), there], high[there, lanes], NN)
        product8 = dot(y8[:, there], low[there, lanes], NN)
        return fold3(product) + fold8(product8) * undo

    with_ones = 3 * BLOCK + 16
    gathered(0, 0)
    undo0 = side_of(0, inverse0, *GROUPS[0])

    def early(t):
        lanes = block(t, 2 * TILE)
        image_acc[:, lanes] = back(0, undo0, *GROUPS[0], lanes)

    pl.loop(0, tiles // 2)(early)
    own = block(c)
    column_sums = None
    older = None
    inverse = inverse0
    gathered(0, 1)
    undo = side_of(0, inverse0, *GROUPS[1])
    eye = lax.broadcasted_iota(jnp.int32, (BLOCK, BLOCK), 0) == lax.broadcasted_iota(jnp.int32, (BLOCK, BLOCK), 1)
    older_mean = None

    for step in range(2):
        count = 2 + step

        def send_stat():
            if step == 0:
                stat = dot(y3[0], y3[0], NT)
            else:
                stat = dot(y3[1], jnp.concatenate([y3[1], y3[0]], axis=0), NT)
            row = fold_lanes(stat[3 * BLOCK : 3 * BLOCK + 8])
            stat = fold3(stat)
            stat_buf[step, c, 0] = pack(fold_lanes(stat))
            stat_buf[step, c, 1] = jnp.concatenate([row, jnp.zeros((8, 128 - BLOCK), F32)], axis=1)
            if step == 1:
                stat_buf[step, c, 2] = pack(fold_lanes(stat, with_ones))
            here = stat_buf.at[step, c, pl.ds(0, count)]
            to_cells(here, here, stat_send_sem.at[step], lambda k: stat_sem.at[step])

        sent, got = i_send.at[step], i_recv.at[step]

        def image(k):
            owner = cell_at(k, 1)
            lanes = block(owner)
            if step == 0:
                sent[k] = image_acc[:, lanes] + back(0, undo, *GROUPS[1], lanes)
            else:
                sent[k] = back(1, undo, 0, chunks, lanes)
            return owner

        def send_image(k, owner):
            pltpu.make_async_remote_copy(
                src_ref=sent.at[k],
                dst_ref=got.at[k],
                send_sem=rs_send_sem.at[step],
                recv_sem=rs_sem.at[step],
                device_id=(owner, g),
                device_id_type=MESH,
            ).start()

        @pl.loop(0, n_cell // 2)
        def _(t):
            one, two = n_cell - 1 - 2 * t, n_cell - 2 - 2 * t
            owner_one = image(one)
            owner_two = image(two)
            send_image(one, owner_one)

            @pl.when(t < n_cell // 2 - 1)
            def _():
                send_image(two, owner_two)

            pl.when(t == 1)(send_stat)

        if step == 0:
            wait_bytes(column_recv.at[pl.ds(1, n_cell - 1)], column_sems.at[1])
            column_sums = column_part[:, own]
            for k in range(1, n_cell):
                column_sums = column_sums + column_recv[k]
            column_sums = jnp.sum(column_sums, axis=0, keepdims=True)

        wait_bytes(stat_buf.at[step, pl.ds(0, n_cell - 1), pl.ds(0, count)], stat_sem.at[step])
        stats = [sum_slots(stat_buf.at[step, :, k], n_cell) / cells for k in range(count)]
        mean_row = stats[1][0:1, 0:BLOCK]
        mean_column = jnp.sum(jnp.where(eye, mean_row, 0.0), axis=1, keepdims=True)
        alpha = unpack(stats[0]) - mean_column * mean_row
        small_ref[1 + step] = alpha

        wait_bytes(got.at[pl.ds(1, n_cell - 1)], rs_sem.at[step])
        piece = sent[0]
        for k in range(1, n_cell):
            piece = piece + got[k]
        piece = (piece - mean_column * column_sums) / cells
        piece = piece - small_product(alpha, current)
        if step > 0:
            prior = unpack(stats[2]) - mean_column * older_mean
            piece = piece - small_product(prior, older)
        place = resid.at[step, :, own]
        place[...] = piece

        if step == 0:
            to_cells(place, place, ag_send_sem.at[step], lambda k: ag_sem.at[step, k], True)
            older_mean = mean_row

            def arrived(k):
                lanes = block(cell_at(k, -1))
                wait_bytes(resid.at[step, :, lanes], ag_sem.at[step, k])
                return lanes

            for first, last in ((0, 5), (5, 11), (11, 16)):
                lanes_of = [own if k == 0 else arrived(k) for k in range(first, last)]
                values = [resid[step, :, lanes] for lanes in lanes_of]
                top = largest(values)
                for lanes, value in zip(lanes_of, values):
                    resid3[:, lanes] = split3(value)
                    resid8[:, lanes] = pieces8(value, 256.0 / top)
                undo = top * (1.0 / (256.0 * LOW_SCALE))

                @pl.loop(0, 2)
                def _(i):
                    for one in (3 * i, 3 * i + 1, 3 * i + 2):
                        there = block(one)
                        total, total8 = 0.0, 0.0
                        for lanes in lanes_of:
                            total = total + dot(resid3[:, lanes], high[there, lanes], NT)
                            total8 = total8 + dot(resid8[:, lanes], low[there, lanes], NT)
                        total = fold3(total) + fold8(total8) * undo
                        z_send[1, :, there] = total if first == 0 else z_send[1, :, there] + total
                    if last == n_cell:
                        for n in range(2):
                            pl.when(i == n)(functools.partial(spread, 1, n))

            send_gram(1, pack(gram_of(resid3[...])))
            gather(1, 0)
            gather(1, 1)
            upper, inverse = factor(take_gram(1))
            small_ref[3] = upper
            older = current
            current = small_product(inverse, piece)
            gathered(1, 0)
            gathered(1, 1)
            undo = side_of(1, inverse, 0, chunks)
        else:
            last_buf[c] = pack(gram_of(split3(piece)))
            here = last_buf.at[c]
            to_cells(here, here, last_sems.at[0], lambda k: last_sems.at[1])
            to_cells(place, place, ag_send_sem.at[step], lambda k: ag_sem.at[step, 0])
            wait_bytes(last_buf.at[pl.ds(0, n_cell - 1)], last_sems.at[1])
            send_gram(2, sum_slots(last_buf, n_cell))
            wait_bytes(resid.at[step, :, pl.ds(0, (n_cell - 1) * TILE)], ag_sem.at[step, 0])
            pltpu.make_async_copy(resid.at[step], resid_ref, out_sem).start()
            upper, inverse = factor(take_gram(2))
            small_ref[0] = inverse
            small_ref[4] = upper
            pltpu.make_async_copy(resid.at[step], resid_ref, out_sem).wait()

    wait_bytes(column_recv.at[pl.ds(1, n_cell - 1)], column_sems.at[0])
    for step in range(3):
        wait_bytes(gram_buf.at[step, pl.ds(0, n_gene - 1)], gram_sems.at[step, 0])
    wait_bytes(last_buf.at[pl.ds(0, n_cell - 1)], last_sems.at[0])
    for step in range(2):
        for n in range(2):
            wait_bytes(z_recv.at[step, n, pl.ds(1, n_gene - 1)], z_send_sem.at[step, n])
            wait_bytes(z_recv.at[step, n, pl.ds(1, n_gene - 1)], zg_send_sem.at[step, n])
        wait_bytes(stat_buf.at[step, pl.ds(0, n_cell - 1), pl.ds(0, 2 + step)], stat_send_sem.at[step])
        wait_bytes(i_recv.at[step, pl.ds(1, n_cell - 1)], rs_send_sem.at[step])
        wait_bytes(resid.at[step, :, pl.ds(0, (n_cell - 1) * TILE)], ag_send_sem.at[step])


def finish(scale, small_ref, resid_ref, alphas_ref, betas_ref, next_ref):
    next_ref[...] = small_product(small_ref[0] * scale, resid_ref[...])
    alphas_ref[...] = small_ref[1:3]
    betas_ref[...] = small_ref[3:5]


def per_device(sizes, expression, tile_mask, start):
    n_cell, n_gene, rows, width = sizes
    chunks = rows // TILE
    vmem = pl.BlockSpec(memory_space=pltpu.VMEM)
    dma = pltpu.SemaphoreType.DMA
    small, resid = pl.pallas_call(
        functools.partial(kernel, sizes),
        out_shape=(
            jax.ShapeDtypeStruct((5, BLOCK, BLOCK), F32),
            jax.ShapeDtypeStruct((BLOCK, width), F32),
        ),
        in_specs=[pl.BlockSpec(memory_space=pl.ANY), pl.BlockSpec(memory_space=pltpu.SMEM), vmem],
        out_specs=(vmem, pl.BlockSpec(memory_space=pl.ANY)),
        scratch_shapes=[
            pltpu.VMEM((rows, width), BF16),
            pltpu.VMEM((rows, width), FP8),
            pltpu.VMEM((3, TILE, width), F32),
            pltpu.VMEM((3 * BLOCK, width), BF16),
            pltpu.VMEM((2 * BLOCK, width), FP8),
            pltpu.VMEM((3, n_gene, 8, 128), F32),
            pltpu.VMEM((n_cell, 8, 128), F32),
            pltpu.VMEM((2, BLOCK, rows), F32),
            pltpu.VMEM((2, 2, n_gene, 8, GROUPS[0][1] * 128), F32),
            pltpu.VMEM((2, BLOCK, rows), F32),
            pltpu.VMEM((2, 3 * BLOCK + 16, rows), BF16),
            pltpu.VMEM((2 * BLOCK, rows), FP8),
            pltpu.VMEM((2, n_cell, 3, 8, 128), F32),
            pltpu.VMEM((BLOCK, width), F32),
            pltpu.VMEM((2, n_cell, BLOCK, TILE), F32),
            pltpu.VMEM((2, n_cell, BLOCK, TILE), F32),
            pltpu.VMEM((8, width), F32),
            pltpu.VMEM((n_cell, 8, TILE), F32),
            pltpu.VMEM((2, BLOCK, width), F32),
            pltpu.VMEM((3 * BLOCK, width), BF16),
            pltpu.VMEM((2 * BLOCK, width), FP8),
            dma((3,)),
            dma((3, 2)),
            dma((2,)),
            dma((2, 2)),
            dma((2, 2)),
            dma((2, 2)),
            dma((2, 2)),
            dma((2,)),
            dma((2,)),
            dma((2,)),
            dma((2,)),
            dma((2,)),
            dma((2, n_cell)),
            dma,
            dma((2,)),
        ],
        compiler_params=pltpu.CompilerParams(
            collective_id=0, has_side_effects=True, vmem_limit_bytes=60 * 2**20
        ),
        name="lanczos",
    )(expression, tile_mask, start.T)
    alphas, betas, fresh = pl.pallas_call(
        functools.partial(finish, math.sqrt(width * n_gene)),
        out_shape=(
            jax.ShapeDtypeStruct((2, BLOCK, BLOCK), F32),
            jax.ShapeDtypeStruct((2, BLOCK, BLOCK), F32),
            jax.ShapeDtypeStruct((BLOCK, width), F32),
        ),
        in_specs=[vmem, vmem],
        out_specs=(vmem, vmem, vmem),
        name="finish",
    )(small, resid)
    return alphas, betas, fresh.T


def solution(mesh):
    n_cell, n_gene = mesh.shape["cell"], mesh.shape["gene"]

    def run(expression, tile_mask, start):
        sizes = (n_cell, n_gene, expression.shape[0] // n_cell, expression.shape[1] // n_gene)
        return jax.shard_map(
            functools.partial(per_device, sizes),
            mesh=mesh,
            in_specs=(P("cell", "gene"), P("cell", "gene"), P("gene", None)),
            out_specs=(P(), P(), P("gene", None)),
            check_vma=False,
        )(expression, tile_mask, start)

    return run
```

```python
import functools
import math

import jax
import jax.numpy as jnp
from jax import lax
from jax.experimental import pallas as pl
from jax.experimental.pallas import tpu as pltpu
from jax.sharding import PartitionSpec as P

TILE = 256
BLOCK = 32
MESH = pl.DeviceIdType.MESH
F32 = jnp.float32
BF16 = jnp.bfloat16
FP8 = jnp.float8_e4m3fn
LOW_SCALE = 4096.0
PIVOTS = 8
GROUPS = ((0, 3), (3, 3))

NN = ((1,), (0,))
NT = ((1,), (1,))
SIDE = 4
ORDER = sorted(
    ((dy, dx) for dy in range(SIDE) for dx in range(SIDE)),
    key=lambda at: (min(at[0], SIDE - at[0]) + min(at[1], SIDE - at[1]), at),
)


def dot(left, right, dims):
    return lax.dot_general(left, right, (dims, ((), ())), preferred_element_type=F32)


def pieces(value):
    first = value.astype(BF16)
    rest = value - first.astype(F32)
    second = rest.astype(BF16)
    third = (rest - second.astype(F32)).astype(BF16)
    return first, second, third


def pieces8(value, scale):
    value = value * scale
    first = value.astype(FP8)
    second = ((value - first.astype(F32)) * 16.0).astype(FP8)
    return jnp.concatenate([first, second], axis=0)


def fold8(value):
    return value[0:BLOCK] + value[BLOCK : 2 * BLOCK] * (1.0 / 16.0)


def largest(values):
    top = functools.reduce(jnp.maximum, [jnp.max(jnp.abs(v), axis=0, keepdims=True) for v in values])
    return jnp.maximum(jnp.max(top, axis=1, keepdims=True), 1e-30)


def split3(value):
    return jnp.concatenate(pieces(value), axis=0)


def fold3(value):
    return value[0:BLOCK] + value[BLOCK : 2 * BLOCK] + value[2 * BLOCK : 3 * BLOCK]


def fold_lanes(value, at=0):
    a, b, d = (value[:, at + BLOCK * k : at + BLOCK * (k + 1)] for k in range(3))
    return a + b + d


def small_product(left, right):
    a1, a2, a3 = pieces(left)
    b1, b2, b3 = pieces(right)
    lhs = jnp.concatenate([a1, a2, a3, a1, a2, a1], axis=1)
    rhs = jnp.concatenate([b1, b1, b1, b2, b2, b3], axis=0)
    return dot(lhs, rhs, NN)


def gram_of(split):
    return fold_lanes(fold3(dot(split, split, NT)))


def pack(matrix):
    return jnp.concatenate([matrix[8 * k : 8 * (k + 1), :] for k in range(4)], axis=1)


def unpack(tile):
    return jnp.concatenate([tile[:, BLOCK * k : BLOCK * (k + 1)] for k in range(4)], axis=0)


def factor(gram):
    row_of = lax.broadcasted_iota(jnp.int32, (BLOCK, 128), 0)
    lane_of = lax.broadcasted_iota(jnp.int32, (BLOCK, 128), 1)
    both = jnp.concatenate([gram, jnp.zeros((BLOCK, 128 - BLOCK), F32)], axis=1)
    both = both + (lane_of == row_of + BLOCK).astype(F32)
    for first in range(0, BLOCK, PIVOTS):
        columns = [jnp.broadcast_to(both[:, first + p : first + p + 1], (BLOCK, 128)) for p in range(PIVOTS)]
        for p in range(PIVOTS):
            at = first + p
            factors = jnp.where(row_of > at, columns[p] * (1.0 / columns[p][at : at + 1, :]), 0.0)
            for q in range(p + 1, PIVOTS):
                columns[q] = columns[q] - factors * columns[q][at : at + 1, :]
            both = both - factors * both[at : at + 1, :]
    diagonal = jnp.sum(jnp.where(lane_of == row_of, both, 0.0), axis=1, keepdims=True)
    both = both / jnp.sqrt(diagonal)
    upper = jnp.where(lane_of >= row_of, both, 0.0)
    return upper[:, 0:BLOCK], both[:, BLOCK : 2 * BLOCK]


def kernel(
    sizes,
    x_ref,
    mask_ref,
    start_ref,
    small_ref,
    resid_ref,
    high,
    low,
    stage,
    start3,
    start8,
    gram_buf,
    last_buf,
    z_send,
    z_recv,
    z_full,
    y3,
    y8,
    stat_buf,
    image_acc,
    i_send,
    i_recv,
    column_part,
    column_recv,
    taken_ref,
    resid,
    resid3,
    resid8,
    load_sem,
    gram_sems,
    last_sems,
    z_send_sem,
    z_sem,
    zg_send_sem,
    zg_sem,
    stat_send_sem,
    stat_sem,
    rs_send_sem,
    rs_sem,
    ag_send_sem,
    ag_sem,
    out_sem,
    column_sems,
):
    n_cell, n_gene, rows, width = sizes
    cells = rows * n_cell
    chunks = rows // TILE
    tiles = width // TILE
    c = lax.axis_index("cell")
    g = lax.axis_index("gene")
    z, core = g // 2, g % 2
    y_at, x_at = c // SIDE, c % SIDE

    def cell_at(k, sign):
        if isinstance(k, int):
            dy, dx = ORDER[k]
        else:
            dy, dx = ORDER[0]
            for i in range(1, n_cell):
                dy = jnp.where(k == i, ORDER[i][0], dy)
                dx = jnp.where(k == i, ORDER[i][1], dx)
        return lax.rem(y_at + sign * dy + SIDE, SIDE) * SIDE + lax.rem(x_at + sign * dx + SIDE, SIDE)

    def block(index, size=TILE):
        return pl.ds(pl.multiple_of(index * size, size), size)

    def wait_bytes(ref, sem):
        pltpu.make_async_copy(ref, ref, sem).wait()

    def load(i, slot):
        return pltpu.make_async_copy(x_ref.at[block(i), :], stage.at[slot], load_sem.at[slot])

    for i in range(3):
        load(i, i).start()

    barrier = pltpu.get_barrier_semaphore()

    @pl.loop(1, n_cell)
    def _(k):
        pl.semaphore_signal(barrier, inc=1, device_id=(lax.rem(c + k, n_cell), g), device_id_type=MESH)

    @pl.loop(1, n_gene)
    def _(k):
        pl.semaphore_signal(barrier, inc=1, device_id=(c, lax.rem(g + k, n_gene)), device_id_type=MESH)

    def to_genes(src, dst, send_sem, recv_sem):
        @pl.loop(1, n_gene)
        def _(k):
            pltpu.make_async_remote_copy(
                src_ref=src,
                dst_ref=dst,
                send_sem=send_sem,
                recv_sem=recv_sem,
                device_id=(c, lax.rem(g + k, n_gene)),
                device_id_type=MESH,
            ).start()

    def to_cells(src, dst, send_sem, recv_sem_of, near=False):
        for t in range(1, n_cell):
            k = t if near else n_cell - t
            pltpu.make_async_remote_copy(
                src_ref=src,
                dst_ref=dst,
                send_sem=send_sem,
                recv_sem=recv_sem_of(k),
                device_id=(cell_at(k, 1), g),
                device_id_type=MESH,
            ).start()

    def sum_slots(buf, count):
        total = buf[0]
        for k in range(1, count):
            total = total + buf[k]
        return total

    def send_gram(step, tile):
        gram_buf[step, g] = tile
        here = gram_buf.at[step, g]
        to_genes(here, here, gram_sems.at[step, 0], gram_sems.at[step, 1])

    def take_gram(step):
        wait_bytes(gram_buf.at[step, pl.ds(0, n_gene - 1)], gram_sems.at[step, 1])
        return unpack(sum_slots(gram_buf.at[step], n_gene))

    start3[...] = split3(start_ref[...])
    start8[...] = pieces8(start_ref[...], 64.0)
    y3[0, pl.ds(3 * BLOCK, 16), :] = jnp.ones((16, rows), BF16)
    y3[1, pl.ds(3 * BLOCK, 16), :] = jnp.ones((16, rows), BF16)
    column_part[...] = jnp.zeros((8, width), F32)

    def spread(step, n):
        first, count = GROUPS[n]
        half = count * 128

        @pl.loop(1, n_gene)
        def _(k):
            peer = lax.rem(g + k, n_gene)
            pltpu.make_async_remote_copy(
                src_ref=z_send.at[
                    step, block(peer // 2, 8), pl.ds(pl.multiple_of(first * TILE + peer % 2 * half, 128), half)
                ],
                dst_ref=z_recv.at[step, n, k],
                send_sem=z_send_sem.at[step, n],
                recv_sem=z_sem.at[step, n],
                device_id=(c, peer),
                device_id_type=MESH,
            ).start()

    def gather(step, n):
        first, count = GROUPS[n]
        half = count * 128
        wait_bytes(z_recv.at[step, n, pl.ds(1, n_gene - 1)], z_sem.at[step, n])
        there = (step, block(z, 8), pl.ds(pl.multiple_of(first * TILE + core * half, 128), half))
        total = z_send[there]
        for k in range(1, n_gene):
            total = total + z_recv[step, n, k]
        place = z_full.at[there]
        place[...] = total
        to_genes(place, place, zg_send_sem.at[step, n], zg_sem.at[step, n])

    def gathered(step, n):
        wait_bytes(z_recv.at[step, n, pl.ds(1, n_gene - 1)], zg_sem.at[step, n])

    @pl.loop(0, chunks)
    def _(i):
        slot = lax.rem(i, 3)
        load(i, slot).wait()
        here = block(i)
        total = jnp.zeros((3 * BLOCK, TILE), F32)
        total8 = jnp.zeros((2 * BLOCK, TILE), F32)
        for j in range(tiles):
            lanes = pl.ds(j * TILE, TILE)
            values = stage[slot, :, lanes] * mask_ref[i, j].astype(F32)
            top = values.astype(BF16)
            rest = ((values - top.astype(F32)) * LOW_SCALE).astype(FP8)
            column_part[:, lanes] += jnp.sum(values.reshape(TILE // 8, 8, TILE), axis=0)
            high[here, lanes] = top
            low[here, lanes] = rest
            total = total + dot(start3[:, lanes], top, NT)
            total8 = total8 + dot(start8[:, lanes], rest, NT)

        @pl.when(i + 3 < chunks)
        def _():
            load(i + 3, slot).start()

        @pl.when(i == 1)
        def _():
            pl.semaphore_wait(barrier, n_cell + n_gene - 2)
            send_gram(0, pack(gram_of(start3[...])))

        z_send[0, :, here] = fold3(total) + fold8(total8) * (1.0 / (64.0 * LOW_SCALE))

        @pl.when(i == GROUPS[1][0] - 1)
        def _():
            spread(0, 0)

        @pl.when(i == chunks - 1)
        def _():
            spread(0, 1)
            gather(0, 0)

    _, inverse0 = factor(take_gram(0))
    current = small_product(inverse0, start_ref[:, block(c)])
    gather(0, 1)

    @pl.loop(1, n_cell)
    def _(k):
        owner = cell_at(k, 1)
        pltpu.make_async_remote_copy(
            src_ref=column_part.at[:, block(owner)],
            dst_ref=column_recv.at[k],
            send_sem=column_sems.at[0],
            recv_sem=column_sems.at[1],
            device_id=(owner, g),
            device_id_type=MESH,
        ).start()


    def side_of(step, inverse, first, count):
        lanes = pl.ds(first * TILE, count * TILE)
        side = small_product(inverse, z_full[step, :, lanes])
        top = largest([side])
        y3[step, pl.ds(0, 3 * BLOCK), lanes] = split3(side)
        y8[:, lanes] = pieces8(side, 256.0 / top)
        return top * (1.0 / (256.0 * LOW_SCALE))

    def back(step, undo, first, count, lanes):
        there = pl.ds(first * TILE, count * TILE)
        product = dot(y3[step, pl.ds(0, 3 * BLOCK), there], high[there, lanes], NN)
        product8 = dot(y8[:, there], low[there, lanes], NN)
        return fold3(product) + fold8(product8) * undo

    with_ones = 3 * BLOCK + 16
    gathered(0, 0)
    undo0 = side_of(0, inverse0, *GROUPS[0])

    def early(t):
        lanes = block(t, 2 * TILE)
        image_acc[:, lanes] = back(0, undo0, *GROUPS[0], lanes)

    pl.loop(0, tiles // 2)(early)
    own = block(c)
    column_sums = None
    older = None
    inverse = inverse0
    gathered(0, 1)
    undo = side_of(0, inverse0, *GROUPS[1])
    eye = lax.broadcasted_iota(jnp.int32, (BLOCK, BLOCK), 0) == lax.broadcasted_iota(jnp.int32, (BLOCK, BLOCK), 1)
    older_mean = None

    for step in range(2):
        count = 2 + step

        def send_stat():
            if step == 0:
                stat = dot(y3[0], y3[0], NT)
            else:
                stat = dot(y3[1], jnp.concatenate([y3[1], y3[0]], axis=0), NT)
            row = fold_lanes(stat[3 * BLOCK : 3 * BLOCK + 8])
            stat = fold3(stat)
            stat_buf[step, c, 0] = pack(fold_lanes(stat))
            stat_buf[step, c, 1] = jnp.concatenate([row, jnp.zeros((8, 128 - BLOCK), F32)], axis=1)
            if step == 1:
                stat_buf[step, c, 2] = pack(fold_lanes(stat, with_ones))
            here = stat_buf.at[step, c, pl.ds(0, count)]
            to_cells(here, here, stat_send_sem.at[step], lambda k: stat_sem.at[step])

        sent, got = i_send.at[step], i_recv.at[step]

        def image(k):
            owner = cell_at(k, 1)
            lanes = block(owner)
            if step == 0:
                sent[k] = image_acc[:, lanes] + back(0, undo, *GROUPS[1], lanes)
            else:
                sent[k] = back(1, undo, 0, chunks, lanes)
            return owner

        def send_image(k, owner):
            pltpu.make_async_remote_copy(
                src_ref=sent.at[k],
                dst_ref=got.at[k],
                send_sem=rs_send_sem.at[step],
                recv_sem=rs_sem.at[step],
                device_id=(owner, g),
                device_id_type=MESH,
            ).start()

        @pl.loop(0, n_cell // 2)
        def _(t):
            one, two = n_cell - 1 - 2 * t, n_cell - 2 - 2 * t
            owner_one = image(one)
            owner_two = image(two)
            send_image(one, owner_one)

            @pl.when(t < n_cell // 2 - 1)
            def _():
                send_image(two, owner_two)

            pl.when(t == 1)(send_stat)

        if step == 0:
            wait_bytes(column_recv.at[pl.ds(1, n_cell - 1)], column_sems.at[1])
            column_sums = column_part[:, own]
            for k in range(1, n_cell):
                column_sums = column_sums + column_recv[k]
            column_sums = jnp.sum(column_sums, axis=0, keepdims=True)

        wait_bytes(stat_buf.at[step, pl.ds(0, n_cell - 1), pl.ds(0, count)], stat_sem.at[step])
        stats = [sum_slots(stat_buf.at[step, :, k], n_cell) / cells for k in range(count)]
        mean_row = stats[1][0:1, 0:BLOCK]
        mean_column = jnp.sum(jnp.where(eye, mean_row, 0.0), axis=1, keepdims=True)
        alpha = unpack(stats[0]) - mean_column * mean_row
        small_ref[1 + step] = alpha

        taken = small_product(alpha, current)
        if step > 0:
            prior = unpack(stats[2]) - mean_column * older_mean
            taken = taken + small_product(prior, older)
        taken_ref[...] = mean_column * column_sums + taken * cells

        wait_bytes(got.at[pl.ds(1, n_cell - 1)], rs_sem.at[step])
        piece = sent[0]
        for k in range(1, n_cell):
            piece = piece + got[k]
        piece = (piece - taken_ref[...]) * (1.0 / cells)
        place = resid.at[step, :, own]
        place[...] = piece

        if step == 0:
            to_cells(place, place, ag_send_sem.at[step], lambda k: ag_sem.at[step, k], True)
            older_mean = mean_row

            def arrived(k):
                lanes = block(cell_at(k, -1))
                wait_bytes(resid.at[step, :, lanes], ag_sem.at[step, k])
                return lanes

            for first, last in ((0, 5), (5, 11), (11, 16)):
                lanes_of = [own if k == 0 else arrived(k) for k in range(first, last)]
                values = [resid[step, :, lanes] for lanes in lanes_of]
                top = largest(values)
                for lanes, value in zip(lanes_of, values):
                    resid3[:, lanes] = split3(value)
                    resid8[:, lanes] = pieces8(value, 256.0 / top)
                undo = top * (1.0 / (256.0 * LOW_SCALE))

                @pl.loop(0, 2)
                def _(i):
                    for one in (3 * i, 3 * i + 1, 3 * i + 2):
                        there = block(one)
                        total, total8 = 0.0, 0.0
                        for lanes in lanes_of:
                            total = total + dot(resid3[:, lanes], high[there, lanes], NT)
                            total8 = total8 + dot(resid8[:, lanes], low[there, lanes], NT)
                        total = fold3(total) + fold8(total8) * undo
                        z_send[1, :, there] = total if first == 0 else z_send[1, :, there] + total
                    if last == n_cell:
                        for n in range(2):
                            pl.when(i == n)(functools.partial(spread, 1, n))

            send_gram(1, pack(gram_of(resid3[...])))
            gather(1, 0)
            gather(1, 1)
            upper, inverse = factor(take_gram(1))
            small_ref[3] = upper
            older = current
            current = small_product(inverse, piece)
            gathered(1, 0)
            gathered(1, 1)
            undo = side_of(1, inverse, 0, chunks)
        else:
            last_buf[c] = pack(gram_of(split3(piece)))
            here = last_buf.at[c]
            to_cells(here, here, last_sems.at[0], lambda k: last_sems.at[1])
            to_cells(place, place, ag_send_sem.at[step], lambda k: ag_sem.at[step, 0])

            wait_bytes(column_recv.at[pl.ds(1, n_cell - 1)], column_sems.at[0])
            for k in range(2):
                wait_bytes(gram_buf.at[k, pl.ds(0, n_gene - 1)], gram_sems.at[k, 0])
                for n in range(2):
                    wait_bytes(z_recv.at[k, n, pl.ds(1, n_gene - 1)], z_send_sem.at[k, n])
                    wait_bytes(z_recv.at[k, n, pl.ds(1, n_gene - 1)], zg_send_sem.at[k, n])
                wait_bytes(stat_buf.at[k, pl.ds(0, n_cell - 1), pl.ds(0, 2 + k)], stat_send_sem.at[k])
                wait_bytes(i_recv.at[k, pl.ds(1, n_cell - 1)], rs_send_sem.at[k])
            wait_bytes(resid.at[0, :, pl.ds(0, (n_cell - 1) * TILE)], ag_send_sem.at[0])

            wait_bytes(last_buf.at[pl.ds(0, n_cell - 1)], last_sems.at[1])
            send_gram(2, sum_slots(last_buf, n_cell))
            wait_bytes(resid.at[step, :, pl.ds(0, (n_cell - 1) * TILE)], ag_sem.at[step, 0])
            pltpu.make_async_copy(resid.at[step], resid_ref, out_sem).start()
            upper, inverse = factor(take_gram(2))
            small_ref[0] = inverse
            small_ref[4] = upper
            pltpu.make_async_copy(resid.at[step], resid_ref, out_sem).wait()

    for sem, part in (
        (gram_sems.at[2, 0], gram_buf.at[2, pl.ds(0, n_gene - 1)]),
        (last_sems.at[0], last_buf.at[pl.ds(0, n_cell - 1)]),
        (ag_send_sem.at[1], resid.at[1, :, pl.ds(0, (n_cell - 1) * TILE)]),
    ):
        wait_bytes(part, sem)


def finish(scale, small_ref, resid_ref, alphas_ref, betas_ref, next_ref):
    next_ref[...] = small_product(small_ref[0] * scale, resid_ref[...])
    alphas_ref[...] = small_ref[1:3]
    betas_ref[...] = small_ref[3:5]


def per_device(sizes, expression, tile_mask, start):
    n_cell, n_gene, rows, width = sizes
    chunks = rows // TILE
    vmem = pl.BlockSpec(memory_space=pltpu.VMEM)
    dma = pltpu.SemaphoreType.DMA
    small, resid = pl.pallas_call(
        functools.partial(kernel, sizes),
        out_shape=(
            jax.ShapeDtypeStruct((5, BLOCK, BLOCK), F32),
            jax.ShapeDtypeStruct((BLOCK, width), F32),
        ),
        in_specs=[pl.BlockSpec(memory_space=pl.ANY), pl.BlockSpec(memory_space=pltpu.SMEM), vmem],
        out_specs=(vmem, pl.BlockSpec(memory_space=pl.ANY)),
        scratch_shapes=[
            pltpu.VMEM((rows, width), BF16),
            pltpu.VMEM((rows, width), FP8),
            pltpu.VMEM((3, TILE, width), F32),
            pltpu.VMEM((3 * BLOCK, width), BF16),
            pltpu.VMEM((2 * BLOCK, width), FP8),
            pltpu.VMEM((3, n_gene, 8, 128), F32),
            pltpu.VMEM((n_cell, 8, 128), F32),
            pltpu.VMEM((2, BLOCK, rows), F32),
            pltpu.VMEM((2, 2, n_gene, 8, GROUPS[0][1] * 128), F32),
            pltpu.VMEM((2, BLOCK, rows), F32),
            pltpu.VMEM((2, 3 * BLOCK + 16, rows), BF16),
            pltpu.VMEM((2 * BLOCK, rows), FP8),
            pltpu.VMEM((2, n_cell, 3, 8, 128), F32),
            pltpu.VMEM((BLOCK, width), F32),
            pltpu.VMEM((2, n_cell, BLOCK, TILE), F32),
            pltpu.VMEM((2, n_cell, BLOCK, TILE), F32),
            pltpu.VMEM((8, width), F32),
            pltpu.VMEM((n_cell, 8, TILE), F32),
            pltpu.VMEM((BLOCK, TILE), F32),
            pltpu.VMEM((2, BLOCK, width), F32),
            pltpu.VMEM((3 * BLOCK, width), BF16),
            pltpu.VMEM((2 * BLOCK, width), FP8),
            dma((3,)),
            dma((3, 2)),
            dma((2,)),
            dma((2, 2)),
            dma((2, 2)),
            dma((2, 2)),
            dma((2, 2)),
            dma((2,)),
            dma((2,)),
            dma((2,)),
            dma((2,)),
            dma((2,)),
            dma((2, n_cell)),
            dma,
            dma((2,)),
        ],
        compiler_params=pltpu.CompilerParams(
            collective_id=0, has_side_effects=True, vmem_limit_bytes=60 * 2**20
        ),
        name="lanczos",
    )(expression, tile_mask, start.T)
    alphas, betas, fresh = pl.pallas_call(
        functools.partial(finish, math.sqrt(width * n_gene)),
        out_shape=(
            jax.ShapeDtypeStruct((2, BLOCK, BLOCK), F32),
            jax.ShapeDtypeStruct((2, BLOCK, BLOCK), F32),
            jax.ShapeDtypeStruct((BLOCK, width), F32),
        ),
        in_specs=[vmem, vmem],
        out_specs=(vmem, vmem, vmem),
        name="finish",
    )(small, resid)
    return alphas, betas, fresh.T


def solution(mesh):
    n_cell, n_gene = mesh.shape["cell"], mesh.shape["gene"]

    def run(expression, tile_mask, start):
        sizes = (n_cell, n_gene, expression.shape[0] // n_cell, expression.shape[1] // n_gene)
        return jax.shard_map(
            functools.partial(per_device, sizes),
            mesh=mesh,
            in_specs=(P("cell", "gene"), P("cell", "gene"), P("gene", None)),
            out_specs=(P(), P(), P("gene", None)),
            check_vma=False,
        )(expression, tile_mask, start)

    return run
```

```python
import functools
import math

import jax
import jax.numpy as jnp
from jax import lax
from jax.experimental import pallas as pl
from jax.experimental.pallas import tpu as pltpu
from jax.sharding import PartitionSpec as P

TILE = 256
BLOCK = 32
MESH = pl.DeviceIdType.MESH
F32 = jnp.float32
BF16 = jnp.bfloat16
FP8 = jnp.float8_e4m3fn
LOW_SCALE = 4096.0
PIVOTS = 8
GROUPS = ((0, 3), (3, 3))

NN = ((1,), (0,))
NT = ((1,), (1,))
SIDE = 4
ORDER = sorted(
    ((dy, dx) for dy in range(SIDE) for dx in range(SIDE)),
    key=lambda at: (min(at[0], SIDE - at[0]) + min(at[1], SIDE - at[1]), at),
)


def dot(left, right, dims):
    return lax.dot_general(left, right, (dims, ((), ())), preferred_element_type=F32)


def pieces(value):
    first = value.astype(BF16)
    rest = value - first.astype(F32)
    second = rest.astype(BF16)
    third = (rest - second.astype(F32)).astype(BF16)
    return first, second, third


def pieces8(value, scale):
    value = value * scale
    first = value.astype(FP8)
    second = ((value - first.astype(F32)) * 16.0).astype(FP8)
    return jnp.concatenate([first, second], axis=0)


def fold8(value):
    return value[0:BLOCK] + value[BLOCK : 2 * BLOCK] * (1.0 / 16.0)


def largest(values):
    top = functools.reduce(jnp.maximum, [jnp.max(jnp.abs(v), axis=0, keepdims=True) for v in values])
    return jnp.maximum(jnp.max(top, axis=1, keepdims=True), 1e-30)


def split3(value):
    return jnp.concatenate(pieces(value), axis=0)


def fold3(value):
    return value[0:BLOCK] + value[BLOCK : 2 * BLOCK] + value[2 * BLOCK : 3 * BLOCK]


def fold_lanes(value, at=0):
    a, b, d = (value[:, at + BLOCK * k : at + BLOCK * (k + 1)] for k in range(3))
    return a + b + d


def small_product(left, right):
    a1, a2, a3 = pieces(left)
    b1, b2, b3 = pieces(right)
    lhs = jnp.concatenate([a1, a2, a3, a1, a2, a1], axis=1)
    rhs = jnp.concatenate([b1, b1, b1, b2, b2, b3], axis=0)
    return dot(lhs, rhs, NN)


def gram_of(split):
    return fold_lanes(fold3(dot(split, split, NT)))


def pack(matrix):
    return jnp.concatenate([matrix[8 * k : 8 * (k + 1), :] for k in range(4)], axis=1)


def unpack(tile):
    return jnp.concatenate([tile[:, BLOCK * k : BLOCK * (k + 1)] for k in range(4)], axis=0)


def factor(gram):
    row_of = lax.broadcasted_iota(jnp.int32, (BLOCK, 128), 0)
    lane_of = lax.broadcasted_iota(jnp.int32, (BLOCK, 128), 1)
    both = jnp.concatenate([gram, jnp.zeros((BLOCK, 128 - BLOCK), F32)], axis=1)
    both = both + (lane_of == row_of + BLOCK).astype(F32)
    for first in range(0, BLOCK, PIVOTS):
        columns = [jnp.broadcast_to(both[:, first + p : first + p + 1], (BLOCK, 128)) for p in range(PIVOTS)]
        for p in range(PIVOTS):
            at = first + p
            factors = jnp.where(row_of > at, columns[p] * (1.0 / columns[p][at : at + 1, :]), 0.0)
            for q in range(p + 1, PIVOTS):
                columns[q] = columns[q] - factors * columns[q][at : at + 1, :]
            both = both - factors * both[at : at + 1, :]
    diagonal = jnp.sum(jnp.where(lane_of == row_of, both, 0.0), axis=1, keepdims=True)
    both = both / jnp.sqrt(diagonal)
    upper = jnp.where(lane_of >= row_of, both, 0.0)
    return upper[:, 0:BLOCK], both[:, BLOCK : 2 * BLOCK]


def kernel(
    sizes,
    x_ref,
    mask_ref,
    start_ref,
    small_ref,
    resid_ref,
    high,
    low,
    stage,
    start3,
    start8,
    gram_buf,
    last_buf,
    z_send,
    z_recv,
    z_full,
    y3,
    y8,
    stat_buf,
    image_acc,
    i_send,
    i_recv,
    column_part,
    column_recv,
    taken_ref,
    resid,
    resid3,
    resid8,
    load_sem,
    gram_sems,
    last_sems,
    z_send_sem,
    z_sem,
    zg_send_sem,
    zg_sem,
    stat_send_sem,
    stat_sem,
    rs_send_sem,
    rs_sem,
    ag_send_sem,
    ag_sem,
    out_sem,
    column_sems,
):
    n_cell, n_gene, rows, width = sizes
    cells = rows * n_cell
    chunks = rows // TILE
    tiles = width // TILE
    c = lax.axis_index("cell")
    g = lax.axis_index("gene")
    z, core = g // 2, g % 2
    y_at, x_at = c // SIDE, c % SIDE

    def cell_at(k, sign):
        if isinstance(k, int):
            dy, dx = ORDER[k]
        else:
            dy, dx = ORDER[0]
            for i in range(1, n_cell):
                dy = jnp.where(k == i, ORDER[i][0], dy)
                dx = jnp.where(k == i, ORDER[i][1], dx)
        return lax.rem(y_at + sign * dy + SIDE, SIDE) * SIDE + lax.rem(x_at + sign * dx + SIDE, SIDE)

    def block(index, size=TILE):
        return pl.ds(pl.multiple_of(index * size, size), size)

    def wait_bytes(ref, sem):
        pltpu.make_async_copy(ref, ref, sem).wait()

    def load(i, slot):
        return pltpu.make_async_copy(x_ref.at[block(i), :], stage.at[slot], load_sem.at[slot])

    for i in range(3):
        load(i, i).start()

    barrier = pltpu.get_barrier_semaphore()

    @pl.loop(1, n_cell)
    def _(k):
        pl.semaphore_signal(barrier, inc=1, device_id=(lax.rem(c + k, n_cell), g), device_id_type=MESH)

    @pl.loop(1, n_gene)
    def _(k):
        pl.semaphore_signal(barrier, inc=1, device_id=(c, lax.rem(g + k, n_gene)), device_id_type=MESH)

    def to_genes(src, dst, send_sem, recv_sem):
        @pl.loop(1, n_gene)
        def _(k):
            pltpu.make_async_remote_copy(
                src_ref=src,
                dst_ref=dst,
                send_sem=send_sem,
                recv_sem=recv_sem,
                device_id=(c, lax.rem(g + k, n_gene)),
                device_id_type=MESH,
            ).start()

    def to_cells(src, dst, send_sem, recv_sem_of, near=False):
        for t in range(1, n_cell):
            k = t if near else n_cell - t
            pltpu.make_async_remote_copy(
                src_ref=src,
                dst_ref=dst,
                send_sem=send_sem,
                recv_sem=recv_sem_of(k),
                device_id=(cell_at(k, 1), g),
                device_id_type=MESH,
            ).start()

    def sum_slots(buf, count):
        total = buf[0]
        for k in range(1, count):
            total = total + buf[k]
        return total

    def send_gram(step, tile):
        gram_buf[step, g] = tile
        here = gram_buf.at[step, g]
        to_genes(here, here, gram_sems.at[step, 0], gram_sems.at[step, 1])

    def take_gram(step):
        wait_bytes(gram_buf.at[step, pl.ds(0, n_gene - 1)], gram_sems.at[step, 1])
        return unpack(sum_slots(gram_buf.at[step], n_gene))

    start3[...] = split3(start_ref[...])
    start8[...] = pieces8(start_ref[...], 64.0)
    y3[0, pl.ds(3 * BLOCK, 16), :] = jnp.ones((16, rows), BF16)
    y3[1, pl.ds(3 * BLOCK, 16), :] = jnp.ones((16, rows), BF16)
    column_part[...] = jnp.zeros((8, width), F32)

    def spread(step, n):
        first, count = GROUPS[n]
        half = count * 128

        @pl.loop(1, n_gene)
        def _(k):
            peer = lax.rem(g + k, n_gene)
            pltpu.make_async_remote_copy(
                src_ref=z_send.at[
                    step, block(peer // 2, 8), pl.ds(pl.multiple_of(first * TILE + peer % 2 * half, 128), half)
                ],
                dst_ref=z_recv.at[step, n, k],
                send_sem=z_send_sem.at[step, n],
                recv_sem=z_sem.at[step, n],
                device_id=(c, peer),
                device_id_type=MESH,
            ).start()

    def gather(step, n):
        first, count = GROUPS[n]
        half = count * 128
        wait_bytes(z_recv.at[step, n, pl.ds(1, n_gene - 1)], z_sem.at[step, n])
        there = (step, block(z, 8), pl.ds(pl.multiple_of(first * TILE + core * half, 128), half))
        total = z_send[there]
        for k in range(1, n_gene):
            total = total + z_recv[step, n, k]
        place = z_full.at[there]
        place[...] = total
        to_genes(place, place, zg_send_sem.at[step, n], zg_sem.at[step, n])

    def gathered(step, n):
        wait_bytes(z_recv.at[step, n, pl.ds(1, n_gene - 1)], zg_sem.at[step, n])

    @pl.loop(0, chunks)
    def _(i):
        slot = lax.rem(i, 3)
        load(i, slot).wait()
        here = block(i)
        total = jnp.zeros((3 * BLOCK, TILE), F32)
        total8 = jnp.zeros((2 * BLOCK, TILE), F32)
        for j in range(tiles):
            lanes = pl.ds(j * TILE, TILE)
            values = stage[slot, :, lanes] * mask_ref[i, j].astype(F32)
            top = values.astype(BF16)
            rest = ((values - top.astype(F32)) * LOW_SCALE).astype(FP8)
            column_part[:, lanes] += jnp.sum(values.reshape(TILE // 8, 8, TILE), axis=0)
            high[here, lanes] = top
            low[here, lanes] = rest
            total = total + dot(start3[:, lanes], top, NT)
            total8 = total8 + dot(start8[:, lanes], rest, NT)

        @pl.when(i + 3 < chunks)
        def _():
            load(i + 3, slot).start()

        @pl.when(i == 1)
        def _():
            pl.semaphore_wait(barrier, n_cell + n_gene - 2)
            send_gram(0, pack(gram_of(start3[...])))

        z_send[0, :, here] = fold3(total) + fold8(total8) * (1.0 / (64.0 * LOW_SCALE))

        @pl.when(i == GROUPS[1][0] - 1)
        def _():
            spread(0, 0)

        @pl.when(i == chunks - 1)
        def _():
            spread(0, 1)
            gather(0, 0)

    _, inverse0 = factor(take_gram(0))
    current = small_product(inverse0, start_ref[:, block(c)])
    gather(0, 1)

    @pl.loop(1, n_cell)
    def _(k):
        owner = cell_at(k, 1)
        pltpu.make_async_remote_copy(
            src_ref=column_part.at[:, block(owner)],
            dst_ref=column_recv.at[k],
            send_sem=column_sems.at[0],
            recv_sem=column_sems.at[1],
            device_id=(owner, g),
            device_id_type=MESH,
        ).start()


    def side_of(step, inverse, first, count):
        lanes = pl.ds(first * TILE, count * TILE)
        side = small_product(inverse, z_full[step, :, lanes])
        top = largest([side])
        y3[step, pl.ds(0, 3 * BLOCK), lanes] = split3(side)
        y8[:, lanes] = pieces8(side, 256.0 / top)
        return top * (1.0 / (256.0 * LOW_SCALE))

    def back(step, undo, first, count, lanes):
        there = pl.ds(first * TILE, count * TILE)
        product = dot(y3[step, pl.ds(0, 3 * BLOCK), there], high[there, lanes], NN)
        product8 = dot(y8[:, there], low[there, lanes], NN)
        return fold3(product) + fold8(product8) * undo

    with_ones = 3 * BLOCK + 16
    gathered(0, 0)
    undo0 = side_of(0, inverse0, *GROUPS[0])

    def early(t):
        lanes = block(t, 2 * TILE)
        image_acc[:, lanes] = back(0, undo0, *GROUPS[0], lanes)

    pl.loop(0, tiles // 2)(early)
    own = block(c)
    column_sums = None
    older = None
    inverse = inverse0
    gathered(0, 1)
    undo = side_of(0, inverse0, *GROUPS[1])
    eye = lax.broadcasted_iota(jnp.int32, (BLOCK, BLOCK), 0) == lax.broadcasted_iota(jnp.int32, (BLOCK, BLOCK), 1)
    older_mean = None

    for step in range(2):
        count = 2 + step

        def to_side(step, stage, part, peer):
            for d in range(1, SIDE):
                pltpu.make_async_remote_copy(
                    src_ref=part,
                    dst_ref=part,
                    send_sem=stat_send_sem.at[step, stage],
                    recv_sem=stat_sem.at[step, stage],
                    device_id=(peer(d), g),
                    device_id_type=MESH,
                ).start()

        def take_stat(stage, tiles):
            wait_bytes(stat_buf.at[step, stage, pl.ds(0, SIDE - 1), pl.ds(0, tiles)], stat_sem.at[step, stage])
            return [sum_slots(stat_buf.at[step, stage, :, k], SIDE) for k in range(tiles)]

        def send_stat():
            if step == 0:
                stat = dot(y3[0], y3[0], NT)
            else:
                stat = dot(y3[1], jnp.concatenate([y3[1], y3[0]], axis=0), NT)
            row = fold_lanes(stat[3 * BLOCK : 3 * BLOCK + 8])
            stat = fold3(stat)
            mine = stat_buf.at[step, 0, x_at, pl.ds(0, count)]
            mine[0] = pack(fold_lanes(stat))
            mine[1] = jnp.concatenate([row, jnp.zeros((8, 128 - BLOCK), F32)], axis=1)
            if step == 1:
                mine[2] = pack(fold_lanes(stat, with_ones))
            to_side(step, 0, mine, lambda d: y_at * SIDE + lax.rem(x_at + d, SIDE))

        sent, got = i_send.at[step], i_recv.at[step]

        def image(k):
            owner = cell_at(k, 1)
            lanes = block(owner)
            if step == 0:
                sent[k] = image_acc[:, lanes] + back(0, undo, *GROUPS[1], lanes)
            else:
                sent[k] = back(1, undo, 0, chunks, lanes)
            return owner

        def send_image(k, owner):
            pltpu.make_async_remote_copy(
                src_ref=sent.at[k],
                dst_ref=got.at[k],
                send_sem=rs_send_sem.at[step],
                recv_sem=rs_sem.at[step],
                device_id=(owner, g),
                device_id_type=MESH,
            ).start()

        @pl.loop(0, n_cell // 2)
        def _(t):
            one, two = n_cell - 1 - 2 * t, n_cell - 2 - 2 * t
            owner_one = image(one)
            owner_two = image(two)
            send_image(one, owner_one)

            @pl.when(t < n_cell // 2 - 1)
            def _():
                send_image(two, owner_two)

            pl.when(t == 1)(send_stat)

        for k, total in enumerate(take_stat(0, count)):
            stat_buf[step, 1, y_at, k] = total
        mine = stat_buf.at[step, 1, y_at, pl.ds(0, count)]
        to_side(step, 1, mine, lambda d: lax.rem(y_at + d, SIDE) * SIDE + x_at)

        if step == 0:
            wait_bytes(column_recv.at[pl.ds(1, n_cell - 1)], column_sems.at[1])
            column_sums = column_part[:, own]
            for k in range(1, n_cell):
                column_sums = column_sums + column_recv[k]
            column_sums = jnp.sum(column_sums, axis=0, keepdims=True)

        stats = [total / cells for total in take_stat(1, count)]
        mean_row = stats[1][0:1, 0:BLOCK]
        mean_column = jnp.sum(jnp.where(eye, mean_row, 0.0), axis=1, keepdims=True)
        alpha = unpack(stats[0]) - mean_column * mean_row
        small_ref[1 + step] = alpha

        taken = small_product(alpha, current)
        if step > 0:
            prior = unpack(stats[2]) - mean_column * older_mean
            taken = taken + small_product(prior, older)
        taken_ref[...] = mean_column * column_sums + taken * cells

        wait_bytes(got.at[pl.ds(1, n_cell - 1)], rs_sem.at[step])
        piece = sent[0]
        for k in range(1, n_cell):
            piece = piece + got[k]
        piece = (piece - taken_ref[...]) * (1.0 / cells)
        place = resid.at[step, :, own]
        place[...] = piece

        if step == 0:
            to_cells(place, place, ag_send_sem.at[step], lambda k: ag_sem.at[step, k], True)
            older_mean = mean_row

            def arrived(k):
                lanes = block(cell_at(k, -1))
                wait_bytes(resid.at[step, :, lanes], ag_sem.at[step, k])
                return lanes

            for first, last in ((0, 5), (5, 11), (11, 16)):
                lanes_of = [own if k == 0 else arrived(k) for k in range(first, last)]
                values = [resid[step, :, lanes] for lanes in lanes_of]
                top = largest(values)
                for lanes, value in zip(lanes_of, values):
                    resid3[:, lanes] = split3(value)
                    resid8[:, lanes] = pieces8(value, 256.0 / top)
                undo = top * (1.0 / (256.0 * LOW_SCALE))

                @pl.loop(0, 2)
                def _(i):
                    for one in (3 * i, 3 * i + 1, 3 * i + 2):
                        there = block(one)
                        total, total8 = 0.0, 0.0
                        for lanes in lanes_of:
                            total = total + dot(resid3[:, lanes], high[there, lanes], NT)
                            total8 = total8 + dot(resid8[:, lanes], low[there, lanes], NT)
                        total = fold3(total) + fold8(total8) * undo
                        z_send[1, :, there] = total if first == 0 else z_send[1, :, there] + total
                    if last == n_cell:
                        for n in range(2):
                            pl.when(i == n)(functools.partial(spread, 1, n))

            send_gram(1, pack(gram_of(resid3[...])))
            gather(1, 0)
            gather(1, 1)
            upper, inverse = factor(take_gram(1))
            small_ref[3] = upper
            older = current
            current = small_product(inverse, piece)
            gathered(1, 0)
            gathered(1, 1)
            undo = side_of(1, inverse, 0, chunks)
        else:
            last_buf[c] = pack(gram_of(split3(piece)))
            here = last_buf.at[c]
            to_cells(here, here, last_sems.at[0], lambda k: last_sems.at[1])
            to_cells(place, place, ag_send_sem.at[step], lambda k: ag_sem.at[step, 0])

            wait_bytes(column_recv.at[pl.ds(1, n_cell - 1)], column_sems.at[0])
            for k in range(2):
                wait_bytes(gram_buf.at[k, pl.ds(0, n_gene - 1)], gram_sems.at[k, 0])
                for n in range(2):
                    wait_bytes(z_recv.at[k, n, pl.ds(1, n_gene - 1)], z_send_sem.at[k, n])
                    wait_bytes(z_recv.at[k, n, pl.ds(1, n_gene - 1)], zg_send_sem.at[k, n])
                for n in range(2):
                    wait_bytes(stat_buf.at[k, n, pl.ds(0, SIDE - 1), pl.ds(0, 2 + k)], stat_send_sem.at[k, n])
                wait_bytes(i_recv.at[k, pl.ds(1, n_cell - 1)], rs_send_sem.at[k])
            wait_bytes(resid.at[0, :, pl.ds(0, (n_cell - 1) * TILE)], ag_send_sem.at[0])

            wait_bytes(last_buf.at[pl.ds(0, n_cell - 1)], last_sems.at[1])
            send_gram(2, sum_slots(last_buf, n_cell))
            wait_bytes(resid.at[step, :, pl.ds(0, (n_cell - 1) * TILE)], ag_sem.at[step, 0])
            pltpu.make_async_copy(resid.at[step], resid_ref, out_sem).start()
            upper, inverse = factor(take_gram(2))
            small_ref[0] = inverse
            small_ref[4] = upper
            pltpu.make_async_copy(resid.at[step], resid_ref, out_sem).wait()

    for sem, part in (
        (gram_sems.at[2, 0], gram_buf.at[2, pl.ds(0, n_gene - 1)]),
        (last_sems.at[0], last_buf.at[pl.ds(0, n_cell - 1)]),
        (ag_send_sem.at[1], resid.at[1, :, pl.ds(0, (n_cell - 1) * TILE)]),
    ):
        wait_bytes(part, sem)


def finish(scale, small_ref, resid_ref, alphas_ref, betas_ref, next_ref):
    next_ref[...] = small_product(small_ref[0] * scale, resid_ref[...])
    alphas_ref[...] = small_ref[1:3]
    betas_ref[...] = small_ref[3:5]


def per_device(sizes, expression, tile_mask, start):
    n_cell, n_gene, rows, width = sizes
    chunks = rows // TILE
    vmem = pl.BlockSpec(memory_space=pltpu.VMEM)
    dma = pltpu.SemaphoreType.DMA
    small, resid = pl.pallas_call(
        functools.partial(kernel, sizes),
        out_shape=(
            jax.ShapeDtypeStruct((5, BLOCK, BLOCK), F32),
            jax.ShapeDtypeStruct((BLOCK, width), F32),
        ),
        in_specs=[pl.BlockSpec(memory_space=pl.ANY), pl.BlockSpec(memory_space=pltpu.SMEM), vmem],
        out_specs=(vmem, pl.BlockSpec(memory_space=pl.ANY)),
        scratch_shapes=[
            pltpu.VMEM((rows, width), BF16),
            pltpu.VMEM((rows, width), FP8),
            pltpu.VMEM((3, TILE, width), F32),
            pltpu.VMEM((3 * BLOCK, width), BF16),
            pltpu.VMEM((2 * BLOCK, width), FP8),
            pltpu.VMEM((3, n_gene, 8, 128), F32),
            pltpu.VMEM((n_cell, 8, 128), F32),
            pltpu.VMEM((2, BLOCK, rows), F32),
            pltpu.VMEM((2, 2, n_gene, 8, GROUPS[0][1] * 128), F32),
            pltpu.VMEM((2, BLOCK, rows), F32),
            pltpu.VMEM((2, 3 * BLOCK + 16, rows), BF16),
            pltpu.VMEM((2 * BLOCK, rows), FP8),
            pltpu.VMEM((2, 2, SIDE, 3, 8, 128), F32),
            pltpu.VMEM((BLOCK, width), F32),
            pltpu.VMEM((2, n_cell, BLOCK, TILE), F32),
            pltpu.VMEM((2, n_cell, BLOCK, TILE), F32),
            pltpu.VMEM((8, width), F32),
            pltpu.VMEM((n_cell, 8, TILE), F32),
            pltpu.VMEM((BLOCK, TILE), F32),
            pltpu.VMEM((2, BLOCK, width), F32),
            pltpu.VMEM((3 * BLOCK, width), BF16),
            pltpu.VMEM((2 * BLOCK, width), FP8),
            dma((3,)),
            dma((3, 2)),
            dma((2,)),
            dma((2, 2)),
            dma((2, 2)),
            dma((2, 2)),
            dma((2, 2)),
            dma((2, 2)),
            dma((2, 2)),
            dma((2,)),
            dma((2,)),
            dma((2,)),
            dma((2, n_cell)),
            dma,
            dma((2,)),
        ],
        compiler_params=pltpu.CompilerParams(
            collective_id=0, has_side_effects=True, vmem_limit_bytes=60 * 2**20
        ),
        name="lanczos",
    )(expression, tile_mask, start.T)
    alphas, betas, fresh = pl.pallas_call(
        functools.partial(finish, math.sqrt(width * n_gene)),
        out_shape=(
            jax.ShapeDtypeStruct((2, BLOCK, BLOCK), F32),
            jax.ShapeDtypeStruct((2, BLOCK, BLOCK), F32),
            jax.ShapeDtypeStruct((BLOCK, width), F32),
        ),
        in_specs=[vmem, vmem],
        out_specs=(vmem, vmem, vmem),
        name="finish",
    )(small, resid)
    return alphas, betas, fresh.T


def solution(mesh):
    n_cell, n_gene = mesh.shape["cell"], mesh.shape["gene"]

    def run(expression, tile_mask, start):
        sizes = (n_cell, n_gene, expression.shape[0] // n_cell, expression.shape[1] // n_gene)
        return jax.shard_map(
            functools.partial(per_device, sizes),
            mesh=mesh,
            in_specs=(P("cell", "gene"), P("cell", "gene"), P("gene", None)),
            out_specs=(P(), P(), P("gene", None)),
            check_vma=False,
        )(expression, tile_mask, start)

    return run
```

```python
import functools
import math

import jax
import jax.numpy as jnp
from jax import lax
from jax.experimental import pallas as pl
from jax.experimental.pallas import tpu as pltpu
from jax.sharding import PartitionSpec as P

TILE = 256
BLOCK = 32
MESH = pl.DeviceIdType.MESH
F32 = jnp.float32
BF16 = jnp.bfloat16
FP8 = jnp.float8_e4m3fn
LOW_SCALE = 4096.0
PIVOTS = 16
GROUPS = ((0, 3), (3, 3))

NN = ((1,), (0,))
NT = ((1,), (1,))
SIDE = 4
ORDER = sorted(
    ((dy, dx) for dy in range(SIDE) for dx in range(SIDE)),
    key=lambda at: (min(at[0], SIDE - at[0]) + min(at[1], SIDE - at[1]), at),
)


def dot(left, right, dims):
    return lax.dot_general(left, right, (dims, ((), ())), preferred_element_type=F32)


def pieces(value):
    first = value.astype(BF16)
    rest = value - first.astype(F32)
    second = rest.astype(BF16)
    third = (rest - second.astype(F32)).astype(BF16)
    return first, second, third


def pieces8(value, scale):
    value = value * scale
    first = value.astype(FP8)
    second = ((value - first.astype(F32)) * 16.0).astype(FP8)
    return jnp.concatenate([first, second], axis=0)


def fold8(value):
    return value[0:BLOCK] + value[BLOCK : 2 * BLOCK] * (1.0 / 16.0)


def largest(values):
    top = functools.reduce(jnp.maximum, [jnp.max(jnp.abs(v), axis=0, keepdims=True) for v in values])
    return jnp.maximum(jnp.max(top, axis=1, keepdims=True), 1e-30)


def split3(value):
    return jnp.concatenate(pieces(value), axis=0)


def fold3(value):
    return value[0:BLOCK] + value[BLOCK : 2 * BLOCK] + value[2 * BLOCK : 3 * BLOCK]


def fold_lanes(value, at=0):
    a, b, d = (value[:, at + BLOCK * k : at + BLOCK * (k + 1)] for k in range(3))
    return a + b + d


def small_product(left, right):
    a1, a2, a3 = pieces(left)
    b1, b2, b3 = pieces(right)
    lhs = jnp.concatenate([a1, a2, a3, a1, a2, a1], axis=1)
    rhs = jnp.concatenate([b1, b1, b1, b2, b2, b3], axis=0)
    return dot(lhs, rhs, NN)


def gram_of(split):
    return fold_lanes(fold3(dot(split, split, NT)))


def pack(matrix):
    return jnp.concatenate([matrix[8 * k : 8 * (k + 1), :] for k in range(4)], axis=1)


def unpack(tile):
    return jnp.concatenate([tile[:, BLOCK * k : BLOCK * (k + 1)] for k in range(4)], axis=0)


def factor(gram):
    row_of = lax.broadcasted_iota(jnp.int32, (BLOCK, 128), 0)
    lane_of = lax.broadcasted_iota(jnp.int32, (BLOCK, 128), 1)
    both = jnp.concatenate([gram, jnp.zeros((BLOCK, 128 - BLOCK), F32)], axis=1)
    both = both + (lane_of == row_of + BLOCK).astype(F32)
    for first in range(0, BLOCK, PIVOTS):
        columns = [jnp.broadcast_to(both[:, first + p : first + p + 1], (BLOCK, 128)) for p in range(PIVOTS)]
        for p in range(PIVOTS):
            at = first + p
            factors = jnp.where(row_of > at, columns[p] * (1.0 / columns[p][at : at + 1, :]), 0.0)
            for q in range(p + 1, PIVOTS):
                columns[q] = columns[q] - factors * columns[q][at : at + 1, :]
            both = both - factors * both[at : at + 1, :]
    diagonal = jnp.sum(jnp.where(lane_of == row_of, both, 0.0), axis=1, keepdims=True)
    both = both / jnp.sqrt(diagonal)
    upper = jnp.where(lane_of >= row_of, both, 0.0)
    return upper[:, 0:BLOCK], both[:, BLOCK : 2 * BLOCK]


def kernel(
    sizes,
    x_ref,
    mask_ref,
    start_ref,
    small_ref,
    resid_ref,
    high,
    low,
    stage,
    start3,
    start8,
    gram_buf,
    last_buf,
    z_send,
    z_recv,
    z_full,
    y3,
    y8,
    stat_buf,
    image_acc,
    i_send,
    i_recv,
    column_part,
    column_recv,
    taken_ref,
    resid,
    resid3,
    resid8,
    load_sem,
    gram_sems,
    last_sems,
    z_send_sem,
    z_sem,
    zg_send_sem,
    zg_sem,
    stat_send_sem,
    stat_sem,
    rs_send_sem,
    rs_sem,
    ag_send_sem,
    ag_sem,
    out_sem,
    column_sems,
):
    n_cell, n_gene, rows, width = sizes
    cells = rows * n_cell
    chunks = rows // TILE
    tiles = width // TILE
    c = lax.axis_index("cell")
    g = lax.axis_index("gene")
    z, core = g // 2, g % 2
    y_at, x_at = c // SIDE, c % SIDE

    def cell_at(k, sign):
        if isinstance(k, int):
            dy, dx = ORDER[k]
        else:
            dy, dx = ORDER[0]
            for i in range(1, n_cell):
                dy = jnp.where(k == i, ORDER[i][0], dy)
                dx = jnp.where(k == i, ORDER[i][1], dx)
        return lax.rem(y_at + sign * dy + SIDE, SIDE) * SIDE + lax.rem(x_at + sign * dx + SIDE, SIDE)

    def block(index, size=TILE):
        return pl.ds(pl.multiple_of(index * size, size), size)

    def wait_bytes(ref, sem):
        pltpu.make_async_copy(ref, ref, sem).wait()

    def load(i, slot):
        return pltpu.make_async_copy(x_ref.at[block(i), :], stage.at[slot], load_sem.at[slot])

    for i in range(3):
        load(i, i).start()

    barrier = pltpu.get_barrier_semaphore()

    @pl.loop(1, n_cell)
    def _(k):
        pl.semaphore_signal(barrier, inc=1, device_id=(lax.rem(c + k, n_cell), g), device_id_type=MESH)

    @pl.loop(1, n_gene)
    def _(k):
        pl.semaphore_signal(barrier, inc=1, device_id=(c, lax.rem(g + k, n_gene)), device_id_type=MESH)

    def to_genes(src, dst, send_sem, recv_sem):
        @pl.loop(1, n_gene)
        def _(k):
            pltpu.make_async_remote_copy(
                src_ref=src,
                dst_ref=dst,
                send_sem=send_sem,
                recv_sem=recv_sem,
                device_id=(c, lax.rem(g + k, n_gene)),
                device_id_type=MESH,
            ).start()

    def to_cells(src, dst, send_sem, recv_sem_of, near=False):
        for t in range(1, n_cell):
            k = t if near else n_cell - t
            pltpu.make_async_remote_copy(
                src_ref=src,
                dst_ref=dst,
                send_sem=send_sem,
                recv_sem=recv_sem_of(k),
                device_id=(cell_at(k, 1), g),
                device_id_type=MESH,
            ).start()

    def sum_slots(buf, count):
        total = buf[0]
        for k in range(1, count):
            total = total + buf[k]
        return total

    def send_gram(step, tile):
        gram_buf[step, g] = tile
        here = gram_buf.at[step, g]
        to_genes(here, here, gram_sems.at[step, 0], gram_sems.at[step, 1])

    def take_gram(step):
        wait_bytes(gram_buf.at[step, pl.ds(0, n_gene - 1)], gram_sems.at[step, 1])
        return unpack(sum_slots(gram_buf.at[step], n_gene))

    start3[...] = split3(start_ref[...])
    start8[...] = pieces8(start_ref[...], 64.0)
    y3[0, pl.ds(3 * BLOCK, 16), :] = jnp.ones((16, rows), BF16)
    y3[1, pl.ds(3 * BLOCK, 16), :] = jnp.ones((16, rows), BF16)
    column_part[...] = jnp.zeros((8, width), F32)

    def spread(step, n):
        first, count = GROUPS[n]
        half = count * 128

        @pl.loop(1, n_gene)
        def _(k):
            peer = lax.rem(g + k, n_gene)
            pltpu.make_async_remote_copy(
                src_ref=z_send.at[
                    step, block(peer // 2, 8), pl.ds(pl.multiple_of(first * TILE + peer % 2 * half, 128), half)
                ],
                dst_ref=z_recv.at[step, n, k],
                send_sem=z_send_sem.at[step, n],
                recv_sem=z_sem.at[step, n],
                device_id=(c, peer),
                device_id_type=MESH,
            ).start()

    def gather(step, n):
        first, count = GROUPS[n]
        half = count * 128
        wait_bytes(z_recv.at[step, n, pl.ds(1, n_gene - 1)], z_sem.at[step, n])
        there = (step, block(z, 8), pl.ds(pl.multiple_of(first * TILE + core * half, 128), half))
        total = z_send[there]
        for k in range(1, n_gene):
            total = total + z_recv[step, n, k]
        place = z_full.at[there]
        place[...] = total
        to_genes(place, place, zg_send_sem.at[step, n], zg_sem.at[step, n])

    def gathered(step, n):
        wait_bytes(z_recv.at[step, n, pl.ds(1, n_gene - 1)], zg_sem.at[step, n])

    @pl.loop(0, chunks)
    def _(i):
        slot = lax.rem(i, 3)
        load(i, slot).wait()
        here = block(i)
        total = jnp.zeros((3 * BLOCK, TILE), F32)
        total8 = jnp.zeros((2 * BLOCK, TILE), F32)
        for j in range(tiles):
            lanes = pl.ds(j * TILE, TILE)
            values = stage[slot, :, lanes] * mask_ref[i, j].astype(F32)
            top = values.astype(BF16)
            rest = ((values - top.astype(F32)) * LOW_SCALE).astype(FP8)
            column_part[:, lanes] += jnp.sum(values.reshape(TILE // 8, 8, TILE), axis=0)
            high[here, lanes] = top
            low[here, lanes] = rest
            total = total + dot(start3[:, lanes], top, NT)
            total8 = total8 + dot(start8[:, lanes], rest, NT)

        @pl.when(i + 3 < chunks)
        def _():
            load(i + 3, slot).start()

        @pl.when(i == 1)
        def _():
            pl.semaphore_wait(barrier, n_cell + n_gene - 2)
            send_gram(0, pack(gram_of(start3[...])))

        z_send[0, :, here] = fold3(total) + fold8(total8) * (1.0 / (64.0 * LOW_SCALE))

        @pl.when(i == GROUPS[1][0] - 1)
        def _():
            spread(0, 0)

        @pl.when(i == chunks - 1)
        def _():
            spread(0, 1)
            gather(0, 0)

    _, inverse0 = factor(take_gram(0))
    current = small_product(inverse0, start_ref[:, block(c)])
    gather(0, 1)

    @pl.loop(1, n_cell)
    def _(k):
        owner = cell_at(k, 1)
        pltpu.make_async_remote_copy(
            src_ref=column_part.at[:, block(owner)],
            dst_ref=column_recv.at[k],
            send_sem=column_sems.at[0],
            recv_sem=column_sems.at[1],
            device_id=(owner, g),
            device_id_type=MESH,
        ).start()


    def side_of(step, inverse, first, count):
        lanes = pl.ds(first * TILE, count * TILE)
        side = small_product(inverse, z_full[step, :, lanes])
        top = largest([side])
        y3[step, pl.ds(0, 3 * BLOCK), lanes] = split3(side)
        y8[:, lanes] = pieces8(side, 256.0 / top)
        return top * (1.0 / (256.0 * LOW_SCALE))

    def back(step, undo, first, count, lanes):
        there = pl.ds(first * TILE, count * TILE)
        product = dot(y3[step, pl.ds(0, 3 * BLOCK), there], high[there, lanes], NN)
        product8 = dot(y8[:, there], low[there, lanes], NN)
        return fold3(product) + fold8(product8) * undo

    with_ones = 3 * BLOCK + 16
    gathered(0, 0)
    undo0 = side_of(0, inverse0, *GROUPS[0])

    def early(t):
        lanes = block(t, 2 * TILE)
        image_acc[:, lanes] = back(0, undo0, *GROUPS[0], lanes)

    pl.loop(0, tiles // 2)(early)
    own = block(c)
    column_sums = None
    older = None
    inverse = inverse0
    gathered(0, 1)
    undo = side_of(0, inverse0, *GROUPS[1])
    eye = lax.broadcasted_iota(jnp.int32, (BLOCK, BLOCK), 0) == lax.broadcasted_iota(jnp.int32, (BLOCK, BLOCK), 1)
    older_mean = None

    for step in range(2):
        count = 2 + step

        def to_side(step, stage, part, peer):
            for d in range(1, SIDE):
                pltpu.make_async_remote_copy(
                    src_ref=part,
                    dst_ref=part,
                    send_sem=stat_send_sem.at[step, stage],
                    recv_sem=stat_sem.at[step, stage],
                    device_id=(peer(d), g),
                    device_id_type=MESH,
                ).start()

        def take_stat(stage, tiles):
            wait_bytes(stat_buf.at[step, stage, pl.ds(0, SIDE - 1), pl.ds(0, tiles)], stat_sem.at[step, stage])
            return [sum_slots(stat_buf.at[step, stage, :, k], SIDE) for k in range(tiles)]

        def send_stat():
            if step == 0:
                stat = dot(y3[0], y3[0], NT)
            else:
                stat = dot(y3[1], jnp.concatenate([y3[1], y3[0]], axis=0), NT)
            row = fold_lanes(stat[3 * BLOCK : 3 * BLOCK + 8])
            stat = fold3(stat)
            mine = stat_buf.at[step, 0, x_at, pl.ds(0, count)]
            mine[0] = pack(fold_lanes(stat))
            mine[1] = jnp.concatenate([row, jnp.zeros((8, 128 - BLOCK), F32)], axis=1)
            if step == 1:
                mine[2] = pack(fold_lanes(stat, with_ones))
            to_side(step, 0, mine, lambda d: y_at * SIDE + lax.rem(x_at + d, SIDE))

        sent, got = i_send.at[step], i_recv.at[step]

        def image(k):
            owner = cell_at(k, 1)
            lanes = block(owner)
            if step == 0:
                sent[k] = image_acc[:, lanes] + back(0, undo, *GROUPS[1], lanes)
            else:
                sent[k] = back(1, undo, 0, chunks, lanes)
            return owner

        def send_image(k, owner):
            pltpu.make_async_remote_copy(
                src_ref=sent.at[k],
                dst_ref=got.at[k],
                send_sem=rs_send_sem.at[step],
                recv_sem=rs_sem.at[step],
                device_id=(owner, g),
                device_id_type=MESH,
            ).start()

        @pl.loop(0, n_cell // 2)
        def _(t):
            one, two = n_cell - 1 - 2 * t, n_cell - 2 - 2 * t
            owner_one = image(one)
            owner_two = image(two)
            send_image(one, owner_one)

            @pl.when(t < n_cell // 2 - 1)
            def _():
                send_image(two, owner_two)

            pl.when(t == 0)(send_stat)

        for k, total in enumerate(take_stat(0, count)):
            stat_buf[step, 1, y_at, k] = total
        mine = stat_buf.at[step, 1, y_at, pl.ds(0, count)]
        to_side(step, 1, mine, lambda d: lax.rem(y_at + d, SIDE) * SIDE + x_at)

        if step == 0:
            wait_bytes(column_recv.at[pl.ds(1, n_cell - 1)], column_sems.at[1])
            column_sums = column_part[:, own]
            for k in range(1, n_cell):
                column_sums = column_sums + column_recv[k]
            column_sums = jnp.sum(column_sums, axis=0, keepdims=True)

        stats = [total / cells for total in take_stat(1, count)]
        mean_row = stats[1][0:1, 0:BLOCK]
        mean_column = jnp.sum(jnp.where(eye, mean_row, 0.0), axis=1, keepdims=True)
        alpha = unpack(stats[0]) - mean_column * mean_row
        small_ref[1 + step] = alpha

        taken = small_product(alpha, current)
        if step > 0:
            prior = unpack(stats[2]) - mean_column * older_mean
            taken = taken + small_product(prior, older)
        taken_ref[...] = mean_column * column_sums + taken * cells

        wait_bytes(got.at[pl.ds(1, n_cell - 1)], rs_sem.at[step])
        piece = sent[0]
        for k in range(1, n_cell):
            piece = piece + got[k]
        piece = (piece - taken_ref[...]) * (1.0 / cells)
        place = resid.at[step, :, own]
        place[...] = piece

        if step == 0:
            to_cells(place, place, ag_send_sem.at[step], lambda k: ag_sem.at[step, k], True)
            older_mean = mean_row

            def arrived(k):
                lanes = block(cell_at(k, -1))
                wait_bytes(resid.at[step, :, lanes], ag_sem.at[step, k])
                return lanes

            for first, last in ((0, 5), (5, 11), (11, 16)):
                lanes_of = [own if k == 0 else arrived(k) for k in range(first, last)]
                values = [resid[step, :, lanes] for lanes in lanes_of]
                top = largest(values)
                for lanes, value in zip(lanes_of, values):
                    resid3[:, lanes] = split3(value)
                    resid8[:, lanes] = pieces8(value, 256.0 / top)
                undo = top * (1.0 / (256.0 * LOW_SCALE))

                @pl.loop(0, 2)
                def _(i):
                    for one in (3 * i, 3 * i + 1, 3 * i + 2):
                        there = block(one)
                        total, total8 = 0.0, 0.0
                        for lanes in lanes_of:
                            total = total + dot(resid3[:, lanes], high[there, lanes], NT)
                            total8 = total8 + dot(resid8[:, lanes], low[there, lanes], NT)
                        total = fold3(total) + fold8(total8) * undo
                        z_send[1, :, there] = total if first == 0 else z_send[1, :, there] + total
                    if last == n_cell:
                        for n in range(2):
                            pl.when(i == n)(functools.partial(spread, 1, n))

            send_gram(1, pack(gram_of(resid3[...])))
            gather(1, 0)
            gather(1, 1)
            upper, inverse = factor(take_gram(1))
            small_ref[3] = upper
            older = current
            current = small_product(inverse, piece)
            gathered(1, 0)
            gathered(1, 1)
            undo = side_of(1, inverse, 0, chunks)
        else:
            last_buf[c] = pack(gram_of(split3(piece)))
            here = last_buf.at[c]
            to_cells(here, here, last_sems.at[0], lambda k: last_sems.at[1])
            to_cells(place, place, ag_send_sem.at[step], lambda k: ag_sem.at[step, 0])

            wait_bytes(column_recv.at[pl.ds(1, n_cell - 1)], column_sems.at[0])
            for k in range(2):
                wait_bytes(gram_buf.at[k, pl.ds(0, n_gene - 1)], gram_sems.at[k, 0])
                for n in range(2):
                    wait_bytes(z_recv.at[k, n, pl.ds(1, n_gene - 1)], z_send_sem.at[k, n])
                    wait_bytes(z_recv.at[k, n, pl.ds(1, n_gene - 1)], zg_send_sem.at[k, n])
                for n in range(2):
                    wait_bytes(stat_buf.at[k, n, pl.ds(0, SIDE - 1), pl.ds(0, 2 + k)], stat_send_sem.at[k, n])
                wait_bytes(i_recv.at[k, pl.ds(1, n_cell - 1)], rs_send_sem.at[k])
            wait_bytes(resid.at[0, :, pl.ds(0, (n_cell - 1) * TILE)], ag_send_sem.at[0])

            wait_bytes(last_buf.at[pl.ds(0, n_cell - 1)], last_sems.at[1])
            send_gram(2, sum_slots(last_buf, n_cell))
            wait_bytes(resid.at[step, :, pl.ds(0, (n_cell - 1) * TILE)], ag_sem.at[step, 0])
            pltpu.make_async_copy(resid.at[step], resid_ref, out_sem).start()
            upper, inverse = factor(take_gram(2))
            small_ref[0] = inverse
            small_ref[4] = upper
            pltpu.make_async_copy(resid.at[step], resid_ref, out_sem).wait()

    for sem, part in (
        (gram_sems.at[2, 0], gram_buf.at[2, pl.ds(0, n_gene - 1)]),
        (last_sems.at[0], last_buf.at[pl.ds(0, n_cell - 1)]),
        (ag_send_sem.at[1], resid.at[1, :, pl.ds(0, (n_cell - 1) * TILE)]),
    ):
        wait_bytes(part, sem)


def finish(scale, small_ref, resid_ref, alphas_ref, betas_ref, next_ref):
    next_ref[...] = small_product(small_ref[0] * scale, resid_ref[...])
    alphas_ref[...] = small_ref[1:3]
    betas_ref[...] = small_ref[3:5]


def per_device(sizes, expression, tile_mask, start):
    n_cell, n_gene, rows, width = sizes
    chunks = rows // TILE
    vmem = pl.BlockSpec(memory_space=pltpu.VMEM)
    dma = pltpu.SemaphoreType.DMA
    small, resid = pl.pallas_call(
        functools.partial(kernel, sizes),
        out_shape=(
            jax.ShapeDtypeStruct((5, BLOCK, BLOCK), F32),
            jax.ShapeDtypeStruct((BLOCK, width), F32),
        ),
        in_specs=[pl.BlockSpec(memory_space=pl.ANY), pl.BlockSpec(memory_space=pltpu.SMEM), vmem],
        out_specs=(vmem, pl.BlockSpec(memory_space=pl.ANY)),
        scratch_shapes=[
            pltpu.VMEM((rows, width), BF16),
            pltpu.VMEM((rows, width), FP8),
            pltpu.VMEM((3, TILE, width), F32),
            pltpu.VMEM((3 * BLOCK, width), BF16),
            pltpu.VMEM((2 * BLOCK, width), FP8),
            pltpu.VMEM((3, n_gene, 8, 128), F32),
            pltpu.VMEM((n_cell, 8, 128), F32),
            pltpu.VMEM((2, BLOCK, rows), F32),
            pltpu.VMEM((2, 2, n_gene, 8, GROUPS[0][1] * 128), F32),
            pltpu.VMEM((2, BLOCK, rows), F32),
            pltpu.VMEM((2, 3 * BLOCK + 16, rows), BF16),
            pltpu.VMEM((2 * BLOCK, rows), FP8),
            pltpu.VMEM((2, 2, SIDE, 3, 8, 128), F32),
            pltpu.VMEM((BLOCK, width), F32),
            pltpu.VMEM((2, n_cell, BLOCK, TILE), F32),
            pltpu.VMEM((2, n_cell, BLOCK, TILE), F32),
            pltpu.VMEM((8, width), F32),
            pltpu.VMEM((n_cell, 8, TILE), F32),
            pltpu.VMEM((BLOCK, TILE), F32),
            pltpu.VMEM((2, BLOCK, width), F32),
            pltpu.VMEM((3 * BLOCK, width), BF16),
            pltpu.VMEM((2 * BLOCK, width), FP8),
            dma((3,)),
            dma((3, 2)),
            dma((2,)),
            dma((2, 2)),
            dma((2, 2)),
            dma((2, 2)),
            dma((2, 2)),
            dma((2, 2)),
            dma((2, 2)),
            dma((2,)),
            dma((2,)),
            dma((2,)),
            dma((2, n_cell)),
            dma,
            dma((2,)),
        ],
        compiler_params=pltpu.CompilerParams(
            collective_id=0, has_side_effects=True, vmem_limit_bytes=60 * 2**20
        ),
        name="lanczos",
    )(expression, tile_mask, start.T)
    alphas, betas, fresh = pl.pallas_call(
        functools.partial(finish, math.sqrt(width * n_gene)),
        out_shape=(
            jax.ShapeDtypeStruct((2, BLOCK, BLOCK), F32),
            jax.ShapeDtypeStruct((2, BLOCK, BLOCK), F32),
            jax.ShapeDtypeStruct((BLOCK, width), F32),
        ),
        in_specs=[vmem, vmem],
        out_specs=(vmem, vmem, vmem),
        name="finish",
    )(small, resid)
    return alphas, betas, fresh.T


def solution(mesh):
    n_cell, n_gene = mesh.shape["cell"], mesh.shape["gene"]

    def run(expression, tile_mask, start):
        sizes = (n_cell, n_gene, expression.shape[0] // n_cell, expression.shape[1] // n_gene)
        return jax.shard_map(
            functools.partial(per_device, sizes),
            mesh=mesh,
            in_specs=(P("cell", "gene"), P("cell", "gene"), P("gene", None)),
            out_specs=(P(), P(), P("gene", None)),
            check_vma=False,
        )(expression, tile_mask, start)

    return run
```
